32 devices in a mesh: dp: 8 (over z, x), tm: 4 (over y, core).
Axes of the slice: x: 2, y: 2, z: 4, core: 2. Of those that a mesh axis runs over, the one named last changes fastest.
Arguments:
- history_series: float32 [65536, 512], P('dp', 'tm'), may hold values from -6 to 6
- frequency_labels: int32 [65536], P(('dp', 'tm')), may hold values from 0 to 3
- affine_kernels: float32 [2, 4, 512, 512], P(None, None, 'dp'), may hold values from -0.375 to 0.375
- affine_offsets: float32 [2, 4, 512], P(None, None, 'dp'), may hold values from -3 to 3
- expansion_projection: float32 [2, 2, 512, 512], P(None, None, 'dp'), may hold values from -0.375 to 0.375
- history_dictionary: float32 [2, 512, 512], P(None, 'dp', 'tm'), may hold values from -0.25 to 0.25
- prediction_dictionary: float32 [2, 512, 80], P(None, 'dp'), may hold values from -0.25 to 0.25
- remainder_adjoint: float32 [65536, 512], P('dp', 'tm'), may hold values from -6 to 6
- prediction_adjoint: float32 [65536, 80], P(('dp', 'tm')), may hold values from -6 to 6
Outputs:
- remainder_signal: float32 [65536, 512], P('dp', 'tm')
- prediction_total: float32 [65536, 80], P(('dp', 'tm'))
- history_derivative: float32 [65536, 512], P('dp', 'tm')
- grad_fc_weight: float32 [2, 4, 512, 512], P(None, None, 'dp')
- grad_fc_bias: float32 [2, 4, 512], P(None, None, 'dp')
- grad_theta_weight: float32 [2, 2, 512, 512], P(None, None, 'dp')
- grad_back_basis: float32 [2, 512, 512], P(None, 'dp', 'tm')
- derivative_prediction_dictionary: float32 [2, 512, 80], P(None, 'dp')
The draws below stay inside these ranges and needn't reach their ends.
All inputs are finite; a program needn't handle non-finite values.
Results may differ from the reference program's by a relative error of at most 0.018.
The reference program's roundings to bfloat16 on the way count: a program that leaves them out, or rounds other values in their place, can miss the bound.
Values may be sent and summed in bfloat16 or wider, within the bound.
No kernel may reach another device: no remote copies, remote signals or barrier semaphores. Data moves between devices by JAX's collectives and lax.ppermute only.
A program may use at most 256 MiB of HBM per device.

```python
import jax
import jax.numpy as jnp
from jax import lax

HISTORY_LENGTH = 512
H = 512
EXPANSION_SIZE = 512
HOR_Y = 6
HOR_Q = 8
HOR_M = 18
AHEAD_WIDTH = 80
MODULE_TOTAL = 2
LAYERS = 4
SAMPLE_TOTAL = 65536


def plant(array, rng, least, high):
    index_at = [jax.random.randint(jax.random.fold_in(rng, axis), (), 0, length) for axis, length in enumerate(array.shape)]
    longest = array.shape.index(max(array.shape))
    neighbour = index_at[:longest] + [(index_at[longest] + 1) % array.shape[longest]] + index_at[longest + 1:]
    return array.at[tuple(index_at)].set(least).at[tuple(neighbour)].set(high)


def block_scale(own_key, extent, pieces, least, largest):
    level, own = 1.0, jax.random.fold_in(own_key, 6)
    for dim, parts in pieces:
        draws = jnp.exp(jax.random.uniform(jax.random.fold_in(own, dim), (parts,), jnp.float32, least / len(pieces), largest / len(pieces)))
        level = level * jnp.repeat(draws, extent[dim] // parts).reshape([-1 if axis == dim else 1 for axis in range(len(extent))])
    return level


def noise(key, dims, spread, bound, split=(), held_as=jnp.bfloat16):
    loudness = block_scale(key, dims, split, -0.22, 0.18) if split else 1.0
    result = jax.random.normal(key, dims, jnp.float32) * spread * loudness
    return jnp.minimum(jnp.maximum(result, -bound), bound).astype(held_as)


def setup_inputs(seed: int = 0) -> dict:
    key_list = jax.random.split(jax.random.key(seed), 10)
    return {
        "history_series": noise(key_list[0], (SAMPLE_TOTAL, HISTORY_LENGTH), 1.0, 6.0, ((0, 8), (1, 4)), jnp.float32),
        "frequency_labels": plant(jax.random.randint(key_list[1], (SAMPLE_TOTAL,), 0, 4), jax.random.fold_in(key_list[1], 1), 0, 3).astype(jnp.int32),
        "affine_kernels": noise(key_list[2], (MODULE_TOTAL, LAYERS, H, H), (H // 2) ** -0.5, 0.375, ((2, 8),), jnp.float32),
        "affine_offsets": noise(key_list[3], (MODULE_TOTAL, LAYERS, H), 0.5, 3.0, ((2, 8),), jnp.float32),
        "expansion_projection": noise(key_list[4], (MODULE_TOTAL, 2, H, EXPANSION_SIZE), (H // 2) ** -0.5, 0.375, ((2, 8),), jnp.float32),
        "history_dictionary": noise(key_list[5], (MODULE_TOTAL, EXPANSION_SIZE, HISTORY_LENGTH), EXPANSION_SIZE ** -0.5, 0.25, ((1, 8), (2, 4)), jnp.float32),
        "prediction_dictionary": noise(key_list[6], (MODULE_TOTAL, EXPANSION_SIZE, AHEAD_WIDTH), EXPANSION_SIZE ** -0.5, 0.25, ((1, 8),), jnp.float32),
        "remainder_adjoint": noise(key_list[7], (SAMPLE_TOTAL, HISTORY_LENGTH), 1.0, 6.0, ((0, 8), (1, 4)), jnp.float32),
        "prediction_adjoint": noise(key_list[8], (SAMPLE_TOTAL, AHEAD_WIDTH), 1.0, 6.0, ((0, 32),), jnp.float32),
    }


@jax.custom_vjp
def floor_limit(v):
    return lax.optimization_barrier(v.astype(jnp.bfloat16)).astype(jnp.float32)

@jax.custom_vjp
def reduce_reconstruction(v):
    return v

def low_keep(v):
    return (floor_limit(v), None)

def low_pass(kept, grad):
    return (grad,)

def back_keep(v):
    return (v, None)

def back_low(kept, grad):
    return (floor_limit(grad),)
floor_limit.defvjp(low_keep, low_pass)
reduce_reconstruction.defvjp(back_keep, back_low)

def linear_compose(left_side, right_side):
    return jnp.dot(left_side, right_side, precision=lax.Precision.HIGHEST, preferred_element_type=jnp.float32)

def build_mask(frequency_labels):
    field_entries = jnp.arange(AHEAD_WIDTH, dtype=jnp.int32)
    column_group = (field_entries >= HOR_Y).astype(jnp.int32) + (field_entries >= HOR_Y + HOR_Q).astype(jnp.int32) + (field_entries >= HOR_Y + HOR_Q + HOR_M).astype(jnp.int32)
    return (frequency_labels[:, None] == column_group[None, :]).astype(jnp.float32)

def evaluate_model(history_samples, frequency_indicator, affine_kernels, affine_offsets, expansion_projection, history_dictionary, prediction_dictionary):
    remainder_signal = history_samples
    prediction_total = jnp.zeros((history_samples.shape[0], AHEAD_WIDTH), jnp.float32)
    for module_ordinal in range(MODULE_TOTAL):
        latent_state = reduce_reconstruction(floor_limit(remainder_signal))
        for layer_index in range(LAYERS):
            preact = reduce_reconstruction(linear_compose(latent_state, floor_limit(affine_kernels[module_ordinal, layer_index])) + floor_limit(affine_offsets[module_ordinal, layer_index]))
            latent_state = floor_limit(jax.nn.silu(preact))
        back_theta = reduce_reconstruction(floor_limit(linear_compose(latent_state, floor_limit(expansion_projection[module_ordinal, 0]))))
        prediction_expansion = reduce_reconstruction(floor_limit(linear_compose(latent_state, floor_limit(expansion_projection[module_ordinal, 1]))))
        backcast = reduce_reconstruction(linear_compose(back_theta, floor_limit(history_dictionary[module_ordinal])))
        remainder_signal = remainder_signal - backcast
        prediction_total = prediction_total + frequency_indicator * reduce_reconstruction(linear_compose(prediction_expansion, floor_limit(prediction_dictionary[module_ordinal])))
    return (remainder_signal, prediction_total)

def reference(history_series, frequency_labels, affine_kernels, affine_offsets, expansion_projection, history_dictionary, prediction_dictionary, remainder_adjoint, prediction_adjoint):
    module_samples = min(4096, SAMPLE_TOTAL)
    sample_sequence = SAMPLE_TOTAL // module_samples
    indicator_sequence = build_mask(frequency_labels)
    joined_tensors = (history_series.reshape(sample_sequence, module_samples, HISTORY_LENGTH), indicator_sequence.reshape(sample_sequence, module_samples, AHEAD_WIDTH), remainder_adjoint.reshape(sample_sequence, module_samples, HISTORY_LENGTH), prediction_adjoint.reshape(sample_sequence, module_samples, AHEAD_WIDTH))

    def scan_step(cumulative_totals, fragments):
        history_samples, frequency_indicator, remainder_derivative, prediction_derivative = fragments

        def chain_modules(windows_arg, fc_w_arg, fc_b_arg, theta_arg, back_arg, fore_arg):
            return evaluate_model(windows_arg, frequency_indicator, fc_w_arg, fc_b_arg, theta_arg, back_arg, fore_arg)
        produced_values, adjoint_mapping = jax.vjp(chain_modules, history_samples, affine_kernels, affine_offsets, expansion_projection, history_dictionary, prediction_dictionary)
        derivatives_bundle = adjoint_mapping((remainder_derivative, prediction_derivative))
        cumulative_totals = jax.tree.map(jnp.add, cumulative_totals, (derivatives_bundle[1], derivatives_bundle[2], derivatives_bundle[3], derivatives_bundle[4], derivatives_bundle[5]))
        return (cumulative_totals, (produced_values[0], produced_values[1], derivatives_bundle[0]))
    starting_state = (jnp.zeros_like(affine_kernels), jnp.zeros_like(affine_offsets), jnp.zeros_like(expansion_projection), jnp.zeros_like(history_dictionary), jnp.zeros_like(prediction_dictionary))
    cumulative_totals, outcome_sequence = lax.scan(scan_step, starting_state, joined_tensors)
    remainder_signal = outcome_sequence[0].reshape(SAMPLE_TOTAL, HISTORY_LENGTH)
    prediction_total = outcome_sequence[1].reshape(SAMPLE_TOTAL, AHEAD_WIDTH)
    history_derivative = outcome_sequence[2].reshape(SAMPLE_TOTAL, HISTORY_LENGTH)
    return (remainder_signal, prediction_total, history_derivative, cumulative_totals[0], cumulative_totals[1], cumulative_totals[2], cumulative_totals[3], cumulative_totals[4])
```

```python
import functools

import jax
import jax.numpy as jnp
from jax import lax
from jax.experimental import pallas as pl
from jax.experimental.pallas import tpu as pltpu
from jax.sharding import PartitionSpec as P

HOR_Y = 6
HOR_Q = 8
HOR_M = 18
LAYERS = 4
LANES = 128
HALF = 32
GROUPS = 8
FRONT = 2 * HALF + 16
BACK = 5 * HALF
SLOT_SHARE = tuple(((s >> 2) & 1) | (s & 2) | ((s & 1) << 2) for s in range(GROUPS))
TILE = 512

f32 = jnp.float32
bf16 = jnp.bfloat16
VMEM_LIMIT = 52 * 1024 * 1024


def mm(a, b):
    return jnp.dot(a, b, preferred_element_type=f32)


def mm_nt(a, b):
    return lax.dot_general(a, b, (((1,), (1,)), ((), ())), preferred_element_type=f32)


def mm_tn(a, b):
    return lax.dot_general(a, b, (((0,), (0,)), ((), ())), preferred_element_type=f32)


def rows_at(start, size, align):
    return pl.ds(pl.multiple_of(start, align), size)


def column_groups(width):
    field = jnp.arange(width, dtype=jnp.int32)
    return (
        (field >= HOR_Y).astype(jnp.int32)
        + (field >= HOR_Y + HOR_Q).astype(jnp.int32)
        + (field >= HOR_Y + HOR_Q + HOR_M).astype(jnp.int32)
    )


def slot_rows(pos, q, s):
    share = pos[0] ^ SLOT_SHARE[s]
    half = pos[1] ^ q
    row = share * (2 * HALF) + half * HALF
    block = share * 2 + half
    window_row = ((block // 4) ^ pos[2]) * LANES + (block % 4) * HALF
    return share * (2 * HALF), row, window_row


def call(body, name, tiles, ins, outs, scratch, flops, pos, args):
    nbytes = sum(a.size * a.dtype.itemsize for a in args)
    nbytes += sum(_size(shape) * jnp.dtype(dtype).itemsize for _, shape, dtype in outs)
    return pl.pallas_call(
        body,
        name=name,
        out_shape=[jax.ShapeDtypeStruct(shape, dtype) for _, shape, dtype in outs],
        grid_spec=pltpu.PrefetchScalarGridSpec(
            num_scalar_prefetch=1,
            grid=(tiles,),
            in_specs=ins,
            out_specs=[spec for spec, _, _ in outs],
            scratch_shapes=scratch,
        ),
        compiler_params=pltpu.CompilerParams(
            dimension_semantics=("arbitrary",), vmem_limit_bytes=VMEM_LIMIT
        ),
        cost_estimate=pl.CostEstimate(
            flops=flops, bytes_accessed=nbytes, transcendentals=0
        ),
    )(pos, *args)


def _size(shape):
    total = 1
    for extent in shape:
        total *= extent
    return total


def whole(shape):
    return pl.BlockSpec(shape, lambda i, pos: (0,) * len(shape))


def tiled(width):
    return pl.BlockSpec((TILE, width), lambda i, pos: (i, 0))


def split_kernel(pos, src, *pieces):
    for r, piece in enumerate(pieces):
        piece[...] = src[pos[2] ^ r].astype(bf16)


def split_windows(array, parts, pos):
    rows = array.shape[0] // parts
    src = array.reshape(parts, rows, LANES)
    return call(
        split_kernel,
        "split_windows",
        rows // TILE,
        [pl.BlockSpec((parts, TILE, LANES), lambda i, pos: (0, i, 0))],
        [(tiled(LANES), (rows, LANES), bf16)] * parts,
        [],
        0,
        pos,
        (src,),
    )


def merge_kernel(sign, pos, base, *refs):
    pieces, out = refs[:-1], refs[-1]
    for r, piece in enumerate(pieces):
        at = pos[2] ^ r
        value = piece[...].astype(f32)
        out[at] = base[at] - value if sign < 0 else base[at] + value


def merge_windows(base, pieces, sign, pos):
    parts = len(pieces)
    rows = pieces[0].shape[0]
    spec = pl.BlockSpec((parts, TILE, LANES), lambda i, pos: (0, i, 0))
    out = call(
        functools.partial(merge_kernel, sign),
        "merge_windows",
        rows // TILE,
        [spec] + [tiled(LANES)] * parts,
        [(spec, (parts, rows, LANES), f32)],
        [],
        0,
        pos,
        (base.reshape(parts, rows, LANES), *pieces),
    )[0]
    return out.reshape(base.shape)


def swap(x, axis, bit, size):
    return lax.ppermute(x, axis, [(i, i ^ bit) for i in range(size)])


def exchange(pieces):
    parts = len(pieces)
    arrived = {r: swap(pieces[r], "tm", r, parts) for r in range(parts - 1, 0, -1)}
    return [pieces[0]] + [arrived[r] for r in range(1, parts)]


def activate(p):
    s = 0.5 * jnp.tanh(0.5 * p) + 0.5
    h = p * s
    return h.astype(bf16), s + h * (1.0 - s)


def front_kernel(n_x, pos, *refs):
    slots = refs[:4]
    xs = refs[4 : 4 + n_x]
    w1, w2, bias, basis, h1, d1, h2, d2 = refs[4 + n_x :]

    @pl.when(pl.program_id(0) == 0)
    def _():
        total = jnp.zeros((16, 2 * LANES), f32)
        for q in range(2):
            for s in range(GROUPS):
                ref, i = slots[2 * q + s // 4], s % 4
                _, row, window_row = slot_rows(pos, q, s)
                w1[rows_at(window_row, HALF, HALF), :] = ref[i, 0:HALF, :]
                w2[rows_at(row, HALF, HALF), :] = ref[i, HALF : 2 * HALF, :]
                low = ref[i, 2 * HALF : FRONT, 0:LANES]
                high = ref[i, 2 * HALF : FRONT, LANES : 2 * LANES]
                basis[rows_at(row, 16, 16), :] = low
                basis[rows_at(row + 16, 16, 16), :] = high
                if q == 0:
                    total += ref[i, 2 * HALF : FRONT, 2 * LANES :].astype(f32)
        bias[:, 0 : 2 * LANES] = total[0:8]
        bias[:, 2 * LANES :] = total[8:16]

    x = xs[0][...] if n_x == 1 else jnp.concatenate([ref[...] for ref in xs], axis=1)
    h, d = activate(mm(x, w1[...]) + bias[0:1, :])
    h1[...] = h
    d1[...] = d.astype(d1.dtype)
    h, d = activate(mm(h, w2[...]) + bias[1:2, :])
    h2[...] = h
    d2[...] = d.astype(d2.dtype)


D_TYPE = f32


def front(slots, xs, pos):
    rows = xs[0].shape[0]
    square = (whole((512, 512)), (512, 512), bf16)
    hidden = (tiled(512), (rows, 512), bf16)
    slope = (tiled(512), (rows, 512), D_TYPE)
    return call(
        functools.partial(front_kernel, len(xs)),
        "front",
        rows // TILE,
        [whole(a.shape) for a in slots] + [tiled(a.shape[1]) for a in xs],
        [
            square,
            square,
            (whole((8, 512)), (8, 512), f32),
            (whole((512, LANES)), (512, LANES), bf16),
            hidden,
            slope,
            hidden,
            slope,
        ],
        [],
        2 * 2 * rows * 512 * 512,
        pos,
        (*slots, *xs),
    )


def rear_kernel(n_x, last, pos, *refs):
    slots = refs[:4]
    h2, bias, basis = refs[4:7]
    extra = refs[7 : 7 + n_x]
    w3, w4, wb, wf, wv, h3, d3, h4, d4, bt, ft = refs[7 + n_x : 18 + n_x]
    outs = refs[18 + n_x :]

    @pl.when(pl.program_id(0) == 0)
    def _():
        for q in range(2):
            for s in range(GROUPS):
                ref, i = slots[2 * q + s // 4], s % 4
                _, row, _ = slot_rows(pos, q, s)
                for m, w in enumerate((w3, w4, wb, wf)):
                    w[rows_at(row, HALF, HALF), :] = ref[i, m * HALF : (m + 1) * HALF, :]
                for r in range(4):
                    part = ref[i, 4 * HALF : 5 * HALF, r * LANES : (r + 1) * LANES]
                    at = r ^ q
                    wv[rows_at(row, HALF, HALF), at * LANES : (at + 1) * LANES] = part

    h, d = activate(mm(h2[...], w3[...]) + bias[2:3, :])
    h3[...] = h
    d3[...] = d.astype(d3.dtype)
    h, d = activate(mm(h, w4[...]) + bias[3:4, :])
    h4[...] = h
    d4[...] = d.astype(d4.dtype)
    back = mm(h, wb[...]).astype(bf16)
    fore = mm(h, wf[...]).astype(bf16)
    bt[...] = back
    ft[...] = fore
    cast = mm(back, wv[...])
    if not last:
        x2, cast_out, fore_out = outs
        x = jnp.concatenate([ref[...] for ref in extra], axis=1).astype(f32)
        x2[...] = (x - cast).astype(bf16)
        cast_out[...] = cast
        fore_out[...] = mm(fore, basis[...])
    else:
        cast1, fore1 = extra
        cast = cast + cast1[...]
        for r in range(4):
            outs[r][...] = cast[:, r * LANES : (r + 1) * LANES].astype(bf16)
        outs[4][...] = fore1[...] + mm(fore, basis[...])


def rear(slots, h2, bias, basis, extra, last, pos):
    rows = h2.shape[0]
    square = (whole((512, 512)), (512, 512), bf16)
    hidden = (tiled(512), (rows, 512), bf16)
    slope = (tiled(512), (rows, 512), D_TYPE)
    if last:
        outs = [(tiled(LANES), (rows, LANES), bf16)] * 4
    else:
        outs = [hidden, (tiled(512), (rows, 512), f32)]
    outs.append((tiled(LANES), (rows, LANES), f32))
    return call(
        functools.partial(rear_kernel, len(extra), last),
        "rear",
        rows // TILE,
        [whole(a.shape) for a in slots]
        + [tiled(512), whole(bias.shape), whole(basis.shape)]
        + [tiled(a.shape[1]) for a in extra],
        [square] * 5 + [hidden, slope, hidden, slope, hidden, hidden] + outs,
        [],
        2 * 5 * rows * 512 * 512 + 2 * rows * 512 * LANES,
        pos,
        (*slots, h2, bias, basis, *extra),
    )


def accumulate(first, ref, value):
    @pl.when(first)
    def _():
        ref[...] = value

    @pl.when(jnp.logical_not(first))
    def _():
        ref[...] += value


def back_rear_kernel(n_g, pos, *refs):
    gs = refs[:n_g]
    fg, bt, ft, h4, h3, h2, d4, d3, wv, basis, wb, wf, w4 = refs[n_g : n_g + 13]
    g3_out, keep, send, d_basis, d_bias, a3, a4, ab, af, av = refs[n_g + 13 :]
    first = pl.program_id(0) == 0

    g = jnp.concatenate([ref[...] for ref in gs[:4]], axis=1)
    if n_g == 5:
        g = (g.astype(f32) + gs[4][...].astype(f32)).astype(bf16)
    g = -g
    accumulate(first, av, mm_tn(bt[...], g))
    g_back = mm_nt(g, wv[...]).astype(bf16)
    accumulate(first, d_basis, mm_tn(ft[...], fg[...]))
    g_fore = mm_nt(fg[...], basis[...]).astype(bf16)
    accumulate(first, ab, mm_tn(h4[...], g_back))
    accumulate(first, af, mm_tn(h4[...], g_fore))
    gh = mm_nt(g_back, wb[...]) + mm_nt(g_fore, wf[...])
    g4 = (gh * d4[...].astype(f32)).astype(bf16)
    accumulate(first, a4, mm_tn(h3[...], g4))
    gh = mm_nt(g4, w4[...])
    g3 = (gh * d3[...].astype(f32)).astype(bf16)
    g3_out[...] = g3
    accumulate(first, a3, mm_tn(h2[...], g3))
    sums = jnp.concatenate(
        [
            jnp.sum(g3.astype(f32), axis=0, keepdims=True),
            jnp.sum(g4.astype(f32), axis=0, keepdims=True),
            jnp.zeros((6, 512), f32),
        ],
        axis=0,
    )
    accumulate(first, d_bias, sums)

    @pl.when(pl.program_id(0) == pl.num_programs(0) - 1)
    def _():
        for q, out in enumerate((keep, send)):
            for s in range(GROUPS):
                share_row, row, _ = slot_rows(pos, q, s)
                for m, a in enumerate((a3, a4, ab, af)):
                    out[s, m * HALF : (m + 1) * HALF, :] = a[rows_at(row, HALF, HALF), :].astype(bf16)
                for j in range(4):
                    at = q + 2 * (j % 2)
                    part = av[
                        rows_at(share_row + (j // 2) * HALF, HALF, HALF),
                        at * LANES : (at + 1) * LANES,
                    ]
                    out[s, 4 * HALF : 5 * HALF, j * LANES : (j + 1) * LANES] = part.astype(bf16)


def back_rear(gs, fg, saved, weights, pos):
    rows = fg.shape[0]
    packed = (whole((GROUPS, BACK, 512)), (GROUPS, BACK, 512), bf16)
    square = pltpu.VMEM((512, 512), f32)
    return call(
        functools.partial(back_rear_kernel, len(gs)),
        "back_rear",
        rows // TILE,
        [tiled(a.shape[1]) for a in (*gs, fg, *saved)] + [whole(a.shape) for a in weights],
        [
            (tiled(512), (rows, 512), bf16),
            packed,
            packed,
            (whole((512, LANES)), (512, LANES), f32),
            (whole((8, 512)), (8, 512), f32),
        ],
        [square] * 5,
        2 * 9 * rows * 512 * 512 + 4 * rows * 512 * LANES,
        pos,
        (*gs, fg, *saved, *weights),
    )


def back_front_kernel(n_x, last, pos, *refs):
    xs = refs[:n_x]
    g3, h1, d2, d1, w3, w2, w1, d_basis, d_bias = refs[n_x : n_x + 9]
    rest = refs[n_x + 9 :]
    if last:
        gh2, rest = rest[0], rest[1:]
        g_outs, rest = rest[:4], rest[4:]
    else:
        g_outs, rest = rest[:1], rest[1:]
    keep, send, a1, a2, ac = rest
    first = pl.program_id(0) == 0

    gh = mm_nt(g3[...], w3[...])
    g2 = (gh * d2[...].astype(f32)).astype(bf16)
    accumulate(first, a2, mm_tn(h1[...], g2))
    gh = mm_nt(g2, w2[...])
    g1 = (gh * d1[...].astype(f32)).astype(bf16)
    gh = mm_nt(g1, w1[...])
    if last:
        gh = gh.astype(bf16).astype(f32) + gh2[...].astype(f32)
        for r, ref in enumerate(g_outs):
            ref[...] = gh[:, r * LANES : (r + 1) * LANES].astype(bf16)
    else:
        g_outs[0][...] = gh.astype(bf16)
    x = xs[0][...] if n_x == 1 else jnp.concatenate([ref[...] for ref in xs], axis=1)
    accumulate(first, a1, mm_tn(x, g1))
    sums = jnp.concatenate(
        [
            jnp.sum(g1.astype(f32), axis=0, keepdims=True),
            jnp.sum(g2.astype(f32), axis=0, keepdims=True),
            jnp.zeros((6, 512), f32),
        ],
        axis=0,
    )
    accumulate(first, ac, sums)

    @pl.when(pl.program_id(0) == pl.num_programs(0) - 1)
    def _():
        bias = jnp.concatenate([ac[0:2, :], d_bias[0:2, :], jnp.zeros((4, 512), f32)], axis=0)
        bias = jnp.concatenate([bias[:, 0 : 2 * LANES], bias[:, 2 * LANES :]], axis=0).astype(bf16)
        for q, out in enumerate((keep, send)):
            for s in range(GROUPS):
                _, row, window_row = slot_rows(pos, q, s)
                out[s, 0:HALF, :] = a1[rows_at(window_row, HALF, HALF), :].astype(bf16)
                out[s, HALF : 2 * HALF, :] = a2[rows_at(row, HALF, HALF), :].astype(bf16)
                low = d_basis[rows_at(row, 16, 16), :].astype(bf16)
                high = d_basis[rows_at(row + 16, 16, 16), :].astype(bf16)
                out[s, 2 * HALF : FRONT, 0:LANES] = low
                out[s, 2 * HALF : FRONT, LANES : 2 * LANES] = high
                out[s, 2 * HALF : FRONT, 2 * LANES :] = bias


def back_front(xs, saved, weights, gh2, pos):
    last = gh2 is not None
    rows = xs[0].shape[0]
    packed = (whole((GROUPS, FRONT, 512)), (GROUPS, FRONT, 512), bf16)
    square = pltpu.VMEM((512, 512), f32)
    if last:
        outs = [(tiled(LANES), (rows, LANES), bf16)] * 4
    else:
        outs = [(tiled(512), (rows, 512), bf16)]
    extra = (gh2,) if last else ()
    return call(
        functools.partial(back_front_kernel, len(xs), last),
        "back_front",
        rows // TILE,
        [tiled(a.shape[1]) for a in (*xs, *saved)]
        + [whole(a.shape) for a in weights]
        + [tiled(512) for _ in extra],
        outs + [packed, packed],
        [square, square, pltpu.VMEM((8, 512), f32)],
        2 * 5 * rows * 512 * 512,
        pos,
        (*xs, *saved, *weights, *extra),
    )


def pack_misc(basis, offsets):
    lead = basis.shape[:-2]
    offsets = jnp.concatenate([offsets, jnp.zeros_like(offsets)], axis=-2)
    return jnp.concatenate(
        [
            basis[..., 0:16, :],
            basis[..., 16:32, :],
            jnp.concatenate([offsets[..., 0 : 2 * LANES], offsets[..., 2 * LANES :]], axis=-2),
        ],
        axis=-1,
    ).reshape(*lead, 16, 512)


def spread(own, n_dp, n_tm):
    x = own[None]
    x = jnp.concatenate([x, swap(x, "dp", 4, n_dp)])
    low = jnp.concatenate([x, swap(x, "dp", 2, n_dp)])
    high = swap(low, "dp", 1, n_dp)
    return low, high, swap(low, "tm", 1, n_tm), swap(high, "tm", 1, n_tm)


def collect(keep, send, n_dp, n_tm):
    total = keep.astype(f32) + swap(send, "tm", 1, n_tm).astype(f32)
    for bit, left in ((1, 4), (2, 2), (4, 1)):
        arrived = swap(total[left : 2 * left].astype(bf16), "dp", bit, n_dp)
        total = total[0:left] + arrived.astype(f32)
    own = total[0].astype(bf16)
    return own.astype(f32), swap(own, "tm", 2, n_tm).astype(f32)


def halves(own, half, n_tm):
    other = swap(own, "tm", 1, n_tm)
    lower = half == 0
    return jnp.where(lower, own, other), jnp.where(lower, other, own)


def unpack_bias(misc):
    return jnp.concatenate([misc[0:4, 2 * LANES : 3 * LANES * 1 + LANES], misc[8:12, 2 * LANES :]], axis=-1)


def shares_fast(kernels, offsets, projection, history_basis, forecast_basis, n_dp, n_tm):
    dp = lax.axis_index("dp")
    tm = lax.axis_index("tm")
    half = tm % 2
    blocks = kernels.shape[0]
    share = kernels.shape[2]

    def cut(x, axis):
        return lax.dynamic_slice_in_dim(x, half * HALF, HALF, axis)

    own_v = history_basis.astype(bf16)
    near = swap(own_v, "tm", 1, n_tm)
    pair = jnp.concatenate([own_v, near], axis=-1)
    v = jnp.concatenate([pair, swap(pair, "tm", 2, n_tm)], axis=-1)
    w = cut(kernels, 2).astype(bf16)
    p = cut(projection, 2).astype(bf16)
    u = cut(jnp.pad(forecast_basis, ((0, 0), (0, 0), (0, LANES - forecast_basis.shape[-1]))), 1)
    column = jnp.arange(512, dtype=jnp.int32) // share
    b = jnp.where(column == dp, jnp.tile(offsets, (1, 1, n_dp)), 0.0)
    misc = pack_misc(u, b).astype(bf16)
    out = []
    for k in range(blocks):
        front_own = jnp.concatenate([w[k, 0], w[k, 1], misc[k]])
        back_own = jnp.concatenate([w[k, 2], w[k, 3], p[k, 0], p[k, 1], cut(v[k], 0)])
        out.append((spread(front_own, n_dp, n_tm), spread(back_own, n_dp, n_tm)))
    return out


def gradients_fast(records, n_dp, n_tm):
    dp = lax.axis_index("dp")
    half = lax.axis_index("tm") % 2
    kernels, offsets, projection, history_basis, forecast_basis = [], [], [], [], []
    for back_keep, back_send, front_keep, front_send in records:
        own, other = collect(back_keep, back_send, n_dp, n_tm)
        first, second = halves(own[0 : 4 * HALF] + other[0 : 4 * HALF], half, n_tm)
        own_v, other_v = own[4 * HALF :], other[4 * HALF :]
        history_basis.append(
            jnp.concatenate(
                [
                    own_v[:, 0:LANES] + other_v[:, LANES : 2 * LANES],
                    own_v[:, 2 * LANES : 3 * LANES] + other_v[:, 3 * LANES :],
                ]
            )
        )
        own, other = collect(front_keep, front_send, n_dp, n_tm)
        total = own + other
        first_f, second_f = halves(total, half, n_tm)

        def rows(a, b, m):
            return jnp.concatenate([a[m * HALF : (m + 1) * HALF], b[m * HALF : (m + 1) * HALF]])

        kernels.append(
            jnp.stack(
                [
                    rows(first_f, second_f, 0),
                    rows(first_f, second_f, 1),
                    rows(first, second, 0),
                    rows(first, second, 1),
                ]
            )
        )
        projection.append(jnp.stack([rows(first, second, 2), rows(first, second, 3)]))
        misc = total[2 * HALF :]
        bias = jnp.concatenate([misc[0:4, 2 * LANES :], misc[8:12, 2 * LANES :]], axis=1)
        offsets.append(lax.dynamic_slice_in_dim(bias, dp * 2 * HALF, 2 * HALF, 1))
        forecast_basis.append(
            jnp.concatenate(
                [
                    part[2 * HALF :, at : at + LANES]
                    for part in (first_f, second_f)
                    for at in (0, LANES)
                ]
            )
        )
    return [jnp.stack(x) for x in (kernels, offsets, projection, history_basis, forecast_basis)]


def slots_of(x):
    x = x.reshape(GROUPS, 2, HALF, x.shape[-1]).swapaxes(0, 1)
    return x[:, jnp.array(SLOT_SHARE)]


def rows_of(x):
    x = x[:, jnp.array(SLOT_SHARE)]
    return x.swapaxes(0, 1).reshape(2 * GROUPS * HALF, x.shape[-1])


def four(x):
    return x[0, 0:4], x[0, 4:8], x[1, 0:4], x[1, 4:8]


def shares_plain(kernels, offsets, projection, history_basis, forecast_basis, n_tm):
    tm = lax.axis_index("tm")

    def gather(x, axis, over="dp"):
        return lax.all_gather(x.astype(bf16), over, axis=axis, tiled=True)

    order = [jnp.bitwise_xor(tm, r) for r in range(n_tm)]
    out = []
    for k in range(kernels.shape[0]):
        w = gather(kernels[k], 1)
        b = gather(offsets[k], 1)
        p = gather(projection[k], 1)
        u = gather(forecast_basis[k], 0)
        u = jnp.pad(u, ((0, 0), (0, LANES - u.shape[-1])))
        v = gather(gather(history_basis[k], 0), 1, "tm")
        v = jnp.concatenate(
            [lax.dynamic_slice_in_dim(v, at * LANES, LANES, 1) for at in order], axis=1
        )
        v = slots_of(v)
        other = jnp.concatenate([v[1, ..., (r ^ 1) * LANES : ((r ^ 1) + 1) * LANES] for r in range(4)], axis=-1)
        v = jnp.stack([v[0], other])
        offs = jnp.zeros((2, GROUPS, LAYERS, 512), bf16).at[0, 0].set(b)
        misc = pack_misc(slots_of(u), offs)
        first = jnp.concatenate([slots_of(w[0]), slots_of(w[1]), misc], axis=2)
        second = jnp.concatenate([slots_of(w[2]), slots_of(w[3]), slots_of(p[0]), slots_of(p[1]), v], axis=2)
        out.append((four(first), four(second)))
    return out


def gradients_plain(records, n_tm):
    tm = lax.axis_index("tm")

    def reduce(x, axis):
        return lax.psum_scatter(
            lax.psum(x.astype(bf16), "tm").astype(f32), "dp", scatter_dimension=axis, tiled=True
        )

    results = [[], [], [], [], []]
    for back_keep, back_send, front_keep, front_send in records:
        back = jnp.stack([back_keep, back_send])
        front_ = jnp.stack([front_keep, front_send])

        def square(x, m):
            return rows_of(x[:, :, m * HALF : (m + 1) * HALF, :])

        kernels = jnp.stack([square(front_, 0), square(front_, 1), square(back, 0), square(back, 1)])
        results[0].append(reduce(kernels, 1))
        misc = front_[:, :, 2 * HALF :, :]
        bias = misc[0, 0]
        bias = jnp.concatenate([bias[0:4, 2 * LANES :], bias[8:12, 2 * LANES :]], axis=1)
        results[1].append(reduce(bias, 1))
        results[2].append(reduce(jnp.stack([square(back, 2), square(back, 3)]), 1))
        v = back[:, :, 4 * HALF :, :][:, jnp.array(SLOT_SHARE)]
        v = jnp.concatenate([v[..., 0 : 2 * LANES], v[..., 2 * LANES :]], axis=2)
        v = v.reshape(2, 2 * GROUPS * HALF, 2, LANES)
        blocks = [v[r % 2, :, r // 2] for r in range(4)]
        total = blocks[0].astype(f32)
        for r in range(1, n_tm):
            total = total + swap(blocks[r], "tm", r, n_tm).astype(f32)
        results[3].append(lax.psum_scatter(total, "dp", scatter_dimension=0, tiled=True))
        u = jnp.concatenate([misc[..., 0:LANES], misc[..., LANES : 2 * LANES]], axis=2)
        results[4].append(reduce(rows_of(u), 0))
    return [jnp.stack(x) for x in results]


def body(
    n_dp,
    n_tm,
    history_series,
    frequency_labels,
    affine_kernels,
    affine_offsets,
    expansion_projection,
    history_dictionary,
    prediction_dictionary,
    remainder_adjoint,
    prediction_adjoint,
):
    dp = lax.axis_index("dp")
    tm = lax.axis_index("tm")
    fast = n_dp == GROUPS
    zero = jnp.zeros((), jnp.int32)
    pos = jnp.stack([dp if fast else zero, tm % 2 if fast else zero, tm]).astype(jnp.int32)
    masters = (
        affine_kernels,
        affine_offsets,
        expansion_projection,
        history_dictionary,
        prediction_dictionary,
    )
    if fast:
        shares = shares_fast(*masters, n_dp, n_tm)
    else:
        shares = shares_plain(*masters, n_tm)
    x1 = exchange(split_windows(history_series, n_tm, pos))
    g0 = exchange(split_windows(remainder_adjoint, n_tm, pos))

    width = prediction_adjoint.shape[1]
    mask = (frequency_labels[:, None] == column_groups(width)[None, :]).astype(f32)
    fg = jnp.pad((mask * prediction_adjoint).astype(bf16), ((0, 0), (0, LANES - width)))

    saved = []
    xs, extra = x1, x1
    for k in range(2):
        last = k == 1
        w1, w2, bias, basis, h1, d1, h2, d2 = front(shares[k][0], xs, pos)
        outs = rear(shares[k][1], h2, bias, basis, extra, last, pos)
        w3, w4, wb, wf, wv, h3, d3, h4, d4, bt, ft = outs[:11]
        saved.append(
            (
                xs,
                (bt, ft, h4, h3, h2, d4, d3),
                (wv, basis, wb, wf, w4),
                (h1, d2, d1),
                (w3, w2, w1),
            )
        )
        if not last:
            x2, cast, fore = outs[11:]
            xs, extra = [x2], [cast, fore]
        else:
            cast, fore = outs[11:15], outs[15]
    remainder = merge_windows(history_series, exchange(cast), -1, pos)
    prediction = mask * fore[:, 0:width]

    records = [None, None]
    gs, gh2 = g0, None
    for k in (1, 0):
        xs, rear_saved, rear_weights, front_saved, front_weights = saved[k]
        g3, back_keep, back_send, d_basis, d_bias = back_rear(gs, fg, rear_saved, rear_weights, pos)
        outs = back_front(
            xs, (g3, *front_saved), (*front_weights, d_basis, d_bias), gh2, pos
        )
        if k == 1:
            gh2 = outs[0]
            gs = [*g0, gh2]
        else:
            pieces = outs[:4]
        records[k] = (back_keep, back_send, outs[-2], outs[-1])
    derivative = merge_windows(remainder_adjoint, exchange(pieces), 1, pos)
    if fast:
        grads = gradients_fast(records, n_dp, n_tm)
    else:
        grads = gradients_plain(records, n_tm)
    kernels, offsets, projection, history_basis, forecast_basis = grads
    return (
        remainder,
        prediction,
        derivative,
        kernels,
        offsets,
        projection,
        history_basis,
        forecast_basis[..., 0:width],
    )


def solution(mesh):
    return jax.shard_map(
        functools.partial(body, mesh.shape["dp"], mesh.shape["tm"]),
        mesh=mesh,
        in_specs=(
            P("dp", "tm"),
            P(("dp", "tm")),
            P(None, None, "dp", None),
            P(None, None, "dp"),
            P(None, None, "dp", None),
            P(None, "dp", "tm"),
            P(None, "dp", None),
            P("dp", "tm"),
            P(("dp", "tm"), None),
        ),
        out_specs=(
            P("dp", "tm"),
            P(("dp", "tm"), None),
            P("dp", "tm"),
            P(None, None, "dp", None),
            P(None, None, "dp"),
            P(None, None, "dp", None),
            P(None, "dp", "tm"),
            P(None, "dp", None),
        ),
        check_vma=False,
    )
```

```python
import functools

import jax
import jax.numpy as jnp
from jax import lax
from jax.experimental import pallas as pl
from jax.experimental.pallas import tpu as pltpu
from jax.sharding import PartitionSpec as P

HOR_Y = 6
HOR_Q = 8
HOR_M = 18
LAYERS = 4
LANES = 128
HALF = 32
GROUPS = 8
FRONT = 2 * HALF + 16
BACK = 5 * HALF
SLOT_SHARE = tuple(((s >> 2) & 1) | (s & 2) | ((s & 1) << 2) for s in range(GROUPS))
TILE = 512
CHUNK = 256

f32 = jnp.float32
bf16 = jnp.bfloat16
MIB = 1024 * 1024
FLOPS_PER_US = 250_000_000


def mm(a, b):
    return jnp.dot(a, b, preferred_element_type=f32)


def mm_nt(a, b):
    return lax.dot_general(a, b, (((1,), (1,)), ((), ())), preferred_element_type=f32)


def mm_tn(a, b):
    return lax.dot_general(a, b, (((0,), (0,)), ((), ())), preferred_element_type=f32)


def rows_at(start, size, align):
    return pl.ds(pl.multiple_of(start, align), size)


def in_group(labels, width):
    field = lax.broadcasted_iota(jnp.int32, (width, labels.shape[1]), 0)
    group = (
        (field >= HOR_Y).astype(jnp.int32)
        + (field >= HOR_Y + HOR_Q).astype(jnp.int32)
        + (field >= HOR_Y + HOR_Q + HOR_M).astype(jnp.int32)
    )
    return group == labels


def slot_rows(pos, q, s):
    share = pos[0] ^ SLOT_SHARE[s]
    half = pos[1] ^ q
    row = share * (2 * HALF) + half * HALF
    block = share * 2 + half
    window_row = ((block // 4) ^ pos[2]) * LANES + (block % 4) * HALF
    return row, window_row


def slot_at(pos, share):
    r = share ^ pos[0]
    return ((r & 1) << 2) | (r & 2) | ((r >> 2) & 1)


def size_of(shape):
    total = 1
    for extent in shape:
        total *= extent
    return total


class Inputs:
    def __init__(self, refs, copies):
        self.refs, self.copies = refs, copies

    def __getitem__(self, i):
        if isinstance(i, slice):
            return [self[j] for j in range(*i.indices(len(self.refs)))]
        if i in self.copies:
            self.copies.pop(i).wait()
        return self.refs[i]


class Line:
    def __init__(self, pos):
        self.pos, self.token = pos, None

    def run(self, body, name, args, outs, scratch=(), fetch=(), save=(), limit=12, after=(), us=0.5, stay=(), out_stays=False):
        token = [] if self.token is None else [self.token]
        extra = [*after, *token]
        fetch, save = list(fetch), list(save)
        n_in, n_out, n_extra = len(args), len(outs), len(extra)
        n_fetch, n_save = len(fetch), len(save)

        def kernel(pos_ref, *refs):
            refs = list(refs)
            given, refs = refs[:n_in], refs[n_in + n_extra :]
            results, refs = refs[:n_out], refs[n_out:]
            saved, refs = refs[:n_save], refs[n_save:]
            landing, refs = refs[:n_fetch], refs[n_fetch:]
            sems = refs.pop() if n_fetch + n_save else None
            inputs, copies, leaving = list(given), {}, []
            for at, (i, buf) in enumerate(zip(fetch, landing)):
                copies[i] = pltpu.make_async_copy(given[i], buf, sems.at[at])
                copies[i].start()
                inputs[i] = buf
            for at, (i, dst) in enumerate(zip(save, saved)):
                leaving.append(pltpu.make_async_copy(given[i], dst, sems.at[n_fetch + at]))
                leaving[-1].start()
            body(pos_ref, Inputs(inputs, copies), results, refs)
            for copy in (*copies.values(), *leaving):
                copy.wait()

        vmem, hbm = pl.BlockSpec(memory_space=pltpu.VMEM), pl.BlockSpec(memory_space=pltpu.HBM)
        anywhere = pl.BlockSpec(memory_space=pl.ANY)
        place = pltpu.HBM if out_stays else jax.ShapeDtypeStruct
        shapes = [place(shape, dtype) for shape, dtype in outs]
        shapes += [pltpu.HBM(args[i].shape, args[i].dtype) for i in save]
        sems = [pltpu.SemaphoreType.DMA((n_fetch + n_save,))] if n_fetch + n_save else []
        results = pl.pallas_call(
            kernel,
            name=name,
            out_shape=shapes,
            in_specs=[pl.BlockSpec(memory_space=pltpu.SMEM)]
            + [hbm if i in fetch or i in stay else vmem for i in range(n_in)]
            + [anywhere] * n_extra,
            out_specs=[hbm if out_stays else vmem] * n_out + [hbm] * n_save,
            scratch_shapes=[pltpu.VMEM(args[i].shape, args[i].dtype) for i in fetch]
            + list(scratch)
            + sems,
            compiler_params=pltpu.CompilerParams(vmem_limit_bytes=limit * MIB),
            cost_estimate=pl.CostEstimate(
                flops=int(us * FLOPS_PER_US), bytes_accessed=1, transcendentals=0
            ),
        )(self.pos, *args, *extra)
        self.token = min(results, key=lambda a: a.size * a.dtype.itemsize)
        return results


def swap(x, axis, bit, size):
    return lax.ppermute(x, axis, [(i, i ^ bit) for i in range(size)])


def exchange(pieces):
    parts = len(pieces)
    arrived = {r: swap(pieces[r], "tm", r, parts) for r in range(parts - 1, 0, -1)}
    return [pieces[0]] + [arrived[r] for r in range(1, parts)]


def split_body(pos, ins, outs, scratch):
    landing, sems = scratch
    copies = []
    for r in range(len(outs)):
        copies.append(pltpu.make_async_copy(ins[0].at[pos[2] ^ r], landing.at[r], sems.at[r]))
        copies[-1].start()
    for r, out in enumerate(outs):
        copies[r].wait()
        out[...] = landing[r].astype(bf16)


def split_windows(line, array, parts):
    shape = (parts, array.shape[0] // parts, LANES)
    return line.run(
        split_body,
        "split_windows",
        (array.reshape(shape),),
        [(shape[1:], bf16)] * parts,
        [pltpu.VMEM(shape, f32), pltpu.SemaphoreType.DMA((parts,))],
        stay=(0,),
        limit=8,
        us=2.0,
    )


def merge_body(sign, pos, ins, outs, scratch):
    base, pieces = ins[0], ins[1:]
    landing, leaving, sems = scratch
    parts = len(pieces)
    arrive, leave = [], []
    for r in range(parts):
        at = pos[2] ^ r
        arrive.append(pltpu.make_async_copy(base.at[at], landing.at[r], sems.at[r]))
        leave.append(pltpu.make_async_copy(leaving.at[r], outs[0].at[at], sems.at[parts + r]))
        arrive[-1].start()
    for r, piece in enumerate(pieces):
        arrive[r].wait()
        value = piece[...].astype(f32)
        leaving[r] = landing[r] - value if sign < 0 else landing[r] + value
        leave[r].start()
    for copy in leave:
        copy.wait()


def merge_windows(line, base, pieces, sign):
    parts = len(pieces)
    shape = (parts, base.shape[0] // parts, LANES)
    out = line.run(
        functools.partial(merge_body, sign),
        "merge_windows",
        (base.reshape(shape), *pieces),
        [(shape, f32)],
        [pltpu.VMEM(shape, f32), pltpu.VMEM(shape, f32), pltpu.SemaphoreType.DMA((2 * parts,))],
        stay=(0,),
        out_stays=True,
        limit=12,
        us=3.5,
    )[0]
    return out.reshape(base.shape)


def activate(p):
    t = jnp.tanh(p)
    u = 1.0 + t
    h = p * u
    return h.astype(bf16), u + h * (1.0 - t)


def columns(refs, at):
    if len(refs) == 1:
        return refs[0][at, :]
    return jnp.concatenate([ref[at, :] for ref in refs], axis=1)


def chunks(rows):
    return [slice(at, at + CHUNK) for at in range(0, rows, CHUNK)]


def front_body(n_x, pos, ins, bufs, scratch):
    w1, w2, bias, basis, h1, d1, h2, d2 = bufs
    total = jnp.zeros((16, 2 * LANES), f32)
    for q in range(2):
        for s in range(GROUPS):
            ref, i = ins[2 * q + s // 4], s % 4
            row, window_row = slot_rows(pos, q, s)
            w1[rows_at(window_row, HALF, HALF), :] = ref[i, 0:HALF, :] * 0.5
            w2[rows_at(row, HALF, HALF), :] = ref[i, HALF : 2 * HALF, :] * 0.5
            low = ref[i, 2 * HALF : FRONT, 0:LANES]
            high = ref[i, 2 * HALF : FRONT, LANES : 2 * LANES]
            basis[rows_at(row, 16, 16), :] = low
            basis[rows_at(row + 16, 16, 16), :] = high
            if q == 0:
                total += ref[i, 2 * HALF : FRONT, 2 * LANES :].astype(f32)
    bias[:, 0 : 2 * LANES] = total[0:8] * 0.5
    bias[:, 2 * LANES :] = total[8:16] * 0.5
    xs = ins[4 : 4 + n_x]
    for at in chunks(h1.shape[0]):
        h, d = activate(mm(columns(xs, at), w1[...]) + bias[0:1, :])
        h1[at, :] = h
        d1[at, :] = d.astype(bf16)
    for at in chunks(h1.shape[0]):
        h, d = activate(mm(h1[at, :], w2[...]) + bias[1:2, :])
        h2[at, :] = h
        d2[at, :] = d.astype(bf16)


def front(line, slots, xs, leaving=()):
    rows = xs[0].shape[0]
    square = ((512, 512), bf16)
    hidden = ((rows, 512), bf16)
    args = (*slots, *xs, *leaving)
    return line.run(
        functools.partial(front_body, len(xs)),
        "front",
        args,
        [square, square, ((8, 512), f32), ((512, LANES), bf16), hidden, hidden, hidden, hidden],
        save=range(len(args) - len(leaving), len(args)),
        limit=6,
        us=4.0,
    )


def rear_body(n_x, last, pos, ins, bufs, scratch):
    w3, w4, wb, wf, wv, h3, d3, h4, d4, bt, ft = bufs[:11]
    for q in range(2):
        for s in range(GROUPS):
            ref, i = ins[2 * q + s // 4], s % 4
            row, _ = slot_rows(pos, q, s)
            for m, w in enumerate((w3, w4, wb, wf)):
                part = ref[i, m * HALF : (m + 1) * HALF, :]
                w[rows_at(row, HALF, HALF), :] = part * 0.5 if m < 2 else part
            for r in range(4):
                part = ref[i, 4 * HALF : 5 * HALF, r * LANES : (r + 1) * LANES]
                at = r ^ q
                wv[rows_at(row, HALF, HALF), at * LANES : (at + 1) * LANES] = part
    bias, h2 = ins[4], ins[5]
    steps = chunks(h3.shape[0])
    for at in steps:
        h, d = activate(mm(h2[at, :], w3[...]) + bias[2:3, :])
        h3[at, :] = h
        d3[at, :] = d.astype(bf16)
    for at in steps:
        h, d = activate(mm(h3[at, :], w4[...]) + bias[3:4, :])
        h4[at, :] = h
        d4[at, :] = (0.5 * d).astype(bf16)
    for at in steps:
        bt[at, :] = mm(h4[at, :], wb[...]).astype(bf16)
    extra = ins[6 : 6 + n_x]
    for at in steps:
        cast = mm(bt[at, :], wv[...])
        if not last:
            bufs[11][at, :] = (columns(extra, at).astype(f32) - cast).astype(bf16)
            bufs[12][at, :] = cast
        else:
            cast = cast + extra[0][at, :]
            for r in range(4):
                bufs[11 + r][at, :] = cast[:, r * LANES : (r + 1) * LANES].astype(bf16)
    for at in steps:
        ft[at, :] = mm(h4[at, :], wf[...]).astype(bf16)
    basis = ins[6 + n_x]
    width = bufs[-1].shape[0]
    for at in steps:
        fore = mm(ft[at, :], basis[...]).T[0:width, :]
        if last:
            fore = extra[1][:, at] + fore
            fore = jnp.where(in_group(extra[2][0:1, at], width), fore, 0.0)
        bufs[-1][:, at] = fore


def rear(line, slots, h2, bias, basis, extra, last, width, leaving=()):
    rows = h2.shape[0]
    square = ((512, 512), bf16)
    hidden = ((rows, 512), bf16)
    if last:
        outs = [((rows, LANES), bf16)] * 4
    else:
        outs = [hidden, ((rows, 512), f32)]
    args = (*slots, bias, h2, *extra, basis, *leaving)
    return line.run(
        functools.partial(rear_body, len(extra), last),
        "rear",
        args,
        [square] * 5 + [hidden] * 6 + outs + [((width, rows), f32)],
        save=range(len(args) - len(leaving), len(args)),
        limit=6,
        us=8.0,
    )


def row_sum(value):
    return jnp.sum(value.astype(f32), axis=0, keepdims=True)


def pack_pair(packed, rows, lanes, slot, first, second, pos):
    keep, send = packed
    lower = pos[1] == 0
    first, second = first.astype(bf16), second.astype(bf16)
    keep[slot, rows, lanes] = jnp.where(lower, first, second)
    send[slot, rows, lanes] = jnp.where(lower, second, first)


def pack_rows(packed, at, value, pos):
    for share in range(GROUPS):
        row = share * 2 * HALF
        pack_pair(
            packed,
            slice(at, at + HALF),
            slice(None),
            slot_at(pos, share),
            value[row : row + HALF, :],
            value[row + HALF : row + 2 * HALF, :],
            pos,
        )


def chain_rear_body(n_g, pos, ins, outs, scratch):
    g, g_back, g_fore, g4, g3, bias = outs
    wv, basis, wb, wf, w4 = ins[n_g + 1 : n_g + 6]
    gs, fg = ins[0:n_g], ins[n_g]
    steps = chunks(g.shape[0])
    for at in steps:
        value = columns(gs[:4], at)
        if n_g == 5:
            value = (value.astype(f32) + gs[4][at, :].astype(f32)).astype(bf16)
        g[at, :] = -value
        g_back[at, :] = mm_nt(g[at, :], wv[...]).astype(bf16)
    for at in steps:
        g_fore[at, :] = mm_nt(fg[:, at].T, basis[...]).astype(bf16)
    d4 = ins[n_g + 6]
    b3 = b4 = jnp.zeros((1, 512), f32)
    for at in steps:
        gh = mm_nt(g_back[at, :], wb[...]) + mm_nt(g_fore[at, :], wf[...])
        value = (gh * d4[at, :].astype(f32)).astype(bf16)
        g4[at, :] = value
        b4 += row_sum(value)
    d3 = ins[n_g + 7]
    for at in steps:
        gh = mm_nt(g4[at, :], w4[...])
        value = (gh * d3[at, :].astype(f32)).astype(bf16)
        g3[at, :] = value
        b3 += row_sum(value)
    bias[...] = jnp.concatenate([b3, b4, jnp.zeros((6, 512), f32)], axis=0)


def chain_rear(line, gs, fg, weights, d4, d3, fetch):
    rows = fg.shape[1]
    n = len(gs) + 1 + len(weights)
    return line.run(
        functools.partial(chain_rear_body, len(gs)),
        "chain_rear",
        (*gs, fg, *weights, d4, d3),
        [((rows, 512), bf16)] * 5 + [((8, 512), f32)],
        fetch=(n, n + 1) if fetch else (),
        limit=10 if fetch else 6,
        us=7.0,
    )


def chain_front_body(last, pos, ins, outs, scratch):
    g2, g1, bias = outs[:3]
    g3, w3, w2, w1 = ins[0:4]
    steps = chunks(g1.shape[0])
    b1 = b2 = jnp.zeros((1, 512), f32)
    d2 = ins[4]
    for at in steps:
        gh = mm_nt(g3[at, :], w3[...])
        value = (gh * d2[at, :].astype(f32)).astype(bf16)
        g2[at, :] = value
        b2 += row_sum(value)
    d1 = ins[5]
    for at in steps:
        gh = mm_nt(g2[at, :], w2[...])
        value = (gh * d1[at, :].astype(f32)).astype(bf16)
        g1[at, :] = value
        b1 += row_sum(value)
    for at in steps:
        gh = (2.0 * mm_nt(g1[at, :], w1[...])).astype(bf16)
        if last:
            gh = (gh.astype(f32) + ins[6][at, :].astype(f32)).astype(bf16)
            for r in range(4):
                outs[3 + r][at, :] = gh[:, r * LANES : (r + 1) * LANES]
        else:
            outs[3][at, :] = gh
    bias[...] = jnp.concatenate([b1, b2, jnp.zeros((6, 512), f32)], axis=0)


def chain_front(line, g3, weights, d2, d1, gh2, fetch):
    rows = g3.shape[0]
    last = gh2 is not None
    outs = [((rows, LANES), bf16)] * 4 if last else [((rows, 512), bf16)]
    return line.run(
        functools.partial(chain_front_body, last),
        "chain_front",
        (g3, *weights, d2, d1, *([gh2] if last else [])),
        [((rows, 512), bf16)] * 2 + [((8, 512), f32)] + outs,
        fetch=(4, 5) if fetch else (),
        limit=10 if fetch else 6,
        us=4.5,
    )


def message_rows(k):
    first = {"B": 0, "F": HALF, "V": 2 * HALF, "U": 3 * HALF}
    second = {"L2": 0, "L1": HALF, "bias": 2 * HALF}
    sizes = [3 * HALF + 16, 2 * HALF + 16]
    at = 1 if k else 0
    for name in ("L4", "L3"):
        (first, second)[at][name] = sizes[at]
        sizes[at] += HALF
    return first, second, sizes


def whole_rows(ref):
    return slice(0, ref.shape[0])


def terms_rear_body(k, pos, ins, packed, scratch):
    at, _, _ = message_rows(k)
    g, g_back, g_fore, fg = ins[0:4]
    bt = ins[4]
    value = mm_tn(bt[...], g[...])
    for share in range(GROUPS):
        slot = slot_at(pos, share)
        for r in range(4):
            for j in range(2):
                row, lane = (2 * share + j) * HALF, (2 * j + r // 2) * LANES
                part = value[row : row + HALF, r * LANES : (r + 1) * LANES].astype(bf16)
                packed[r % 2][slot, at["V"] : at["V"] + HALF, lane : lane + LANES] = part
    h4 = ins[5]
    pack_rows(packed, at["B"], mm_tn(h4[...], g_back[...]), pos)
    pack_rows(packed, at["F"], mm_tn(h4[...], g_fore[...]), pos)
    ft = ins[6]
    value = mm(fg[...], ft[...]).T
    rows = slice(at["U"], at["U"] + 16)
    for share in range(GROUPS):
        row, slot = share * 2 * HALF, slot_at(pos, share)
        for j in range(2):
            lanes = slice(j * LANES, (j + 1) * LANES)
            low = value[row + 16 * j : row + 16 * (j + 1), :]
            high = value[row + HALF + 16 * j : row + HALF + 16 * (j + 1), :]
            pack_pair(packed, rows, lanes, slot, low, high, pos)
        for out in packed:
            out[slot, rows, 2 * LANES :] = jnp.zeros((16, 2 * LANES), bf16)
    if "L4" in at:
        h3, h2, g4, g3 = ins[7], ins[8], ins[9], ins[10]
        pack_rows(packed, at["L4"], mm_tn(h3[...], g4[...]), pos)
        pack_rows(packed, at["L3"], mm_tn(h2[...], g3[...]), pos)


def terms_rear(line, k, grads, hidden, more, fetch):
    args = (*grads, *hidden, *more)
    out = ((GROUPS, message_rows(k)[2][0], 512), bf16)
    return line.run(
        functools.partial(terms_rear_body, k),
        "terms_rear",
        args,
        [out, out],
        fetch=[i for i in range(4, min(9, len(args)))] if fetch else (),
        limit=16 if fetch else 6,
        us=4.5 if k else 8.0,
    )


def terms_front_body(k, n_x, pos, ins, packed, scratch):
    _, at, _ = message_rows(k)
    g2, g1, low_bias, high_bias = ins[0:4]
    bias = jnp.concatenate([low_bias[0:2, :], high_bias[0:2, :], jnp.zeros((4, 512), f32)], axis=0)
    bias = jnp.concatenate([bias[:, 0 : 2 * LANES], bias[:, 2 * LANES :]], axis=0).astype(bf16)
    rows = slice(at["bias"], at["bias"] + 16)
    for s in range(GROUPS):
        for out in packed:
            out[s, rows, 0 : 2 * LANES] = jnp.zeros((16, 2 * LANES), bf16)
            out[s, rows, 2 * LANES :] = bias
    xs = ins[4 : 4 + n_x]
    value = mm_tn(columns(xs, whole_rows(g1)), g1[...])
    for r in range(4):
        for i in range(2):
            row = r * LANES + i * 2 * HALF
            pack_pair(
                packed,
                slice(at["L1"], at["L1"] + HALF),
                slice(None),
                slot_at(pos, (pos[2] ^ r) * 2 + i),
                value[row : row + HALF, :],
                value[row + HALF : row + 2 * HALF, :],
                pos,
            )
    h1 = ins[4 + n_x]
    pack_rows(packed, at["L2"], mm_tn(h1[...], g2[...]), pos)
    if "L4" in at:
        h3, h2, g4, g3 = ins[5 + n_x : 9 + n_x]
        pack_rows(packed, at["L4"], mm_tn(h3[...], g4[...]), pos)
        pack_rows(packed, at["L3"], mm_tn(h2[...], g3[...]), pos)


def terms_front(line, k, grads, xs, h1, more, fetch):
    args = (*grads, *xs, h1, *more)
    out = ((GROUPS, message_rows(k)[2][1], 512), bf16)
    return line.run(
        functools.partial(terms_front_body, k, len(xs)),
        "terms_front",
        args,
        [out, out],
        fetch=(4 + len(xs),) if fetch else (),
        limit=8,
        us=5.5 if k else 3.0,
    )


def pack_misc(basis, offsets):
    lead = basis.shape[:-2]
    offsets = jnp.concatenate([offsets, jnp.zeros_like(offsets)], axis=-2)
    return jnp.concatenate(
        [
            basis[..., 0:16, :],
            basis[..., 16:32, :],
            jnp.concatenate([offsets[..., 0 : 2 * LANES], offsets[..., 2 * LANES :]], axis=-2),
        ],
        axis=-1,
    ).reshape(*lead, 16, 512)


def select_body(pos, ins, outs, scratch):
    labels, adjoint = ins[0], ins[1]
    width = adjoint.shape[0]
    for at in chunks(adjoint.shape[1]):
        value = jnp.where(in_group(labels[0:1, at], width), adjoint[:, at], 0.0)
        outs[0][0:width, at] = value.astype(bf16)
    outs[0][width:, :] = jnp.zeros((LANES - width, adjoint.shape[1]), bf16)


def cut_front_body(k, pos, ins, outs, scratch):
    kernels, offsets, basis = ins[0:3]
    out = outs[0]
    half = rows_at(pos[1] * HALF, HALF, HALF)
    for layer in range(2):
        out[0, layer * HALF : (layer + 1) * HALF, :] = kernels[k, layer, half, :].astype(bf16)
    rows, width = slice(2 * HALF, FRONT), basis.shape[2]
    out[0, rows, :] = jnp.zeros((16, 512), bf16)
    for j in range(2):
        part = basis[k, rows_at(pos[1] * HALF + 16 * j, 16, 16), :]
        out[0, rows, j * LANES : j * LANES + width] = part.astype(bf16)
    own = jnp.concatenate([offsets[k], jnp.zeros_like(offsets[k])], axis=0)
    own = jnp.concatenate([jnp.where(pos[0] % 4 == i, own, 0.0) for i in range(4)], axis=1)
    own = jnp.concatenate([jnp.where(pos[0] // 4 == i, own, 0.0) for i in range(2)], axis=0)
    out[0, rows, 2 * LANES :] = own.astype(bf16)


def cut_v_body(pos, ins, outs, scratch):
    outs[0][...] = ins[0][...].astype(bf16)


def pair_v_body(pos, ins, outs, scratch):
    outs[0][...] = jnp.concatenate([ins[0][...], ins[1][...]], axis=2)


def cut_back_body(k, pos, ins, outs, scratch):
    kernels, projection, near, far = ins[0:4]
    half = rows_at(pos[1] * HALF, HALF, HALF)
    parts = (kernels[k, 2, half, :], kernels[k, 3, half, :], projection[k, 0, half, :])
    parts += (projection[k, 1, half, :],)
    parts += (jnp.concatenate([near[k, half, :], far[k, half, :]], axis=1),)
    for m, part in enumerate(parts):
        outs[0][0, m * HALF : (m + 1) * HALF, :] = part.astype(bf16)


def join_body(pos, ins, outs, scratch):
    at = 0
    for ref in ins[0 : len(ins.refs)]:
        outs[0][at : at + ref.shape[0]] = ref[...]
        at += ref.shape[0]


def join(line, *parts):
    count = sum(part.shape[0] for part in parts)
    return line.run(join_body, "join", parts, [((count, *parts[0].shape[1:]), bf16)], limit=2)[0]


def fold_body(n, pos, ins, outs, scratch):
    for s in range(2 * n):
        total = ins[0][s].astype(f32) + ins[1][s].astype(f32)
        if s < n:
            outs[0][s] = total
        else:
            outs[1][s - n] = total.astype(bf16)


def fold(line, kept, arrived):
    n = kept.shape[0] // 2
    tail = kept.shape[1:]
    return line.run(
        functools.partial(fold_body, n),
        "fold",
        (kept, arrived),
        [((n, *tail), f32), ((n, *tail), bf16)],
        limit=4,
    )


def settle_body(pos, ins, outs, scratch):
    outs[0][...] = (ins[0][0] + ins[1][0].astype(f32)).astype(bf16)


def settle(line, kept, arrived):
    return line.run(settle_body, "settle", (kept, arrived), [(kept.shape[1:], bf16)], limit=4)[0]


def finish_body(width, pos, ins, outs, scratch):
    kernels, bias_out, projection, history_basis, forecast_basis = outs
    lower = pos[1] == 0
    for k in range(2):
        first, second, _ = message_rows(k)
        places = {}
        for m, rows in enumerate((first, second)):
            own, core, far, across = ins[8 * k + 4 * m : 8 * k + 4 * m + 4]
            for name, at in rows.items():
                places[name] = (own, core, far, across, at)

        def both(name, height):
            own, core, far, across, at = places[name]
            rows = slice(at, at + height)
            mine = own[rows, :].astype(f32) + far[rows, :].astype(f32)
            other = core[rows, :].astype(f32) + across[rows, :].astype(f32)
            return jnp.where(lower, mine, other), jnp.where(lower, other, mine), mine

        targets = [("B", projection, 0), ("F", projection, 1)]
        targets += [("L" + str(layer + 1), kernels, layer) for layer in range(LAYERS)]
        for name, out, index in targets:
            a, b, _ = both(name, HALF)
            out[k, index, 0:HALF, :] = a
            out[k, index, HALF : 2 * HALF, :] = b
        own, _, far, _, at = places["V"]
        for j in range(2):
            lanes = slice(2 * j * LANES, (2 * j + 1) * LANES)
            theirs = slice((2 * j + 1) * LANES, (2 * j + 2) * LANES)
            rows = slice(at, at + HALF)
            total = own[rows, lanes].astype(f32) + far[rows, theirs].astype(f32)
            history_basis[k, j * HALF : (j + 1) * HALF, :] = total
        a, b, _ = both("U", 16)
        for j, value in enumerate((a, b)):
            for i in range(2):
                row = j * HALF + i * 16
                part = value[:, i * LANES : i * LANES + width]
                forecast_basis[k, row : row + 16, :] = part
        _, _, mine = both("bias", 16)
        bias_out[k, :, 0 : 2 * LANES] = mine[0:8, 2 * LANES :]
        bias_out[k, :, 2 * LANES :] = mine[8:16, 2 * LANES :]


def finish(line, sums, width):
    share = 2 * HALF
    return line.run(
        functools.partial(finish_body, width),
        "finish",
        sums,
        [
            ((2, LAYERS, share, 512), f32),
            ((2, 8, 512), f32),
            ((2, 2, share, 512), f32),
            ((2, share, LANES), f32),
            ((2, share, width), f32),
        ],
        limit=8,
    )


def slots_of(x):
    x = x.reshape(GROUPS, 2, HALF, x.shape[-1]).swapaxes(0, 1)
    return x[:, jnp.array(SLOT_SHARE)]


def rows_of(x):
    x = x[:, jnp.array(SLOT_SHARE)]
    return x.swapaxes(0, 1).reshape(2 * GROUPS * HALF, x.shape[-1])


def four(x):
    return x[0, 0:4], x[0, 4:8], x[1, 0:4], x[1, 4:8]


def shares_plain(kernels, offsets, projection, history_basis, forecast_basis, n_tm):
    tm = lax.axis_index("tm")

    def gather(x, axis, over="dp"):
        return lax.all_gather(x.astype(bf16), over, axis=axis, tiled=True)

    order = [jnp.bitwise_xor(tm, r) for r in range(n_tm)]
    out = []
    for k in range(kernels.shape[0]):
        w = gather(kernels[k], 1)
        b = gather(offsets[k], 1)
        p = gather(projection[k], 1)
        u = gather(forecast_basis[k], 0)
        u = jnp.pad(u, ((0, 0), (0, LANES - u.shape[-1])))
        v = gather(gather(history_basis[k], 0), 1, "tm")
        v = jnp.concatenate(
            [lax.dynamic_slice_in_dim(v, at * LANES, LANES, 1) for at in order], axis=1
        )
        v = slots_of(v)
        other = [v[1, ..., (r ^ 1) * LANES : ((r ^ 1) + 1) * LANES] for r in range(4)]
        v = jnp.stack([v[0], jnp.concatenate(other, axis=-1)])
        offs = jnp.zeros((2, GROUPS, LAYERS, 512), bf16).at[0, 0].set(b)
        misc = pack_misc(slots_of(u), offs)
        first = jnp.concatenate([slots_of(w[0]), slots_of(w[1]), misc], axis=2)
        second = [slots_of(w[2]), slots_of(w[3]), slots_of(p[0]), slots_of(p[1]), v]
        out.append((four(first), four(jnp.concatenate(second, axis=2))))
    return out


def gradients_plain(records, n_tm, width):
    def reduce(x, axis):
        return lax.psum_scatter(
            lax.psum(x.astype(bf16), "tm").astype(f32), "dp", scatter_dimension=axis, tiled=True
        )

    results = [[], [], [], [], []]
    for k, messages in enumerate(records):
        pieces = {}
        for message, rows in zip(messages, message_rows(k)):
            message = jnp.stack(message)
            for name, at in rows.items():
                height = 16 if name in ("U", "bias") else HALF
                pieces[name] = message[:, :, at : at + height, :]
        square = {name: rows_of(pieces[name]) for name in ("L1", "L2", "L3", "L4", "B", "F")}
        results[0].append(reduce(jnp.stack([square["L" + str(i)] for i in range(1, 5)]), 1))
        bias = pieces["bias"][0, 0]
        bias = jnp.concatenate([bias[0:4, 2 * LANES :], bias[8:12, 2 * LANES :]], axis=1)
        results[1].append(reduce(bias, 1))
        results[2].append(reduce(jnp.stack([square["B"], square["F"]]), 1))
        v = pieces["V"][:, jnp.array(SLOT_SHARE)]
        v = jnp.concatenate([v[..., 0 : 2 * LANES], v[..., 2 * LANES :]], axis=2)
        v = v.reshape(2, 2 * GROUPS * HALF, 2, LANES)
        blocks = [v[r % 2, :, r // 2] for r in range(4)]
        total = blocks[0].astype(f32)
        for r in range(1, n_tm):
            total = total + swap(blocks[r], "tm", r, n_tm).astype(f32)
        results[3].append(lax.psum_scatter(total, "dp", scatter_dimension=0, tiled=True))
        u = pieces["U"]
        u = jnp.concatenate([u[..., 0:LANES], u[..., LANES : 2 * LANES]], axis=2)
        results[4].append(reduce(rows_of(u), 0)[:, 0:width])
    return [jnp.stack(x) for x in results]


def body(
    n_dp,
    n_tm,
    history_series,
    frequency_labels,
    affine_kernels,
    affine_offsets,
    expansion_projection,
    history_dictionary,
    prediction_dictionary,
    remainder_adjoint,
    prediction_adjoint,
):
    dp = lax.axis_index("dp")
    tm = lax.axis_index("tm")
    fast = n_dp == GROUPS
    zero = jnp.zeros((), jnp.int32)
    pos = jnp.stack([dp if fast else zero, tm % 2 if fast else zero, tm]).astype(jnp.int32)
    line = Line(pos)
    width = prediction_adjoint.shape[1]
    rows = frequency_labels.shape[0]
    labels = frequency_labels.reshape(1, rows)

    def select():
        args = (labels, prediction_adjoint.T)
        return line.run(select_body, "select", args, [((LANES, rows), bf16)], limit=4)[0]

    first, second = {}, {}
    if fast:
        share = affine_kernels.shape[2]

        def cut_front(k):
            out = [((1, FRONT, 512), bf16)]
            args = (affine_kernels, affine_offsets, prediction_dictionary)
            return line.run(functools.partial(cut_front_body, k), "cut_front", args, out, limit=2)[0]

        def cut_back(k, near, far):
            out = [((1, BACK, 512), bf16)]
            args = (affine_kernels, expansion_projection, near, far)
            return line.run(functools.partial(cut_back_body, k), "cut_back", args, out, limit=2)[0]

        def hop(x, bit):
            return swap(x, "dp", bit, n_dp)

        def core(x):
            return swap(x, "tm", 1, n_tm)

        def relay(x):
            return join(line, x)

        fa = cut_front(0)
        fa_z = hop(fa, 4)
        x1 = exchange(split_windows(line, history_series, n_tm))
        v_shape = history_dictionary.shape
        own_v = line.run(cut_v_body, "cut_v", (history_dictionary,), [(v_shape, bf16)], limit=2)[0]
        pair_shape = (*v_shape[:2], 2 * v_shape[2])
        args = (own_v, core(own_v))
        near = line.run(pair_v_body, "pair_v", args, [(pair_shape, bf16)], limit=2)[0]
        far = swap(near, "tm", 2, n_tm)
        fb = cut_back(0, near, far)
        fb_z = hop(fb, 4)
        fa = join(line, fa, fa_z)
        fa_z = hop(fa, 2)
        sa = cut_front(1)
        sa_z = hop(sa, 4)
        fa_low = join(line, fa, fa_z)
        fa_x, fa_low_c = hop(fa_low, 1), core(fa_low)
        fb = join(line, fb, fb_z)
        fb_z = hop(fb, 2)
        g0 = exchange(split_windows(line, remainder_adjoint, n_tm))
        fg = select()
        sa = join(line, sa, sa_z)
        sa_z = hop(sa, 2)
        sb = cut_back(1, near, far)
        sb_z = hop(sb, 4)
        fa_high = relay(fa_x)
        fa_high_c = core(fa_high)
        fb_low = join(line, fb, fb_z)
        fb_x, fb_low_c = hop(fb_low, 1), core(fb_low)
        first[0] = (fa_low, fa_high, fa_low_c, fa_high_c)
    else:
        masters = (
            affine_kernels,
            affine_offsets,
            expansion_projection,
            history_dictionary,
            prediction_dictionary,
        )
        shares = shares_plain(*masters, n_tm)
        for k in range(2):
            first[k], second[k] = shares[k]
        x1 = exchange(split_windows(line, history_series, n_tm))
        g0 = exchange(split_windows(line, remainder_adjoint, n_tm))
        fg = select()

    w1a, w2a, bias, basis_a, h1, d1, h2, d2 = front(line, first[0], x1)
    if fast:
        sa_low = join(line, sa, sa_z)
        sa_x, sa_low_c = hop(sa_low, 1), core(sa_low)
        sb = join(line, sb, sb_z)
        sb_z = hop(sb, 2)
        fb_high = relay(fb_x)
        fb_high_c = core(fb_high)
        second[0] = (fb_low, fb_high, fb_low_c, fb_high_c)
    outs = rear(line, second[0], h2, bias, basis_a, x1, False, width, (h1, d1, h2, d2))
    w3a, w4a, wba, wfa, wva, h3, d3, h4, d4, bt, ft, x2, cast, fore = outs[:14]
    h1a, d1a, h2a, d2a = outs[14:]
    if fast:
        sa_high = relay(sa_x)
        sa_high_c = core(sa_high)
        sb_low = join(line, sb, sb_z)
        sb_x, sb_low_c = hop(sb_low, 1), core(sb_low)
        first[1] = (sa_low, sa_high, sa_low_c, sa_high_c)
    outs = front(line, first[1], [x2], (h3, d3, h4, d4, bt, ft))
    w1b, w2b, bias, basis_b, h1, d1, h2, d2 = outs[:8]
    h3a, d3a, h4a, d4a, bta, fta = outs[8:]
    if fast:
        sb_high = relay(sb_x)
        sb_high_c = core(sb_high)
        second[1] = (sb_low, sb_high, sb_low_c, sb_high_c)
    outs = rear(line, second[1], h2, bias, basis_b, [cast, fore, labels], True, width)
    w3b, w4b, wbb, wfb, wvb, h3, d3, h4, d4, bt, ft = outs[:11]
    cast, fore = outs[11:15], outs[15]
    remainder_parts = exchange(cast)

    class Message:
        def __init__(self, packed):
            self.packed, self.kept, self.way = packed, packed[0], [1, 2, 4]
            if fast:
                self.arriving = core(packed[1])

        def step(self):
            if not fast:
                return
            self.kept, out = fold(line, self.kept, self.arriving)
            self.arriving = hop(out, self.way.pop(0))

        def last(self):
            if not fast:
                return
            own = settle(line, self.kept, self.arriving)
            self.sums = [own] + [swap(own, "tm", r, n_tm) for r in (1, 2, 3)]

    g, gb, gf, g4, g3, high_bias = chain_rear(line, g0, fg, (wvb, basis_b, wbb, wfb, w4b), d4, d3, False)
    m1 = Message(terms_rear(line, 1, (g, gb, gf, fg), (bt, h4, ft), (), False))
    g2, g1, low_bias, gh2 = chain_front(line, g3, (w3b, w2b, w1b), d2, d1, None, False)
    m1.step()
    more = (h3, h2, g4, g3)
    m2 = Message(terms_front(line, 1, (g2, g1, low_bias, high_bias), [x2], h1, more, False))
    outs = chain_rear(line, [*g0, gh2], fg, (wva, basis_a, wba, wfa, w4a), d4a, d3a, True)
    g, gb, gf, g4, g3, high_bias = outs
    m2.step()
    m1.step()
    more = (h3a, h2a, g4, g3)
    m3 = Message(terms_rear(line, 0, (g, gb, gf, fg), (bta, h4a, fta), more, True))
    m1.step()
    outs = chain_front(line, g3, (w3a, w2a, w1a), d2a, d1a, gh2, True)
    g2, g1, low_bias = outs[:3]
    derivative_parts = exchange(outs[3:7])
    m3.step()
    m2.step()
    m4 = Message(terms_front(line, 0, (g2, g1, low_bias, high_bias), x1, h1a, (), True))
    m1.last()
    m4.step()
    m2.step()
    m3.step()
    remainder = merge_windows(line, history_series, remainder_parts, -1)
    m4.step()
    m2.last()
    m3.step()
    m4.step()
    m3.last()
    derivative = merge_windows(line, remainder_adjoint, derivative_parts, 1)
    m4.last()
    prediction = fore.T
    if fast:
        sums = (*m3.sums, *m4.sums, *m1.sums, *m2.sums)
        kernels, offsets, projection, history_basis, forecast_basis = finish(line, sums, width)
        offsets = lax.dynamic_slice_in_dim(offsets[:, 0:LAYERS], dp * share, share, 2)
    else:
        records = [(m3.packed, m4.packed), (m1.packed, m2.packed)]
        grads = gradients_plain(records, n_tm, width)
        kernels, offsets, projection, history_basis, forecast_basis = grads
    return (
        remainder,
        prediction,
        derivative,
        kernels,
        offsets,
        projection,
        history_basis,
        forecast_basis,
    )


def solution(mesh):
    return jax.shard_map(
        functools.partial(body, mesh.shape["dp"], mesh.shape["tm"]),
        mesh=mesh,
        in_specs=(
            P("dp", "tm"),
            P(("dp", "tm")),
            P(None, None, "dp", None),
            P(None, None, "dp"),
            P(None, None, "dp", None),
            P(None, "dp", "tm"),
            P(None, "dp", None),
            P("dp", "tm"),
            P(("dp", "tm"), None),
        ),
        out_specs=(
            P("dp", "tm"),
            P(("dp", "tm"), None),
            P("dp", "tm"),
            P(None, None, "dp", None),
            P(None, None, "dp"),
            P(None, None, "dp", None),
            P(None, "dp", "tm"),
            P(None, "dp", None),
        ),
        check_vma=False,
    )
```

```python
import functools

import jax
import jax.numpy as jnp
from jax import lax
from jax.experimental import pallas as pl
from jax.experimental.pallas import tpu as pltpu
from jax.sharding import PartitionSpec as P

HOR_Y = 6
HOR_Q = 8
HOR_M = 18
LAYERS = 4
LANES = 128
HALF = 32
GROUPS = 8
FRONT = 2 * HALF + 16
BACK = 4 * HALF
BASIS = 2 * HALF
HOPS = (4, 2, 1)
SLOT_SHARE = tuple(sum(bit for i, bit in enumerate(HOPS) if s >> i & 1) for s in range(GROUPS))
TILE = 512
CHUNK = 256

f32 = jnp.float32
bf16 = jnp.bfloat16
MIB = 1024 * 1024
FLOPS_PER_US = 250_000_000


def mm(a, b):
    return jnp.dot(a, b, preferred_element_type=f32)


def mm_nt(a, b):
    return lax.dot_general(a, b, (((1,), (1,)), ((), ())), preferred_element_type=f32)


def mm_tn(a, b):
    return lax.dot_general(a, b, (((0,), (0,)), ((), ())), preferred_element_type=f32)


def rows_at(start, size, align):
    return pl.ds(pl.multiple_of(start, align), size)


def in_group(labels, width):
    field = lax.broadcasted_iota(jnp.int32, (width, labels.shape[1]), 0)
    group = (
        (field >= HOR_Y).astype(jnp.int32)
        + (field >= HOR_Y + HOR_Q).astype(jnp.int32)
        + (field >= HOR_Y + HOR_Q + HOR_M).astype(jnp.int32)
    )
    return group == labels


def slot_rows(pos, q, s):
    share = pos[0] ^ SLOT_SHARE[s]
    half = pos[1] ^ q
    row = share * (2 * HALF) + half * HALF
    block = share * 2 + half
    window_row = ((block // 4) ^ pos[2]) * LANES + (block % 4) * HALF
    return row, window_row


def slot_at(pos, share):
    r = share ^ pos[0]
    return ((r & 1) << 2) | (r & 2) | ((r >> 2) & 1)


def size_of(shape):
    total = 1
    for extent in shape:
        total *= extent
    return total


class Inputs:
    def __init__(self, refs, copies):
        self.refs, self.copies = refs, copies

    def __getitem__(self, i):
        if isinstance(i, slice):
            return [self[j] for j in range(*i.indices(len(self.refs)))]
        if i in self.copies:
            self.copies.pop(i).wait()
        return self.refs[i]


class Line:
    def __init__(self, pos):
        self.pos, self.token = pos, None

    def run(self, body, name, args, outs, scratch=(), fetch=(), save=(), limit=12, after=(), us=0.5, stay=(), out_stays=False):
        token = [] if self.token is None else [self.token]
        extra = [*after, *token]
        fetch, save = list(fetch), list(save)
        n_in, n_out, n_extra = len(args), len(outs), len(extra)
        n_fetch, n_save = len(fetch), len(save)

        def kernel(pos_ref, *refs):
            refs = list(refs)
            given, refs = refs[:n_in], refs[n_in + n_extra :]
            results, refs = refs[:n_out], refs[n_out:]
            saved, refs = refs[:n_save], refs[n_save:]
            if out_stays:
                refs.pop(0)[...] = jnp.zeros((8, LANES), f32)
            landing, refs = refs[:n_fetch], refs[n_fetch:]
            sems = refs.pop() if n_fetch + n_save else None
            inputs, copies, leaving = list(given), {}, []
            for at, (i, buf) in enumerate(zip(fetch, landing)):
                copies[i] = pltpu.make_async_copy(given[i], buf, sems.at[at])
                copies[i].start()
                inputs[i] = buf
            for at, (i, dst) in enumerate(zip(save, saved)):
                leaving.append(pltpu.make_async_copy(given[i], dst, sems.at[n_fetch + at]))
                leaving[-1].start()
            body(pos_ref, Inputs(inputs, copies), results, refs)
            for copy in (*copies.values(), *leaving):
                copy.wait()

        vmem, hbm = pl.BlockSpec(memory_space=pltpu.VMEM), pl.BlockSpec(memory_space=pltpu.HBM)
        anywhere = pl.BlockSpec(memory_space=pl.ANY)
        place = pltpu.HBM if out_stays else jax.ShapeDtypeStruct
        shapes = [place(shape, dtype) for shape, dtype in outs]
        placed = [
            pltpu.with_memory_space_constraint(a, pltpu.HBM) if i in fetch or i in stay else a
            for i, a in enumerate(args)
        ]
        shapes += [pltpu.HBM(args[i].shape, args[i].dtype) for i in save]
        mark = [jax.ShapeDtypeStruct((8, LANES), f32)] if out_stays else []
        sems = [pltpu.SemaphoreType.DMA((n_fetch + n_save,))] if n_fetch + n_save else []
        results = list(pl.pallas_call(
            kernel,
            name=name,
            out_shape=shapes + mark,
            in_specs=[pl.BlockSpec(memory_space=pltpu.SMEM)]
            + [hbm if i in fetch or i in stay else vmem for i in range(n_in)]
            + [anywhere] * n_extra,
            out_specs=[hbm if out_stays else vmem] * n_out + [hbm] * n_save + [vmem] * len(mark),
            scratch_shapes=[pltpu.VMEM(args[i].shape, args[i].dtype) for i in fetch]
            + list(scratch)
            + sems,
            compiler_params=pltpu.CompilerParams(vmem_limit_bytes=limit * MIB),
            cost_estimate=pl.CostEstimate(
                flops=int(us * FLOPS_PER_US), bytes_accessed=1, transcendentals=0
            ),
        )(self.pos, *placed, *extra))
        if out_stays:
            self.token = results.pop()
        else:
            self.token = min(results, key=lambda a: a.size * a.dtype.itemsize)
        return results


def swap(x, axis, bit, size):
    return lax.ppermute(x, axis, [(i, i ^ bit) for i in range(size)])


class Exchange:
    def __init__(self, line, pieces, n_tm):
        self.line, self.n_tm = line, n_tm
        self.own, near, far = pieces
        self.far = swap(far, "tm", 2, n_tm)
        self.near = swap(near, "tm", 1, n_tm)

    def relay(self):
        shape = self.far.shape[1:]
        out = [(shape, bf16)]
        across = self.line.run(relay_body, "relay", (self.far,), out, limit=2)[0]
        self.across = swap(across, "tm", 1, self.n_tm)

    def pieces(self):
        return [self.own, self.near, self.far, self.across]


def relay_body(pos, ins, outs, scratch):
    outs[0][...] = ins[0][1]


def flat(refs):
    return [ref if len(ref.shape) == 2 else ref.at[0] for ref in refs]


def split_body(with_basis, pos, ins, outs, scratch):
    landing, sems = scratch
    rows = landing.shape[1]
    copies = []
    for r in range(4):
        copies.append(pltpu.make_async_copy(ins[0].at[pos[2] ^ r], landing.at[r], sems.at[r]))
    for r in (2, 3, 1, 0):
        copies[r].start()
    if with_basis:
        for k in range(2):
            at = slice(rows + 2 * HALF * k, rows + 2 * HALF * (k + 1))
            value = ins[1][k].astype(bf16)
            for out in (outs[1], outs[2].at[0], outs[2].at[1]):
                out[at, :] = value
    for r in (2, 3, 1, 0):
        copies[r].wait()
        out = outs[2].at[r - 2] if r >= 2 else outs[r]
        out[0:rows, :] = landing[r].astype(bf16)


def piece_shapes(rows, more=0):
    sent = rows + more
    return [((rows, LANES), bf16), ((sent, LANES), bf16), ((2, sent, LANES), bf16)]


def split_windows(line, array, parts, basis=None):
    shape = (parts, array.shape[0] // parts, LANES)
    args = (array.reshape(shape),) if basis is None else (array.reshape(shape), basis)
    return line.run(
        functools.partial(split_body, basis is not None),
        "split_windows",
        args,
        piece_shapes(shape[1], 0 if basis is None else 2 * basis.shape[1]),
        [pltpu.VMEM(shape, f32), pltpu.SemaphoreType.DMA((parts,))],
        stay=(0,),
        limit=8,
        us=2.0,
    )


def merge_body(sign, pos, ins, outs, scratch):
    base, pieces = ins[0], flat(ins[1:5])
    landing, leaving, sems = scratch
    parts = len(pieces)
    arrive, leave = [], []
    for r in range(parts):
        at = pos[2] ^ r
        arrive.append(pltpu.make_async_copy(base.at[at], landing.at[r], sems.at[r]))
        leave.append(pltpu.make_async_copy(leaving.at[r], outs[0].at[at], sems.at[parts + r]))
        arrive[-1].start()
    for r, piece in enumerate(pieces):
        arrive[r].wait()
        value = piece[...].astype(f32)
        leaving[r] = landing[r] - value if sign < 0 else landing[r] + value
        leave[r].start()
    for copy in leave:
        copy.wait()


def merge_windows(line, base, pieces, sign):
    parts = len(pieces)
    shape = (parts, base.shape[0] // parts, LANES)
    out = line.run(
        functools.partial(merge_body, sign),
        "merge_windows",
        (base.reshape(shape), *pieces),
        [(shape, f32)],
        [pltpu.VMEM(shape, f32), pltpu.VMEM(shape, f32), pltpu.SemaphoreType.DMA((2 * parts,))],
        stay=(0,),
        out_stays=True,
        limit=12,
        us=3.5,
    )[0]
    return out.reshape(base.shape)


def activate(p):
    t = jnp.tanh(p)
    u = 1.0 + t
    h = p * u
    return h.astype(bf16), u + h * (1.0 - t)


def columns(refs, at):
    if len(refs) == 1:
        return refs[0][at, :]
    return jnp.concatenate([ref[at, :] for ref in refs], axis=1)


def put_pieces(refs, at, value):
    for r in range(4):
        ref = refs[2].at[r - 2] if r >= 2 else refs[r]
        ref[at, :] = value[:, r * LANES : (r + 1) * LANES]


def chunks(rows):
    return [slice(at, at + CHUNK) for at in range(0, rows, CHUNK)]


def front_body(n_x, pos, ins, bufs, scratch):
    w1, w2, bias, basis, h1, d1, h2, d2 = bufs
    total = jnp.zeros((16, 2 * LANES), f32)
    for q in range(2):
        for s in range(GROUPS):
            ref, i = ins[2 * q + s // 4], s % 4
            row, window_row = slot_rows(pos, q, s)
            w1[rows_at(window_row, HALF, HALF), :] = ref[i, 0:HALF, :] * 0.5
            w2[rows_at(row, HALF, HALF), :] = ref[i, HALF : 2 * HALF, :] * 0.5
            low = ref[i, 2 * HALF : FRONT, 0:LANES]
            high = ref[i, 2 * HALF : FRONT, LANES : 2 * LANES]
            basis[rows_at(row, 16, 16), :] = low
            basis[rows_at(row + 16, 16, 16), :] = high
            if q == 0:
                total += ref[i, 2 * HALF : FRONT, 2 * LANES :].astype(f32)
    bias[:, 0 : 2 * LANES] = total[0:8] * 0.5
    bias[:, 2 * LANES :] = total[8:16] * 0.5
    xs = flat(ins[4 : 4 + n_x])
    for at in chunks(h1.shape[0]):
        h, d = activate(mm(columns(xs, at), w1[...]) + bias[0:1, :])
        h1[at, :] = h
        d1[at, :] = d.astype(bf16)
    for at in chunks(h1.shape[0]):
        h, d = activate(mm(h1[at, :], w2[...]) + bias[1:2, :])
        h2[at, :] = h
        d2[at, :] = d.astype(bf16)


def front(line, slots, xs, rows, leaving=()):
    square = ((512, 512), bf16)
    hidden = ((rows, 512), bf16)
    args = (*slots, *xs, *leaving)
    return line.run(
        functools.partial(front_body, len(xs)),
        "front",
        args,
        [square, square, ((8, 512), f32), ((512, LANES), bf16), hidden, hidden, hidden, hidden],
        save=range(len(args) - len(leaving), len(args)),
        limit=6,
        us=4.0,
    )


def rear_body(last, pos, ins, bufs, scratch):
    w3, w4, wb, wf, h3, d3, h4, d4, bt, ft, fore_out = bufs
    for q in range(2):
        for s in range(GROUPS):
            ref, i = ins[2 * q + s // 4], s % 4
            row, _ = slot_rows(pos, q, s)
            for m, w in enumerate((w3, w4, wb, wf)):
                part = ref[i, m * HALF : (m + 1) * HALF, :]
                w[rows_at(row, HALF, HALF), :] = part * 0.5 if m < 2 else part
    bias, h2, basis = ins[4], ins[5], ins[6]
    steps = chunks(h3.shape[0])
    for at in steps:
        h, d = activate(mm(h2[at, :], w3[...]) + bias[2:3, :])
        h3[at, :] = h
        d3[at, :] = d.astype(bf16)
    for at in steps:
        h, d = activate(mm(h3[at, :], w4[...]) + bias[3:4, :])
        h4[at, :] = h
        d4[at, :] = (0.5 * d).astype(bf16)
    for at in steps:
        bt[at, :] = mm(h4[at, :], wb[...]).astype(bf16)
    for at in steps:
        ft[at, :] = mm(h4[at, :], wf[...]).astype(bf16)
    width = fore_out.shape[0]
    for at in steps:
        fore = mm(ft[at, :], basis[...]).T[0:width, :]
        if last:
            fore = ins[7][:, at] + fore
            fore = jnp.where(in_group(ins[8][0:1, at], width), fore, 0.0)
        fore_out[:, at] = fore


def rear(line, slots, h2, bias, basis, extra, width, leaving=()):
    rows = h2.shape[0]
    square = ((512, 512), bf16)
    hidden = ((rows, 512), bf16)
    args = (*slots, bias, h2, basis, *extra, *leaving)
    return line.run(
        functools.partial(rear_body, bool(extra)),
        "rear",
        args,
        [square] * 4 + [hidden] * 6 + [((width, rows), f32)],
        save=range(len(args) - len(leaving), len(args)),
        limit=6,
        us=6.5,
    )


def cast_body(k, pos, ins, bufs, scratch):
    wv = bufs[0]
    for q in range(2):
        for s in range(GROUPS):
            ref, i = ins[2 * q + s // 4], s % 4
            row, _ = slot_rows(pos, q, s)
            for r in range(4):
                part = ref[i, k * HALF : (k + 1) * HALF, r * LANES : (r + 1) * LANES]
                at = r ^ q
                wv[rows_at(row, HALF, HALF), at * LANES : (at + 1) * LANES] = part
    bt = ins[4]
    for at in chunks(bt.shape[0]):
        cast = mm(bt[at, :], wv[...])
        if k == 0:
            bufs[1][at, :] = (columns(flat(ins[5:9]), at).astype(f32) - cast).astype(bf16)
            bufs[2][at, :] = cast
        else:
            put_pieces(bufs[1:4], at, (cast + ins[5][at, :]).astype(bf16))


def backcast(line, k, slots, bt, extra):
    rows = bt.shape[0]
    hidden = (rows, 512)
    outs = [(hidden, bf16), (hidden, f32)] if k == 0 else piece_shapes(rows)
    return line.run(
        functools.partial(cast_body, k),
        "backcast",
        (*slots, bt, *extra),
        [((512, 512), bf16)] + outs,
        limit=6,
        us=1.5,
    )


def row_sum(value):
    return jnp.sum(value.astype(f32), axis=0, keepdims=True)


def pack_pair(packed, rows, lanes, slot, first, second, pos):
    keep, send = packed
    lower = pos[1] == 0
    first, second = first.astype(bf16), second.astype(bf16)
    keep[slot, rows, lanes] = jnp.where(lower, first, second)
    send[slot, rows, lanes] = jnp.where(lower, second, first)


def pack_rows(packed, at, value, pos):
    for share in range(GROUPS):
        row = share * 2 * HALF
        pack_pair(
            packed,
            slice(at, at + HALF),
            slice(None),
            slot_at(pos, share),
            value[row : row + HALF, :],
            value[row + HALF : row + 2 * HALF, :],
            pos,
        )


def chain_rear_body(n_g, pos, ins, outs, scratch):
    g, g_back, g_fore, g4, g3, bias = outs
    wv, basis, wb, wf, w4 = ins[n_g + 1 : n_g + 6]
    gs, fg = flat(ins[0:4]) + ins[4:n_g], ins[n_g]
    steps = chunks(g.shape[0])
    for at in steps:
        value = columns(gs[:4], at)
        if n_g == 5:
            value = (value.astype(f32) + gs[4][at, :].astype(f32)).astype(bf16)
        g[at, :] = -value
        g_back[at, :] = mm_nt(g[at, :], wv[...]).astype(bf16)
    for at in steps:
        g_fore[at, :] = mm_nt(fg[:, at].T, basis[...]).astype(bf16)
    d4 = ins[n_g + 6]
    b3 = b4 = jnp.zeros((1, 512), f32)
    for at in steps:
        gh = mm_nt(g_back[at, :], wb[...]) + mm_nt(g_fore[at, :], wf[...])
        value = (gh * d4[at, :].astype(f32)).astype(bf16)
        g4[at, :] = value
        b4 += row_sum(value)
    d3 = ins[n_g + 7]
    for at in steps:
        gh = mm_nt(g4[at, :], w4[...])
        value = (gh * d3[at, :].astype(f32)).astype(bf16)
        g3[at, :] = value
        b3 += row_sum(value)
    bias[...] = jnp.concatenate([b3, b4, jnp.zeros((6, 512), f32)], axis=0)


def chain_rear(line, gs, fg, weights, d4, d3, fetch):
    rows = fg.shape[1]
    n = len(gs) + 1 + len(weights)
    return line.run(
        functools.partial(chain_rear_body, len(gs)),
        "chain_rear",
        (*gs, fg, *weights, d4, d3),
        [((rows, 512), bf16)] * 5 + [((8, 512), f32)],
        fetch=(n, n + 1) if fetch else (),
        limit=10 if fetch else 6,
        us=7.0,
    )


def chain_front_body(last, pos, ins, outs, scratch):
    g2, g1, bias = outs[:3]
    g3, w3, w2, w1 = ins[0:4]
    steps = chunks(g1.shape[0])
    b1 = b2 = jnp.zeros((1, 512), f32)
    d2 = ins[4]
    for at in steps:
        gh = mm_nt(g3[at, :], w3[...])
        value = (gh * d2[at, :].astype(f32)).astype(bf16)
        g2[at, :] = value
        b2 += row_sum(value)
    d1 = ins[5]
    for at in steps:
        gh = mm_nt(g2[at, :], w2[...])
        value = (gh * d1[at, :].astype(f32)).astype(bf16)
        g1[at, :] = value
        b1 += row_sum(value)
    for at in steps:
        gh = (2.0 * mm_nt(g1[at, :], w1[...])).astype(bf16)
        if last:
            gh = (gh.astype(f32) + ins[6][at, :].astype(f32)).astype(bf16)
            put_pieces(outs[3:6], at, gh)
        else:
            outs[3][at, :] = gh
    bias[...] = jnp.concatenate([b1, b2, jnp.zeros((6, 512), f32)], axis=0)


def chain_front(line, g3, weights, d2, d1, gh2, fetch):
    rows = g3.shape[0]
    last = gh2 is not None
    outs = piece_shapes(rows) if last else [((rows, 512), bf16)]
    return line.run(
        functools.partial(chain_front_body, last),
        "chain_front",
        (g3, *weights, d2, d1, *([gh2] if last else [])),
        [((rows, 512), bf16)] * 2 + [((8, 512), f32)] + outs,
        fetch=(4, 5) if fetch else (),
        limit=10 if fetch else 6,
        us=4.5,
    )


def message_rows(k):
    first = {"B": 0, "F": HALF, "V": 2 * HALF, "U": 3 * HALF}
    second = {"L2": 0, "L1": HALF, "bias": 2 * HALF}
    sizes = [3 * HALF + 16, 2 * HALF + 16]
    at = 1 if k else 0
    for name in ("L4", "L3"):
        (first, second)[at][name] = sizes[at]
        sizes[at] += HALF
    return first, second, sizes


def whole_rows(ref):
    return slice(0, ref.shape[0])


def terms_rear_body(k, pos, ins, packed, scratch):
    at, _, _ = message_rows(k)
    g, g_back, g_fore, fg = ins[0:4]
    bt = ins[4]
    value = mm_tn(bt[...], g[...])
    for share in range(GROUPS):
        slot = slot_at(pos, share)
        for r in range(4):
            for j in range(2):
                row, lane = (2 * share + j) * HALF, (2 * j + r // 2) * LANES
                part = value[row : row + HALF, r * LANES : (r + 1) * LANES].astype(bf16)
                packed[r % 2][slot, at["V"] : at["V"] + HALF, lane : lane + LANES] = part
    h4 = ins[5]
    pack_rows(packed, at["B"], mm_tn(h4[...], g_back[...]), pos)
    pack_rows(packed, at["F"], mm_tn(h4[...], g_fore[...]), pos)
    ft = ins[6]
    value = mm(fg[...], ft[...]).T
    rows = slice(at["U"], at["U"] + 16)
    for share in range(GROUPS):
        row, slot = share * 2 * HALF, slot_at(pos, share)
        for j in range(2):
            lanes = slice(j * LANES, (j + 1) * LANES)
            low = value[row + 16 * j : row + 16 * (j + 1), :]
            high = value[row + HALF + 16 * j : row + HALF + 16 * (j + 1), :]
            pack_pair(packed, rows, lanes, slot, low, high, pos)
        for out in packed:
            out[slot, rows, 2 * LANES :] = jnp.zeros((16, 2 * LANES), bf16)
    if "L4" in at:
        h3, h2, g4, g3 = ins[7], ins[8], ins[9], ins[10]
        pack_rows(packed, at["L4"], mm_tn(h3[...], g4[...]), pos)
        pack_rows(packed, at["L3"], mm_tn(h2[...], g3[...]), pos)


def terms_rear(line, k, grads, hidden, more, fetch):
    args = (*grads, *hidden, *more)
    out = ((GROUPS, message_rows(k)[2][0], 512), bf16)
    return line.run(
        functools.partial(terms_rear_body, k),
        "terms_rear",
        args,
        [out, out],
        fetch=[i for i in range(4, min(9, len(args)))] if fetch else (),
        limit=16 if fetch else 6,
        us=4.5 if k else 8.0,
    )


def terms_front_body(k, n_x, pos, ins, packed, scratch):
    _, at, _ = message_rows(k)
    g2, g1, low_bias, high_bias = ins[0:4]
    bias = jnp.concatenate([low_bias[0:2, :], high_bias[0:2, :], jnp.zeros((4, 512), f32)], axis=0)
    bias = jnp.concatenate([bias[:, 0 : 2 * LANES], bias[:, 2 * LANES :]], axis=0).astype(bf16)
    rows = slice(at["bias"], at["bias"] + 16)
    for s in range(GROUPS):
        for out in packed:
            out[s, rows, 0 : 2 * LANES] = jnp.zeros((16, 2 * LANES), bf16)
            out[s, rows, 2 * LANES :] = bias
    xs = flat(ins[4 : 4 + n_x])
    value = mm_tn(columns(xs, whole_rows(g1)), g1[...])
    for r in range(4):
        for i in range(2):
            row = r * LANES + i * 2 * HALF
            pack_pair(
                packed,
                slice(at["L1"], at["L1"] + HALF),
                slice(None),
                slot_at(pos, (pos[2] ^ r) * 2 + i),
                value[row : row + HALF, :],
                value[row + HALF : row + 2 * HALF, :],
                pos,
            )
    h1 = ins[4 + n_x]
    pack_rows(packed, at["L2"], mm_tn(h1[...], g2[...]), pos)
    if "L4" in at:
        h3, h2, g4, g3 = ins[5 + n_x : 9 + n_x]
        pack_rows(packed, at["L4"], mm_tn(h3[...], g4[...]), pos)
        pack_rows(packed, at["L3"], mm_tn(h2[...], g3[...]), pos)


def terms_front(line, k, grads, xs, h1, more, fetch):
    args = (*grads, *xs, h1, *more)
    out = ((GROUPS, message_rows(k)[2][1], 512), bf16)
    return line.run(
        functools.partial(terms_front_body, k, len(xs)),
        "terms_front",
        args,
        [out, out],
        fetch=(4 + len(xs),) if fetch else (),
        limit=8,
        us=5.5 if k else 3.0,
    )


def pack_misc(basis, offsets):
    lead = basis.shape[:-2]
    offsets = jnp.concatenate([offsets, jnp.zeros_like(offsets)], axis=-2)
    return jnp.concatenate(
        [
            basis[..., 0:16, :],
            basis[..., 16:32, :],
            jnp.concatenate([offsets[..., 0 : 2 * LANES], offsets[..., 2 * LANES :]], axis=-2),
        ],
        axis=-1,
    ).reshape(*lead, 16, 512)


def select_body(pos, ins, outs, scratch):
    labels, adjoint = ins[0], ins[1]
    width = adjoint.shape[0]
    for at in chunks(adjoint.shape[1]):
        value = jnp.where(in_group(labels[0:1, at], width), adjoint[:, at], 0.0)
        outs[0][0:width, at] = value.astype(bf16)
    outs[0][width:, :] = jnp.zeros((LANES - width, adjoint.shape[1]), bf16)


def cut_front_body(k, pos, ins, outs, scratch):
    kernels, basis, offsets = ins[0:3]
    rows_in, basis_in, sems = scratch
    out = outs[0]
    half = rows_at(pos[1] * HALF, HALF, HALF)
    copies = [
        pltpu.make_async_copy(kernels.at[k, 0:2, half, :], rows_in, sems.at[0]),
        pltpu.make_async_copy(basis.at[k, half, :], basis_in, sems.at[1]),
    ]
    for copy in copies:
        copy.start()
    rows, width = slice(2 * HALF, FRONT), basis.shape[2]
    out[0, rows, :] = jnp.zeros((16, 512), bf16)
    own = jnp.concatenate([offsets[k], jnp.zeros_like(offsets[k])], axis=0)
    own = jnp.concatenate([jnp.where(pos[0] % 4 == i, own, 0.0) for i in range(4)], axis=1)
    own = jnp.concatenate([jnp.where(pos[0] // 4 == i, own, 0.0) for i in range(2)], axis=0)
    out[0, rows, 2 * LANES :] = own.astype(bf16)
    copies[1].wait()
    for j in range(2):
        part = basis_in[16 * j : 16 * (j + 1), :]
        out[0, rows, j * LANES : j * LANES + width] = part.astype(bf16)
    copies[0].wait()
    for layer in range(2):
        out[0, layer * HALF : (layer + 1) * HALF, :] = rows_in[layer].astype(bf16)


def cut_back_body(k, pos, ins, outs, scratch):
    kernels, projection = ins[0:2]
    rows_in, pair_in, sems = scratch
    half = rows_at(pos[1] * HALF, HALF, HALF)
    copies = [
        pltpu.make_async_copy(kernels.at[k, 2:4, half, :], rows_in, sems.at[0]),
        pltpu.make_async_copy(projection.at[k, :, half, :], pair_in, sems.at[1]),
    ]
    for copy in copies:
        copy.start()
    for m, landed in enumerate((rows_in, pair_in)):
        copies[m].wait()
        for i in range(2):
            at = (2 * m + i) * HALF
            outs[0][0, at : at + HALF, :] = landed[i].astype(bf16)


def cut_basis_body(pos, ins, outs, scratch):
    own, near, far, across = ins[0:4]
    first = near.shape[0] - 4 * HALF
    for k in range(2):
        at = first + 2 * HALF * k + pos[1] * HALF
        parts = [own[k, rows_at(pos[1] * HALF, HALF, HALF), :].astype(bf16)]
        parts += [ref[rows_at(at, HALF, HALF), :] for ref in (near, far.at[0], across)]
        outs[0][0, k * HALF : (k + 1) * HALF, :] = jnp.concatenate(parts, axis=1)


def join_body(pos, ins, outs, scratch):
    at = 0
    for ref in ins[0 : len(ins.refs)]:
        outs[0][at : at + ref.shape[0]] = ref[...]
        at += ref.shape[0]


def join(line, *parts):
    count = sum(part.shape[0] for part in parts)
    return line.run(join_body, "join", parts, [((count, *parts[0].shape[1:]), bf16)], limit=2)[0]


def fold_body(n, pos, ins, outs, scratch):
    at = 0
    for kept, arrived in zip(ins[0 : len(ins.refs) : 2], ins[1 : len(ins.refs) : 2]):
        rows = slice(at, at + kept.shape[1])
        at += kept.shape[1]
        for s in range(2 * n):
            total = kept[s].astype(f32) + arrived[s].astype(f32)
            if s < n:
                outs[0][s, rows, :] = total
            else:
                outs[1][s - n, rows, :] = total.astype(bf16)


def fold(line, *terms):
    n = terms[0].shape[0] // 2
    shape = (n, sum(term.shape[1] for term in terms[::2]), terms[0].shape[2])
    return line.run(
        functools.partial(fold_body, n),
        "fold",
        terms,
        [(shape, f32), (shape, bf16)],
        limit=4,
    )


def settle_body(pos, ins, outs, scratch):
    outs[0][...] = (ins[0][0] + ins[1][0].astype(f32)).astype(bf16)


def settle(line, kept, arrived):
    return line.run(settle_body, "settle", (kept, arrived), [(kept.shape[1:], bf16)], limit=4)[0]


def finish_body(width, pos, ins, outs, scratch):
    kernels, bias_out, projection, history_basis, forecast_basis = outs
    lower = pos[1] == 0
    for k in range(2):
        first, second, sizes = message_rows(k)
        places = {}
        for m, rows in enumerate((first, second)):
            one = 0 if k else 4 * m
            own, core, far, across = ins[8 * k + one : 8 * k + one + 4]
            for name, at in rows.items():
                places[name] = (own, core, far, across, at + (sizes[0] if k and m else 0))

        def both(name, height):
            own, core, far, across, at = places[name]
            rows = slice(at, at + height)
            mine = own[rows, :].astype(f32) + far[rows, :].astype(f32)
            other = core[rows, :].astype(f32) + across[rows, :].astype(f32)
            return jnp.where(lower, mine, other), jnp.where(lower, other, mine), mine

        targets = [("B", projection, 0), ("F", projection, 1)]
        targets += [("L" + str(layer + 1), kernels, layer) for layer in range(LAYERS)]
        for name, out, index in targets:
            a, b, _ = both(name, HALF)
            out[k, index, 0:HALF, :] = a
            out[k, index, HALF : 2 * HALF, :] = b
        own, _, far, _, at = places["V"]
        for j in range(2):
            lanes = slice(2 * j * LANES, (2 * j + 1) * LANES)
            theirs = slice((2 * j + 1) * LANES, (2 * j + 2) * LANES)
            rows = slice(at, at + HALF)
            total = own[rows, lanes].astype(f32) + far[rows, theirs].astype(f32)
            history_basis[k, j * HALF : (j + 1) * HALF, :] = total
        a, b, _ = both("U", 16)
        for j, value in enumerate((a, b)):
            for i in range(2):
                row = j * HALF + i * 16
                part = value[:, i * LANES : i * LANES + width]
                forecast_basis[k, row : row + 16, :] = part
        _, _, mine = both("bias", 16)
        total = jnp.zeros(bias_out.shape[1:], f32)
        for share in range(GROUPS):
            row, lane = 8 * (share // 4), 2 * LANES + (share % 4) * 2 * HALF
            part = mine[row : row + LAYERS, lane : lane + 2 * HALF]
            total = total + jnp.where(pos[0] == share, part, 0.0)
        bias_out[k] = total


def finish(line, sums, width):
    share = 2 * HALF
    return line.run(
        functools.partial(finish_body, width),
        "finish",
        sums,
        [
            ((2, LAYERS, share, 512), f32),
            ((2, LAYERS, share), f32),
            ((2, 2, share, 512), f32),
            ((2, share, LANES), f32),
            ((2, share, width), f32),
        ],
        limit=8,
    )


def slots_of(x):
    x = x.reshape(GROUPS, 2, HALF, x.shape[-1]).swapaxes(0, 1)
    return x[:, jnp.array(SLOT_SHARE)]


def in_order(x):
    return x[:, jnp.array([SLOT_SHARE.index(share) for share in range(GROUPS)])]


def rows_of(x):
    return in_order(x).swapaxes(0, 1).reshape(2 * GROUPS * HALF, x.shape[-1])


def four(x):
    return x[0, 0:4], x[0, 4:8], x[1, 0:4], x[1, 4:8]


def shares_plain(kernels, offsets, projection, history_basis, forecast_basis, n_tm):
    tm = lax.axis_index("tm")

    def gather(x, axis, over="dp"):
        return lax.all_gather(x.astype(bf16), over, axis=axis, tiled=True)

    order = [jnp.bitwise_xor(tm, r) for r in range(n_tm)]
    out, bases = [], []
    for k in range(kernels.shape[0]):
        w = gather(kernels[k], 1)
        b = gather(offsets[k], 1)
        p = gather(projection[k], 1)
        u = gather(forecast_basis[k], 0)
        u = jnp.pad(u, ((0, 0), (0, LANES - u.shape[-1])))
        v = gather(gather(history_basis[k], 0), 1, "tm")
        v = jnp.concatenate(
            [lax.dynamic_slice_in_dim(v, at * LANES, LANES, 1) for at in order], axis=1
        )
        v = slots_of(v)
        other = [v[1, ..., (r ^ 1) * LANES : ((r ^ 1) + 1) * LANES] for r in range(4)]
        v = jnp.stack([v[0], jnp.concatenate(other, axis=-1)])
        offs = jnp.zeros((2, GROUPS, LAYERS, 512), bf16).at[0, 0].set(b)
        misc = pack_misc(slots_of(u), offs)
        first = jnp.concatenate([slots_of(w[0]), slots_of(w[1]), misc], axis=2)
        second = jnp.concatenate([slots_of(x) for x in (w[2], w[3], p[0], p[1])], axis=2)
        out.append((four(first), four(second)))
        bases.append(v)
    return out, four(jnp.concatenate(bases, axis=2))


def gradients_plain(records, n_tm, width):
    def reduce(x, axis):
        return lax.psum_scatter(
            lax.psum(x.astype(bf16), "tm").astype(f32), "dp", scatter_dimension=axis, tiled=True
        )

    results = [[], [], [], [], []]
    for k, messages in enumerate(records):
        pieces = {}
        for message, rows in zip(messages, message_rows(k)):
            message = jnp.stack(message)
            for name, at in rows.items():
                height = 16 if name in ("U", "bias") else HALF
                pieces[name] = message[:, :, at : at + height, :]
        square = {name: rows_of(pieces[name]) for name in ("L1", "L2", "L3", "L4", "B", "F")}
        results[0].append(reduce(jnp.stack([square["L" + str(i)] for i in range(1, 5)]), 1))
        bias = pieces["bias"][0, 0]
        bias = jnp.concatenate([bias[0:4, 2 * LANES :], bias[8:12, 2 * LANES :]], axis=1)
        results[1].append(reduce(bias, 1))
        results[2].append(reduce(jnp.stack([square["B"], square["F"]]), 1))
        v = in_order(pieces["V"])
        v = jnp.concatenate([v[..., 0 : 2 * LANES], v[..., 2 * LANES :]], axis=2)
        v = v.reshape(2, 2 * GROUPS * HALF, 2, LANES)
        blocks = [v[r % 2, :, r // 2] for r in range(4)]
        total = blocks[0].astype(f32)
        for r in range(1, n_tm):
            total = total + swap(blocks[r], "tm", r, n_tm).astype(f32)
        results[3].append(lax.psum_scatter(total, "dp", scatter_dimension=0, tiled=True))
        u = pieces["U"]
        u = jnp.concatenate([u[..., 0:LANES], u[..., LANES : 2 * LANES]], axis=2)
        results[4].append(reduce(rows_of(u), 0)[:, 0:width])
    return [jnp.stack(x) for x in results]


def body(
    n_dp,
    n_tm,
    history_series,
    frequency_labels,
    affine_kernels,
    affine_offsets,
    expansion_projection,
    history_dictionary,
    prediction_dictionary,
    remainder_adjoint,
    prediction_adjoint,
):
    dp = lax.axis_index("dp")
    tm = lax.axis_index("tm")
    fast = n_dp == GROUPS
    zero = jnp.zeros((), jnp.int32)
    pos = jnp.stack([dp if fast else zero, tm % 2 if fast else zero, tm]).astype(jnp.int32)
    line = Line(pos)
    width = prediction_adjoint.shape[1]
    rows = frequency_labels.shape[0]
    labels = frequency_labels.reshape(1, rows)

    def select():
        args = (labels, prediction_adjoint.T)
        return line.run(select_body, "select", args, [((LANES, rows), bf16)], limit=4)[0]

    def hop(x, bit):
        return swap(x, "dp", bit, n_dp)

    def core(x):
        return swap(x, "tm", 1, n_tm)

    class Gather:
        def __init__(self, own):
            self.x, self.hops = own, list(HOPS)
            self.arriving = hop(own, self.hops.pop(0))

        def step(self):
            self.x = join(line, self.x, self.arriving)
            self.arriving = hop(self.x, self.hops.pop(0))
            if not self.hops:
                self.low_core = core(self.x)

        def last(self):
            high = join(line, self.arriving)
            self.slots = self.x, high, self.low_core, core(high)

    class Message:
        def __init__(self, *packed):
            self.packed, self.terms, self.hops = packed, [], list(HOPS)
            if fast:
                for kept, sent in packed:
                    self.terms += [kept, core(sent)]

        def fold(self):
            kept, out = fold(line, *self.terms)
            self.terms = [kept, hop(out, self.hops.pop())]

        def last(self):
            own = settle(line, *self.terms)
            self.sums = [own] + [swap(own, "tm", r, n_tm) for r in (1, 2, 3)]

    v = {}
    tasks = {}

    def task(run):
        tasks[run.__name__] = run
        return run

    def cut_front(k):
        args = (affine_kernels, prediction_dictionary, affine_offsets)
        scratch = [
            pltpu.VMEM((2, HALF, 512), f32),
            pltpu.VMEM((HALF, width), f32),
            pltpu.SemaphoreType.DMA((2,)),
        ]
        out = [((1, FRONT, 512), bf16)]
        run = functools.partial(cut_front_body, k)
        return Gather(line.run(run, "cut_front", args, out, scratch, stay=(0, 1), limit=3)[0])

    def cut_back(k):
        args = (affine_kernels, expansion_projection)
        scratch = [
            pltpu.VMEM((2, HALF, 512), f32),
            pltpu.VMEM((2, HALF, 512), f32),
            pltpu.SemaphoreType.DMA((2,)),
        ]
        out = [((1, BACK, 512), bf16)]
        run = functools.partial(cut_back_body, k)
        return Gather(line.run(run, "cut_back", args, out, scratch, stay=(0, 1), limit=3)[0])

    @task
    def cut_a0():
        v["a0"] = cut_front(0)

    @task
    def cut_b0():
        v["b0"] = cut_back(0)

    @task
    def cut_a1():
        v["a1"] = cut_front(1)

    @task
    def cut_b1():
        v["b1"] = cut_back(1)

    @task
    def cut_c():
        args = (history_dictionary, *v["x"].pieces()[1:])
        out = [((1, BASIS, 512), bf16)]
        v["c"] = Gather(line.run(cut_basis_body, "cut_basis", args, out, limit=3)[0])

    for name in ("a0", "b0", "a1", "b1", "c"):
        tasks["step_" + name] = lambda name=name: v[name].step()
        tasks["last_" + name] = lambda name=name: v[name].last()

    @task
    def split_x():
        pieces = split_windows(line, history_series, n_tm, history_dictionary if fast else None)
        v["x"] = Exchange(line, pieces, n_tm)

    @task
    def split_g():
        v["g"] = Exchange(line, split_windows(line, remainder_adjoint, n_tm), n_tm)

    @task
    def select():
        args = (labels, prediction_adjoint.T)
        v["fg"] = line.run(select_body, "select", args, [((LANES, rows), bf16)], limit=4)[0]

    for name in ("x", "g", "rem", "der"):
        tasks["relay_" + name] = lambda name=name: v[name].relay()

    @task
    def merge_rem():
        pieces = v["rem"].pieces()
        v["remainder"] = merge_windows(line, history_series, pieces, -1)

    @task
    def merge_der():
        pieces = v["der"].pieces()
        v["derivative"] = merge_windows(line, remainder_adjoint, pieces, 1)

    @task
    def front_0():
        outs = front(line, v["a0"].slots, v["x"].pieces(), rows)
        v["w1a"], v["w2a"], v["bias"], v["basis_a"], *v["h12"] = outs

    @task
    def rear_0():
        args = (v["b0"].slots, v["h12"][2], v["bias"], v["basis_a"], ())
        outs = rear(line, *args, width, v["h12"])
        v["w3a"], v["w4a"], v["wba"], v["wfa"] = outs[:4]
        v["act"], v["fore"] = outs[4:10], outs[10]
        v["h1a"], v["d1a"], v["h2a"], v["d2a"] = outs[11:]

    @task
    def cast_0():
        outs = backcast(line, 0, v["c"].slots, v["act"][4], v["x"].pieces())
        v["wva"], v["x2"], v["cast"] = outs

    @task
    def front_1():
        outs = front(line, v["a1"].slots, [v["x2"]], rows, v["act"])
        v["w1b"], v["w2b"], v["bias"], v["basis_b"], v["h1"], v["d1"], v["h2"], v["d2"] = outs[:8]
        v["h3a"], v["d3a"], v["h4a"], v["d4a"], v["bta"], v["fta"] = outs[8:]

    @task
    def rear_1():
        args = (v["b1"].slots, v["h2"], v["bias"], v["basis_b"], (v["fore"], labels))
        outs = rear(line, *args, width)
        v["w3b"], v["w4b"], v["wbb"], v["wfb"] = outs[:4]
        v["h3"], v["d3"], v["h4"], v["d4"], v["bt"], v["ft"], v["fore"] = outs[4:]

    @task
    def cast_1():
        outs = backcast(line, 1, v["c"].slots, v["bt"], [v["cast"]])
        v["wvb"], v["rem"] = outs[0], Exchange(line, outs[1:], n_tm)

    @task
    def chain_rear_1():
        weights = (v["wvb"], v["basis_b"], v["wbb"], v["wfb"], v["w4b"])
        v["cr"] = chain_rear(line, v["g"].pieces(), v["fg"], weights, v["d4"], v["d3"], False)

    @task
    def terms_rear_1():
        args = ((*v["cr"][0:3], v["fg"]), (v["bt"], v["h4"], v["ft"]), ())
        v["t1"] = terms_rear(line, 1, *args, False)
        if fast:
            v["t1_core"] = core(v["t1"][1])

    @task
    def chain_front_1():
        weights = (v["w3b"], v["w2b"], v["w1b"])
        outs = chain_front(line, v["cr"][4], weights, v["d2"], v["d1"], None, False)
        v["cf"], v["gh2"] = outs[0:3], outs[3]

    @task
    def terms_front_1():
        more = (v["h3"], v["h2"], v["cr"][3], v["cr"][4])
        args = ((*v["cf"], v["cr"][5]), [v["x2"]], v["h1"], more)
        v["t2"] = terms_front(line, 1, *args, False)
        v["m1"] = Message(v["t1"], v["t2"])

    @task
    def chain_rear_0():
        weights = (v["wva"], v["basis_a"], v["wba"], v["wfa"], v["w4a"])
        gs = [*v["g"].pieces(), v["gh2"]]
        v["cr"] = chain_rear(line, gs, v["fg"], weights, v["d4a"], v["d3a"], True)

    @task
    def terms_rear_0():
        more = (v["h3a"], v["h2a"], v["cr"][3], v["cr"][4])
        args = ((*v["cr"][0:3], v["fg"]), (v["bta"], v["h4a"], v["fta"]), more)
        v["m3"] = Message(terms_rear(line, 0, *args, True))

    @task
    def chain_front_0():
        weights = (v["w3a"], v["w2a"], v["w1a"])
        outs = chain_front(line, v["cr"][4], weights, v["d2a"], v["d1a"], v["gh2"], True)
        v["cf"], v["der"] = outs[0:3], Exchange(line, outs[3:6], n_tm)

    @task
    def terms_front_0():
        args = ((*v["cf"], v["cr"][5]), v["x"].pieces(), v["h1a"], ())
        v["m4"] = Message(terms_front(line, 0, *args, True))

    for name in ("m1", "m3", "m4"):
        tasks["fold_" + name] = lambda name=name: v[name].fold()
        tasks["settle_" + name] = lambda name=name: v[name].last()

    if not fast:
        masters = (
            affine_kernels,
            affine_offsets,
            expansion_projection,
            history_dictionary,
            prediction_dictionary,
        )
        blocks, bases = shares_plain(*masters, n_tm)
        slots = {"a0": blocks[0][0], "b0": blocks[0][1], "a1": blocks[1][0], "b1": blocks[1][1], "c": bases}
        for name, value in slots.items():
            v[name] = Gather.__new__(Gather)
            v[name].slots = value
    for name in ORDER:
        if fast or name.split("_")[0] not in ("cut", "step", "last", "fold", "settle"):
            tasks[name]()
    if fast:
        sums = (*v["m3"].sums, *v["m4"].sums, *v["m1"].sums)
        grads = finish(line, sums, width)
    else:
        records = [(v["m3"].packed[0], v["m4"].packed[0]), v["m1"].packed]
        grads = gradients_plain(records, n_tm, width)
    return (v["remainder"], v["fore"].T, v["derivative"], *grads)


ORDER = """
split_x cut_a0 cut_b0 step_a0 cut_a1 step_a0 step_b0 cut_b1 relay_x last_a0 step_b0 step_a1 step_a1
cut_c front_0 step_c last_b0 split_g step_c last_a1 step_b1 rear_0 last_c step_b1 select cast_0
front_1 last_b1 relay_g rear_1 cast_1 chain_rear_1 terms_rear_1 chain_front_1 terms_front_1
chain_rear_0 fold_m1 terms_rear_0 chain_front_0 fold_m3 terms_front_0 fold_m1 fold_m4 relay_rem
fold_m1 fold_m3 fold_m4 fold_m3 settle_m1 relay_der merge_der fold_m4 settle_m3 merge_rem settle_m4
""".split()


def solution(mesh):
    return jax.shard_map(
        functools.partial(body, mesh.shape["dp"], mesh.shape["tm"]),
        mesh=mesh,
        in_specs=(
            P("dp", "tm"),
            P(("dp", "tm")),
            P(None, None, "dp", None),
            P(None, None, "dp"),
            P(None, None, "dp", None),
            P(None, "dp", "tm"),
            P(None, "dp", None),
            P("dp", "tm"),
            P(("dp", "tm"), None),
        ),
        out_specs=(
            P("dp", "tm"),
            P(("dp", "tm"), None),
            P("dp", "tm"),
            P(None, None, "dp", None),
            P(None, None, "dp"),
            P(None, None, "dp", None),
            P(None, "dp", "tm"),
            P(None, "dp", None),
        ),
        check_vma=False,
    )
```

```python
import functools

import jax
import jax.numpy as jnp
from jax import lax
from jax.experimental import pallas as pl
from jax.experimental.pallas import tpu as pltpu
from jax.sharding import PartitionSpec as P

HOR_Y = 6
HOR_Q = 8
HOR_M = 18
LAYERS = 4
LANES = 128
HALF = 32
GROUPS = 8
FRONT = 2 * HALF + 16
BACK = 4 * HALF
BASIS = 2 * HALF
HOPS = {
    "a0": (4, 2, 1),
    "b0": (4, 2, 1),
    "a1": (4, 2, 1),
    "b1": (4, 2, 1),
    "c": (4, 2, 1),
    "m1": (4, 1, 2),
    "m3": (4, 1, 2),
    "m4": (2, 1, 4),
}


def slot_shares(hops):
    return tuple(sum(bit for i, bit in enumerate(hops) if s >> i & 1) for s in range(GROUPS))


TILE = 512
CHUNK = 256

f32 = jnp.float32
bf16 = jnp.bfloat16
MIB = 1024 * 1024
FLOPS_PER_US = 250_000_000


def mm(a, b):
    return jnp.dot(a, b, preferred_element_type=f32)


def mm_nt(a, b):
    return lax.dot_general(a, b, (((1,), (1,)), ((), ())), preferred_element_type=f32)


def mm_tn(a, b):
    return lax.dot_general(a, b, (((0,), (0,)), ((), ())), preferred_element_type=f32)


def rows_at(start, size, align):
    return pl.ds(pl.multiple_of(start, align), size)


def in_group(labels, width):
    field = lax.broadcasted_iota(jnp.int32, (width, labels.shape[1]), 0)
    group = (
        (field >= HOR_Y).astype(jnp.int32)
        + (field >= HOR_Y + HOR_Q).astype(jnp.int32)
        + (field >= HOR_Y + HOR_Q + HOR_M).astype(jnp.int32)
    )
    return group == labels


def slot_rows(pos, q, s, hops):
    share = pos[0] ^ slot_shares(hops)[s]
    half = pos[1] ^ q
    row = share * (2 * HALF) + half * HALF
    block = share * 2 + half
    window_row = ((block // 4) ^ pos[2]) * LANES + (block % 4) * HALF
    return row, window_row


def slot_at(pos, share, hops):
    r = share ^ pos[0]
    place = {1: 0, 2: 1, 4: 2}
    return sum(((r >> place[bit]) & 1) << i for i, bit in enumerate(hops))


def size_of(shape):
    total = 1
    for extent in shape:
        total *= extent
    return total


class Inputs:
    def __init__(self, refs, copies):
        self.refs, self.copies = refs, copies

    def __getitem__(self, i):
        if isinstance(i, slice):
            return [self[j] for j in range(*i.indices(len(self.refs)))]
        if i in self.copies:
            self.copies.pop(i).wait()
        return self.refs[i]


class Line:
    def __init__(self, pos):
        self.pos, self.token, self.us = pos, None, None

    def run(self, body, name, args, outs, scratch=(), fetch=(), save=(), limit=12, after=(), us=0.5, stay=(), out_stays=False):
        token = [] if self.token is None else [self.token]
        extra = [*after, *token]
        fetch, save = list(fetch), list(save)
        n_in, n_out, n_extra = len(args), len(outs), len(extra)
        n_fetch, n_save = len(fetch), len(save)

        def kernel(pos_ref, *refs):
            refs = list(refs)
            given, refs = refs[:n_in], refs[n_in + n_extra :]
            results, refs = refs[:n_out], refs[n_out:]
            saved, refs = refs[:n_save], refs[n_save:]
            if out_stays:
                refs.pop(0)[...] = jnp.zeros((8, LANES), f32)
            landing, refs = refs[:n_fetch], refs[n_fetch:]
            sems = refs.pop() if n_fetch + n_save else None
            inputs, copies, leaving = list(given), {}, []
            for at, (i, buf) in enumerate(zip(fetch, landing)):
                copies[i] = pltpu.make_async_copy(given[i], buf, sems.at[at])
                copies[i].start()
                inputs[i] = buf
            for at, (i, dst) in enumerate(zip(save, saved)):
                leaving.append(pltpu.make_async_copy(given[i], dst, sems.at[n_fetch + at]))
                leaving[-1].start()
            body(pos_ref, Inputs(inputs, copies), results, refs)
            for copy in (*copies.values(), *leaving):
                copy.wait()

        vmem, hbm = pl.BlockSpec(memory_space=pltpu.VMEM), pl.BlockSpec(memory_space=pltpu.HBM)
        anywhere = pl.BlockSpec(memory_space=pl.ANY)
        place = pltpu.HBM if out_stays else jax.ShapeDtypeStruct
        shapes = [place(shape, dtype) for shape, dtype in outs]
        placed = [
            pltpu.with_memory_space_constraint(a, pltpu.HBM) if i in fetch or i in stay else a
            for i, a in enumerate(args)
        ]
        shapes += [pltpu.HBM(args[i].shape, args[i].dtype) for i in save]
        mark = [jax.ShapeDtypeStruct((8, LANES), f32)] if out_stays else []
        sems = [pltpu.SemaphoreType.DMA((n_fetch + n_save,))] if n_fetch + n_save else []
        results = list(pl.pallas_call(
            kernel,
            name=name,
            out_shape=shapes + mark,
            in_specs=[pl.BlockSpec(memory_space=pltpu.SMEM)]
            + [hbm if i in fetch or i in stay else vmem for i in range(n_in)]
            + [anywhere] * n_extra,
            out_specs=[hbm if out_stays else vmem] * n_out + [hbm] * n_save + [vmem] * len(mark),
            scratch_shapes=[pltpu.VMEM(args[i].shape, args[i].dtype) for i in fetch]
            + list(scratch)
            + sems,
            compiler_params=pltpu.CompilerParams(vmem_limit_bytes=limit * MIB),
            cost_estimate=pl.CostEstimate(
                flops=int((us if self.us is None else self.us) * FLOPS_PER_US),
                bytes_accessed=1,
                transcendentals=0,
            ),
        )(self.pos, *placed, *extra))
        if out_stays:
            self.token = results.pop()
        else:
            self.token = min(results, key=lambda a: a.size * a.dtype.itemsize)
        return results


def swap(x, axis, bit, size):
    return lax.ppermute(x, axis, [(i, i ^ bit) for i in range(size)])


class Exchange:
    def __init__(self, line, pieces, n_tm):
        self.line, self.n_tm = line, n_tm
        self.own, near, far = pieces
        self.far = swap(far, "tm", 2, n_tm)
        self.near = swap(near, "tm", 1, n_tm)

    def relay(self):
        shape = self.far.shape[1:]
        out = [(shape, bf16)]
        across = self.line.run(relay_body, "relay", (self.far,), out, limit=2)[0]
        self.across = swap(across, "tm", 1, self.n_tm)

    def pieces(self):
        return [self.own, self.near, self.far, self.across]


def relay_body(pos, ins, outs, scratch):
    outs[0][...] = ins[0][1]


def flat(refs):
    return [ref if len(ref.shape) == 2 else ref.at[0] for ref in refs]


def split_body(with_basis, pos, ins, outs, scratch):
    landing, sems = scratch
    rows = landing.shape[1]
    copies = []
    for r in range(4):
        copies.append(pltpu.make_async_copy(ins[0].at[pos[2] ^ r], landing.at[r], sems.at[r]))
    for r in (2, 3, 1, 0):
        copies[r].start()
    if with_basis:
        for k in range(2):
            at = slice(rows + 2 * HALF * k, rows + 2 * HALF * (k + 1))
            value = ins[1][k].astype(bf16)
            for out in (outs[1], outs[2].at[0], outs[2].at[1]):
                out[at, :] = value
    for r in (2, 3, 1, 0):
        copies[r].wait()
        out = outs[2].at[r - 2] if r >= 2 else outs[r]
        out[0:rows, :] = landing[r].astype(bf16)


def piece_shapes(rows, more=0):
    sent = rows + more
    return [((rows, LANES), bf16), ((sent, LANES), bf16), ((2, sent, LANES), bf16)]


def split_windows(line, array, parts, basis=None):
    shape = (parts, array.shape[0] // parts, LANES)
    args = (array.reshape(shape),) if basis is None else (array.reshape(shape), basis)
    return line.run(
        functools.partial(split_body, basis is not None),
        "split_windows",
        args,
        piece_shapes(shape[1], 0 if basis is None else 2 * basis.shape[1]),
        [pltpu.VMEM(shape, f32), pltpu.SemaphoreType.DMA((parts,))],
        stay=(0,),
        limit=8,
        us=2.0,
    )


def merge_body(sign, pos, ins, outs, scratch):
    base, pieces = ins[0], flat(ins[1:5])
    leaving, sems = scratch
    parts = len(pieces)
    arrive, leave = [], []
    for r in range(parts):
        at = pos[2] ^ r
        leave.append(pltpu.make_async_copy(leaving.at[r], outs[0].at[at], sems.at[parts + r]))
    for r, piece in enumerate(pieces):
        value = piece[...].astype(f32)
        own = base[pos[2] ^ r]
        leaving[r] = own - value if sign < 0 else own + value
        leave[r].start()
    for copy in leave:
        copy.wait()


def merge_windows(line, base, pieces, sign):
    parts = len(pieces)
    shape = (parts, base.shape[0] // parts, LANES)
    out = line.run(
        functools.partial(merge_body, sign),
        "merge_windows",
        (base.reshape(shape), *pieces),
        [(shape, f32)],
        [pltpu.VMEM(shape, f32), pltpu.SemaphoreType.DMA((2 * parts,))],
        stay=(),
        out_stays=True,
        limit=12,
        us=3.5,
    )[0]
    return out.reshape(base.shape)


def activate(p):
    t = jnp.tanh(p)
    u = 1.0 + t
    h = p * u
    return h.astype(bf16), u + h * (1.0 - t)


def columns(refs, at):
    if len(refs) == 1:
        return refs[0][at, :]
    return jnp.concatenate([ref[at, :] for ref in refs], axis=1)


def put_pieces(refs, at, value):
    for r in range(4):
        ref = refs[2].at[r - 2] if r >= 2 else refs[r]
        ref[at, :] = value[:, r * LANES : (r + 1) * LANES]


def chunks(rows):
    return [slice(at, at + CHUNK) for at in range(0, rows, CHUNK)]


def front_body(n_x, hops, pos, ins, bufs, scratch):
    w1, w2, bias, basis, h1, d1, h2, d2 = bufs
    total = jnp.zeros((16, 2 * LANES), f32)
    for q in range(2):
        for s in range(GROUPS):
            ref, i = ins[2 * q + s // 4], s % 4
            row, window_row = slot_rows(pos, q, s, hops)
            w1[rows_at(window_row, HALF, HALF), :] = ref[i, 0:HALF, :] * 0.5
            w2[rows_at(row, HALF, HALF), :] = ref[i, HALF : 2 * HALF, :] * 0.5
            low = ref[i, 2 * HALF : FRONT, 0:LANES]
            high = ref[i, 2 * HALF : FRONT, LANES : 2 * LANES]
            basis[rows_at(row, 16, 16), :] = low
            basis[rows_at(row + 16, 16, 16), :] = high
            if q == 0:
                total += ref[i, 2 * HALF : FRONT, 2 * LANES :].astype(f32)
    bias[:, 0 : 2 * LANES] = total[0:8] * 0.5
    bias[:, 2 * LANES :] = total[8:16] * 0.5
    xs = flat(ins[4 : 4 + n_x])
    for at in chunks(h1.shape[0]):
        h, d = activate(mm(columns(xs, at), w1[...]) + bias[0:1, :])
        h1[at, :] = h
        d1[at, :] = d.astype(bf16)
    for at in chunks(h1.shape[0]):
        h, d = activate(mm(h1[at, :], w2[...]) + bias[1:2, :])
        h2[at, :] = h
        d2[at, :] = d.astype(bf16)


def front(line, k, slots, xs, rows, leaving=()):
    square = ((512, 512), bf16)
    hidden = ((rows, 512), bf16)
    args = (*slots, *xs, *leaving)
    return line.run(
        functools.partial(front_body, len(xs), HOPS["a" + str(k)]),
        "front",
        args,
        [square, square, ((8, 512), f32), ((512, LANES), bf16), hidden, hidden, hidden, hidden],
        save=range(len(args) - len(leaving), len(args)),
        limit=6,
        us=4.0,
    )


def rear_body(last, hops, pos, ins, bufs, scratch):
    w3, w4, wb, wf, h3, d3, h4, d4, bt, ft, fore_out = bufs
    for q in range(2):
        for s in range(GROUPS):
            ref, i = ins[2 * q + s // 4], s % 4
            row, _ = slot_rows(pos, q, s, hops)
            for m, w in enumerate((w3, w4, wb, wf)):
                part = ref[i, m * HALF : (m + 1) * HALF, :]
                w[rows_at(row, HALF, HALF), :] = part * 0.5 if m < 2 else part
    bias, h2, basis = ins[4], ins[5], ins[6]
    steps = chunks(h3.shape[0])
    for at in steps:
        h, d = activate(mm(h2[at, :], w3[...]) + bias[2:3, :])
        h3[at, :] = h
        d3[at, :] = d.astype(bf16)
    for at in steps:
        h, d = activate(mm(h3[at, :], w4[...]) + bias[3:4, :])
        h4[at, :] = h
        d4[at, :] = (0.5 * d).astype(bf16)
    for at in steps:
        bt[at, :] = mm(h4[at, :], wb[...]).astype(bf16)
    for at in steps:
        ft[at, :] = mm(h4[at, :], wf[...]).astype(bf16)
    width = fore_out.shape[0]
    for at in steps:
        fore = mm(ft[at, :], basis[...]).T[0:width, :]
        if last:
            fore = ins[7][:, at] + fore
            fore = jnp.where(in_group(ins[8][0:1, at], width), fore, 0.0)
        fore_out[:, at] = fore


def rear(line, slots, h2, bias, basis, extra, width, leaving=()):
    rows = h2.shape[0]
    square = ((512, 512), bf16)
    hidden = ((rows, 512), bf16)
    args = (*slots, bias, h2, basis, *extra, *leaving)
    return line.run(
        functools.partial(rear_body, bool(extra), HOPS["b1" if extra else "b0"]),
        "rear",
        args,
        [square] * 4 + [hidden] * 6 + [((width, rows), f32)],
        save=range(len(args) - len(leaving), len(args)),
        limit=6,
        us=6.5,
    )


def cast_body(k, pos, ins, bufs, scratch):
    wv = bufs[0]
    for q in range(2):
        for s in range(GROUPS):
            ref, i = ins[2 * q + s // 4], s % 4
            row, _ = slot_rows(pos, q, s, HOPS["c"])
            for r in range(4):
                part = ref[i, k * HALF : (k + 1) * HALF, r * LANES : (r + 1) * LANES]
                at = r ^ q
                wv[rows_at(row, HALF, HALF), at * LANES : (at + 1) * LANES] = part
    bt = ins[4]
    for at in chunks(bt.shape[0]):
        cast = mm(bt[at, :], wv[...])
        if k == 0:
            bufs[1][at, :] = (columns(flat(ins[5:9]), at).astype(f32) - cast).astype(bf16)
            bufs[2][at, :] = cast
        else:
            put_pieces(bufs[1:4], at, (cast + ins[5][at, :]).astype(bf16))


def backcast(line, k, slots, bt, extra):
    rows = bt.shape[0]
    hidden = (rows, 512)
    outs = [(hidden, bf16), (hidden, f32)] if k == 0 else piece_shapes(rows)
    return line.run(
        functools.partial(cast_body, k),
        "backcast",
        (*slots, bt, *extra),
        [((512, 512), bf16)] + outs,
        limit=6,
        us=1.5,
    )


def row_sum(value):
    return jnp.sum(value.astype(f32), axis=0, keepdims=True)


def pack_pair(packed, rows, lanes, slot, first, second, pos):
    keep, send = packed
    lower = pos[1] == 0
    first, second = first.astype(bf16), second.astype(bf16)
    keep[slot, rows, lanes] = jnp.where(lower, first, second)
    send[slot, rows, lanes] = jnp.where(lower, second, first)


def pack_rows(packed, at, value, pos, hops):
    for share in range(GROUPS):
        row = share * 2 * HALF
        pack_pair(
            packed,
            slice(at, at + HALF),
            slice(None),
            slot_at(pos, share, hops),
            value[row : row + HALF, :],
            value[row + HALF : row + 2 * HALF, :],
            pos,
        )


def chain_rear_body(n_g, pos, ins, outs, scratch):
    g, g_back, g_fore, g4, g3, bias = outs
    wv, basis, wb, wf, w4 = ins[n_g + 1 : n_g + 6]
    gs, fg = flat(ins[0:4]) + ins[4:n_g], ins[n_g]
    steps = chunks(g.shape[0])
    for at in steps:
        value = columns(gs[:4], at)
        if n_g == 5:
            value = (value.astype(f32) + gs[4][at, :].astype(f32)).astype(bf16)
        g[at, :] = -value
        g_back[at, :] = mm_nt(g[at, :], wv[...]).astype(bf16)
    for at in steps:
        g_fore[at, :] = mm_nt(fg[:, at].T, basis[...]).astype(bf16)
    d4 = ins[n_g + 6]
    b3 = b4 = jnp.zeros((1, 512), f32)
    for at in steps:
        gh = mm_nt(g_back[at, :], wb[...]) + mm_nt(g_fore[at, :], wf[...])
        value = (gh * d4[at, :].astype(f32)).astype(bf16)
        g4[at, :] = value
        b4 += row_sum(value)
    d3 = ins[n_g + 7]
    for at in steps:
        gh = mm_nt(g4[at, :], w4[...])
        value = (gh * d3[at, :].astype(f32)).astype(bf16)
        g3[at, :] = value
        b3 += row_sum(value)
    bias[...] = jnp.concatenate([b3, b4, jnp.zeros((6, 512), f32)], axis=0)


def chain_rear(line, gs, fg, weights, d4, d3, fetch):
    rows = fg.shape[1]
    n = len(gs) + 1 + len(weights)
    return line.run(
        functools.partial(chain_rear_body, len(gs)),
        "chain_rear",
        (*gs, fg, *weights, d4, d3),
        [((rows, 512), bf16)] * 5 + [((8, 512), f32)],
        fetch=(n, n + 1) if fetch else (),
        limit=10 if fetch else 6,
        us=7.0,
    )


def chain_front_body(last, pos, ins, outs, scratch):
    g2, g1, bias = outs[:3]
    g3, w3, w2, w1 = ins[0:4]
    steps = chunks(g1.shape[0])
    b1 = b2 = jnp.zeros((1, 512), f32)
    d2 = ins[4]
    for at in steps:
        gh = mm_nt(g3[at, :], w3[...])
        value = (gh * d2[at, :].astype(f32)).astype(bf16)
        g2[at, :] = value
        b2 += row_sum(value)
    d1 = ins[5]
    for at in steps:
        gh = mm_nt(g2[at, :], w2[...])
        value = (gh * d1[at, :].astype(f32)).astype(bf16)
        g1[at, :] = value
        b1 += row_sum(value)
    for at in steps:
        gh = (2.0 * mm_nt(g1[at, :], w1[...])).astype(bf16)
        if last:
            gh = (gh.astype(f32) + ins[6][at, :].astype(f32)).astype(bf16)
            put_pieces(outs[3:6], at, gh)
        else:
            outs[3][at, :] = gh
    bias[...] = jnp.concatenate([b1, b2, jnp.zeros((6, 512), f32)], axis=0)


def chain_front(line, g3, weights, d2, d1, gh2, fetch):
    rows = g3.shape[0]
    last = gh2 is not None
    outs = piece_shapes(rows) if last else [((rows, 512), bf16)]
    return line.run(
        functools.partial(chain_front_body, last),
        "chain_front",
        (g3, *weights, d2, d1, *([gh2] if last else [])),
        [((rows, 512), bf16)] * 2 + [((8, 512), f32)] + outs,
        fetch=(4, 5) if fetch else (),
        limit=10 if fetch else 6,
        us=4.5,
    )


def message_rows(k):
    first = {"B": 0, "F": HALF, "V": 2 * HALF, "U": 3 * HALF}
    second = {"L2": 0, "L1": HALF, "bias": 2 * HALF}
    sizes = [3 * HALF + 16, 2 * HALF + 16]
    at = 1 if k else 0
    for name in ("L4", "L3"):
        (first, second)[at][name] = sizes[at]
        sizes[at] += HALF
    return first, second, sizes


def whole_rows(ref):
    return slice(0, ref.shape[0])


def terms_rear_body(k, pos, ins, outs, scratch):
    packed, second = outs[0:2], outs[2:4]
    at, _, _ = message_rows(k)
    hops = HOPS["m1" if k else "m3"]
    g, g_back, g_fore, fg = ins[0:4]
    bt = ins[4]
    value = mm_tn(bt[...], g[...])
    for share in range(GROUPS):
        slot = slot_at(pos, share, hops)
        for r in range(4):
            for j in range(2):
                row, lane = (2 * share + j) * HALF, (2 * j + r // 2) * LANES
                part = value[row : row + HALF, r * LANES : (r + 1) * LANES].astype(bf16)
                packed[r % 2][slot, at["V"] : at["V"] + HALF, lane : lane + LANES] = part
    h4 = ins[5]
    pack_rows(packed, at["B"], mm_tn(h4[...], g_back[...]), pos, hops)
    pack_rows(packed, at["F"], mm_tn(h4[...], g_fore[...]), pos, hops)
    ft = ins[6]
    value = mm(fg[...], ft[...]).T
    rows = slice(at["U"], at["U"] + 16)
    for share in range(GROUPS):
        row, slot = share * 2 * HALF, slot_at(pos, share, hops)
        for j in range(2):
            lanes = slice(j * LANES, (j + 1) * LANES)
            low = value[row + 16 * j : row + 16 * (j + 1), :]
            high = value[row + HALF + 16 * j : row + HALF + 16 * (j + 1), :]
            pack_pair(packed, rows, lanes, slot, low, high, pos)
        for out in packed:
            out[slot, rows, 2 * LANES :] = jnp.zeros((16, 2 * LANES), bf16)
    if "L4" in at:
        h3, h2, g4, g3 = ins[7], ins[8], ins[9], ins[10]
        pack_rows(second, 0, mm_tn(h3[...], g4[...]), pos, hops)
        pack_rows(second, HALF, mm_tn(h2[...], g3[...]), pos, hops)


def terms_rear(line, k, grads, hidden, more, fetch):
    args = (*grads, *hidden, *more)
    heights = (3 * HALF + 16, 2 * HALF)
    outs = [((GROUPS, height, 512), bf16) for height in heights[: 2 if more else 1] for _ in range(2)]
    return line.run(
        functools.partial(terms_rear_body, k),
        "terms_rear",
        args,
        outs,
        fetch=[i for i in range(4, min(9, len(args)))] if fetch else (),
        limit=16 if fetch else 6,
        us=4.5 if k else 8.0,
    )


def terms_front_body(k, n_x, pos, ins, packed, scratch):
    _, at, _ = message_rows(k)
    hops = HOPS["m1" if k else "m4"]
    g2, g1, low_bias, high_bias = ins[0:4]
    bias = jnp.concatenate([low_bias[0:2, :], high_bias[0:2, :], jnp.zeros((4, 512), f32)], axis=0)
    bias = jnp.concatenate([bias[:, 0 : 2 * LANES], bias[:, 2 * LANES :]], axis=0).astype(bf16)
    rows = slice(at["bias"], at["bias"] + 16)
    for s in range(GROUPS):
        for out in packed:
            out[s, rows, 0 : 2 * LANES] = jnp.zeros((16, 2 * LANES), bf16)
            out[s, rows, 2 * LANES :] = bias
    xs = flat(ins[4 : 4 + n_x])
    value = mm_tn(columns(xs, whole_rows(g1)), g1[...])
    for r in range(4):
        for i in range(2):
            row = r * LANES + i * 2 * HALF
            pack_pair(
                packed,
                slice(at["L1"], at["L1"] + HALF),
                slice(None),
                slot_at(pos, (pos[2] ^ r) * 2 + i, hops),
                value[row : row + HALF, :],
                value[row + HALF : row + 2 * HALF, :],
                pos,
            )
    h1 = ins[4 + n_x]
    pack_rows(packed, at["L2"], mm_tn(h1[...], g2[...]), pos, hops)
    if "L4" in at:
        h3, h2, g4, g3 = ins[5 + n_x : 9 + n_x]
        pack_rows(packed, at["L4"], mm_tn(h3[...], g4[...]), pos, hops)
        pack_rows(packed, at["L3"], mm_tn(h2[...], g3[...]), pos, hops)


def terms_front(line, k, grads, xs, h1, more, fetch):
    args = (*grads, *xs, h1, *more)
    out = ((GROUPS, message_rows(k)[2][1], 512), bf16)
    return line.run(
        functools.partial(terms_front_body, k, len(xs)),
        "terms_front",
        args,
        [out, out],
        fetch=(4 + len(xs),) if fetch else (),
        limit=8,
        us=5.5 if k else 3.0,
    )


def pack_misc(basis, offsets):
    lead = basis.shape[:-2]
    offsets = jnp.concatenate([offsets, jnp.zeros_like(offsets)], axis=-2)
    return jnp.concatenate(
        [
            basis[..., 0:16, :],
            basis[..., 16:32, :],
            jnp.concatenate([offsets[..., 0 : 2 * LANES], offsets[..., 2 * LANES :]], axis=-2),
        ],
        axis=-1,
    ).reshape(*lead, 16, 512)


def select_body(pos, ins, outs, scratch):
    labels, adjoint = ins[0], ins[1]
    width = adjoint.shape[0]
    for at in chunks(adjoint.shape[1]):
        value = jnp.where(in_group(labels[0:1, at], width), adjoint[:, at], 0.0)
        outs[0][0:width, at] = value.astype(bf16)
    outs[0][width:, :] = jnp.zeros((LANES - width, adjoint.shape[1]), bf16)


def cut_front_body(k, pos, ins, outs, scratch):
    kernels, basis, offsets = ins[0:3]
    rows_in, basis_in, sems = scratch
    out = outs[0]
    half = rows_at(pos[1] * HALF, HALF, HALF)
    copies = [
        pltpu.make_async_copy(kernels.at[k, 0:2, half, :], rows_in, sems.at[0]),
        pltpu.make_async_copy(basis.at[k, half, :], basis_in, sems.at[1]),
    ]
    for copy in copies:
        copy.start()
    rows, width = slice(2 * HALF, FRONT), basis.shape[2]
    out[0, rows, :] = jnp.zeros((16, 512), bf16)
    own = jnp.concatenate([offsets[k], jnp.zeros_like(offsets[k])], axis=0)
    own = jnp.concatenate([jnp.where(pos[0] % 4 == i, own, 0.0) for i in range(4)], axis=1)
    own = jnp.concatenate([jnp.where(pos[0] // 4 == i, own, 0.0) for i in range(2)], axis=0)
    out[0, rows, 2 * LANES :] = own.astype(bf16)
    copies[1].wait()
    for j in range(2):
        part = basis_in[16 * j : 16 * (j + 1), :]
        out[0, rows, j * LANES : j * LANES + width] = part.astype(bf16)
    copies[0].wait()
    for layer in range(2):
        out[0, layer * HALF : (layer + 1) * HALF, :] = rows_in[layer].astype(bf16)


def cut_back_body(k, pos, ins, outs, scratch):
    kernels, projection = ins[0:2]
    rows_in, pair_in, sems = scratch
    half = rows_at(pos[1] * HALF, HALF, HALF)
    copies = [
        pltpu.make_async_copy(kernels.at[k, 2:4, half, :], rows_in, sems.at[0]),
        pltpu.make_async_copy(projection.at[k, :, half, :], pair_in, sems.at[1]),
    ]
    for copy in copies:
        copy.start()
    for m, landed in enumerate((rows_in, pair_in)):
        copies[m].wait()
        for i in range(2):
            at = (2 * m + i) * HALF
            outs[0][0, at : at + HALF, :] = landed[i].astype(bf16)


def cut_basis_body(pos, ins, outs, scratch):
    own, near, far, across = ins[0:4]
    first = near.shape[0] - 4 * HALF
    for k in range(2):
        at = first + 2 * HALF * k + pos[1] * HALF
        parts = [own[k, rows_at(pos[1] * HALF, HALF, HALF), :].astype(bf16)]
        parts += [ref[rows_at(at, HALF, HALF), :] for ref in (near, far.at[0], across)]
        outs[0][0, k * HALF : (k + 1) * HALF, :] = jnp.concatenate(parts, axis=1)


def join_body(pos, ins, outs, scratch):
    at = 0
    for ref in ins[0 : len(ins.refs)]:
        outs[0][at : at + ref.shape[0]] = ref[...]
        at += ref.shape[0]


def join(line, *parts):
    count = sum(part.shape[0] for part in parts)
    return line.run(join_body, "join", parts, [((count, *parts[0].shape[1:]), bf16)], limit=2)[0]


def fold_body(n, pos, ins, outs, scratch):
    at = 0
    for kept, arrived in zip(ins[0 : len(ins.refs) : 2], ins[1 : len(ins.refs) : 2]):
        rows = slice(at, at + kept.shape[1])
        at += kept.shape[1]
        for s in range(2 * n):
            total = kept[s].astype(f32) + arrived[s].astype(f32)
            if s < n:
                outs[0][s, rows, :] = total
            else:
                outs[1][s - n, rows, :] = total.astype(bf16)


def fold(line, *terms):
    n = terms[0].shape[0] // 2
    shape = (n, sum(term.shape[1] for term in terms[::2]), terms[0].shape[2])
    return line.run(
        functools.partial(fold_body, n),
        "fold",
        terms,
        [(shape, f32), (shape, bf16)],
        limit=4,
    )


def settle_body(pos, ins, outs, scratch):
    outs[0][...] = (ins[0][0] + ins[1][0].astype(f32)).astype(bf16)


def settle(line, kept, arrived):
    return line.run(settle_body, "settle", (kept, arrived), [(kept.shape[1:], bf16)], limit=4)[0]


def finish_body(width, pos, ins, outs, scratch):
    kernels, bias_out, projection, history_basis, forecast_basis = outs
    lower = pos[1] == 0
    for k in range(2):
        first, second, sizes = message_rows(k)
        places = {}
        for m, rows in enumerate((first, second)):
            one = 0 if k else 4 * m
            own, core, far, across = ins[8 * k + one : 8 * k + one + 4]
            for name, at in rows.items():
                places[name] = (own, core, far, across, at + (sizes[0] if k and m else 0))

        def both(name, height):
            own, core, far, across, at = places[name]
            rows = slice(at, at + height)
            mine = own[rows, :].astype(f32) + far[rows, :].astype(f32)
            other = core[rows, :].astype(f32) + across[rows, :].astype(f32)
            return jnp.where(lower, mine, other), jnp.where(lower, other, mine), mine

        targets = [("B", projection, 0), ("F", projection, 1)]
        targets += [("L" + str(layer + 1), kernels, layer) for layer in range(LAYERS)]
        for name, out, index in targets:
            a, b, _ = both(name, HALF)
            out[k, index, 0:HALF, :] = a
            out[k, index, HALF : 2 * HALF, :] = b
        own, _, far, _, at = places["V"]
        for j in range(2):
            lanes = slice(2 * j * LANES, (2 * j + 1) * LANES)
            theirs = slice((2 * j + 1) * LANES, (2 * j + 2) * LANES)
            rows = slice(at, at + HALF)
            total = own[rows, lanes].astype(f32) + far[rows, theirs].astype(f32)
            history_basis[k, j * HALF : (j + 1) * HALF, :] = total
        a, b, _ = both("U", 16)
        for j, value in enumerate((a, b)):
            for i in range(2):
                row = j * HALF + i * 16
                part = value[:, i * LANES : i * LANES + width]
                forecast_basis[k, row : row + 16, :] = part
        _, _, mine = both("bias", 16)
        total = jnp.zeros(bias_out.shape[1:], f32)
        for share in range(GROUPS):
            row, lane = 8 * (share // 4), 2 * LANES + (share % 4) * 2 * HALF
            part = mine[row : row + LAYERS, lane : lane + 2 * HALF]
            total = total + jnp.where(pos[0] == share, part, 0.0)
        bias_out[k] = total


def finish(line, sums, width):
    share = 2 * HALF
    return line.run(
        functools.partial(finish_body, width),
        "finish",
        sums,
        [
            ((2, LAYERS, share, 512), f32),
            ((2, LAYERS, share), f32),
            ((2, 2, share, 512), f32),
            ((2, share, LANES), f32),
            ((2, share, width), f32),
        ],
        limit=8,
    )


def slots_of(x, hops):
    x = x.reshape(GROUPS, 2, HALF, x.shape[-1]).swapaxes(0, 1)
    return x[:, jnp.array(slot_shares(hops))]


def in_order(x, hops):
    shares = slot_shares(hops)
    return x[:, jnp.array([shares.index(share) for share in range(GROUPS)])]


def flat_rows(x):
    return x.swapaxes(0, 1).reshape(2 * GROUPS * HALF, x.shape[-1])


def four(x):
    return x[0, 0:4], x[0, 4:8], x[1, 0:4], x[1, 4:8]


def shares_plain(kernels, offsets, projection, history_basis, forecast_basis, n_tm):
    tm = lax.axis_index("tm")

    def gather(x, axis, over="dp"):
        return lax.all_gather(x.astype(bf16), over, axis=axis, tiled=True)

    order = [jnp.bitwise_xor(tm, r) for r in range(n_tm)]
    out, bases = [], []
    for k in range(kernels.shape[0]):
        w = gather(kernels[k], 1)
        b = gather(offsets[k], 1)
        p = gather(projection[k], 1)
        u = gather(forecast_basis[k], 0)
        u = jnp.pad(u, ((0, 0), (0, LANES - u.shape[-1])))
        v = gather(gather(history_basis[k], 0), 1, "tm")
        v = jnp.concatenate(
            [lax.dynamic_slice_in_dim(v, at * LANES, LANES, 1) for at in order], axis=1
        )
        v = slots_of(v, HOPS["c"])
        other = [v[1, ..., (r ^ 1) * LANES : ((r ^ 1) + 1) * LANES] for r in range(4)]
        v = jnp.stack([v[0], jnp.concatenate(other, axis=-1)])
        offs = jnp.zeros((2, GROUPS, LAYERS, 512), bf16).at[0, 0].set(b)
        front_hops, back_hops = HOPS["a" + str(k)], HOPS["b" + str(k)]
        misc = pack_misc(slots_of(u, front_hops), offs)
        first = [slots_of(x, front_hops) for x in (w[0], w[1])] + [misc]
        first = jnp.concatenate(first, axis=2)
        second = jnp.concatenate([slots_of(x, back_hops) for x in (w[2], w[3], p[0], p[1])], axis=2)
        out.append((four(first), four(second)))
        bases.append(v)
    return out, four(jnp.concatenate(bases, axis=2))


def gradients_plain(records, n_tm, width):
    def reduce(x, axis):
        return lax.psum_scatter(
            lax.psum(x.astype(bf16), "tm").astype(f32), "dp", scatter_dimension=axis, tiled=True
        )

    results = [[], [], [], [], []]
    for k, messages in enumerate(records):
        pieces = {}
        for m, message in enumerate(messages):
            message = jnp.stack(message)
            hops = HOPS["m1" if k else ("m3", "m4")[m]]
            for name, at in message_rows(k)[m].items():
                height = 16 if name in ("U", "bias") else HALF
                pieces[name] = in_order(message[:, :, at : at + height, :], hops)
        square = {name: flat_rows(pieces[name]) for name in ("L1", "L2", "L3", "L4", "B", "F")}
        results[0].append(reduce(jnp.stack([square["L" + str(i)] for i in range(1, 5)]), 1))
        bias = pieces["bias"][0, 0]
        bias = jnp.concatenate([bias[0:4, 2 * LANES :], bias[8:12, 2 * LANES :]], axis=1)
        results[1].append(reduce(bias, 1))
        results[2].append(reduce(jnp.stack([square["B"], square["F"]]), 1))
        v = pieces["V"]
        v = jnp.concatenate([v[..., 0 : 2 * LANES], v[..., 2 * LANES :]], axis=2)
        v = v.reshape(2, 2 * GROUPS * HALF, 2, LANES)
        blocks = [v[r % 2, :, r // 2] for r in range(4)]
        total = blocks[0].astype(f32)
        for r in range(1, n_tm):
            total = total + swap(blocks[r], "tm", r, n_tm).astype(f32)
        results[3].append(lax.psum_scatter(total, "dp", scatter_dimension=0, tiled=True))
        u = pieces["U"]
        u = jnp.concatenate([u[..., 0:LANES], u[..., LANES : 2 * LANES]], axis=2)
        results[4].append(reduce(flat_rows(u), 0)[:, 0:width])
    return [jnp.stack(x) for x in results]


def body(
    n_dp,
    n_tm,
    history_series,
    frequency_labels,
    affine_kernels,
    affine_offsets,
    expansion_projection,
    history_dictionary,
    prediction_dictionary,
    remainder_adjoint,
    prediction_adjoint,
):
    dp = lax.axis_index("dp")
    tm = lax.axis_index("tm")
    fast = n_dp == GROUPS
    zero = jnp.zeros((), jnp.int32)
    pos = jnp.stack([dp if fast else zero, tm % 2 if fast else zero, tm]).astype(jnp.int32)
    line = Line(pos)
    width = prediction_adjoint.shape[1]
    rows = frequency_labels.shape[0]
    labels = frequency_labels.reshape(1, rows)

    def select():
        args = (labels, prediction_adjoint.T)
        return line.run(select_body, "select", args, [((LANES, rows), bf16)], limit=4)[0]

    def hop(x, bit):
        return swap(x, "dp", bit, n_dp)

    def core(x):
        return swap(x, "tm", 1, n_tm)

    class Gather:
        def __init__(self, own, name):
            self.x, self.hops = own, list(HOPS[name])
            self.arriving = hop(own, self.hops.pop(0))

        def step(self):
            self.x = join(line, self.x, self.arriving)
            self.arriving = hop(self.x, self.hops.pop(0))
            if not self.hops:
                self.low_core = core(self.x)

        def last(self):
            high = join(line, self.arriving)
            self.slots = self.x, high, self.low_core, core(high)

    class Message:
        def __init__(self, name, *packed):
            self.packed, self.terms, self.hops = packed, [], list(HOPS[name])
            if fast:
                for kept, sent in packed:
                    self.terms += [kept, core(sent)]

        def fold(self):
            kept, out = fold(line, *self.terms)
            self.terms = [kept, hop(out, self.hops.pop())]

        def last(self):
            own = settle(line, *self.terms)
            self.sums = [own] + [swap(own, "tm", r, n_tm) for r in (1, 2, 3)]

    v = {}
    tasks = {}

    def task(run):
        tasks[run.__name__] = run
        return run

    def cut_front(k):
        args = (affine_kernels, prediction_dictionary, affine_offsets)
        scratch = [
            pltpu.VMEM((2, HALF, 512), f32),
            pltpu.VMEM((HALF, width), f32),
            pltpu.SemaphoreType.DMA((2,)),
        ]
        out = [((1, FRONT, 512), bf16)]
        run = functools.partial(cut_front_body, k)
        return Gather(line.run(run, "cut_front", args, out, scratch, stay=(0, 1), limit=3)[0], "a" + str(k))

    def cut_back(k):
        args = (affine_kernels, expansion_projection)
        scratch = [
            pltpu.VMEM((2, HALF, 512), f32),
            pltpu.VMEM((2, HALF, 512), f32),
            pltpu.SemaphoreType.DMA((2,)),
        ]
        out = [((1, BACK, 512), bf16)]
        run = functools.partial(cut_back_body, k)
        return Gather(line.run(run, "cut_back", args, out, scratch, stay=(0, 1), limit=3)[0], "b" + str(k))

    @task
    def cut_a0():
        v["a0"] = cut_front(0)

    @task
    def cut_b0():
        v["b0"] = cut_back(0)

    @task
    def cut_a1():
        v["a1"] = cut_front(1)

    @task
    def cut_b1():
        v["b1"] = cut_back(1)

    @task
    def cut_c():
        args = (history_dictionary, *v["x"].pieces()[1:])
        out = [((1, BASIS, 512), bf16)]
        v["c"] = Gather(line.run(cut_basis_body, "cut_basis", args, out, limit=3)[0], "c")

    for name in ("a0", "b0", "a1", "b1", "c"):
        tasks["step_" + name] = lambda name=name: v[name].step()
        tasks["last_" + name] = lambda name=name: v[name].last()

    @task
    def split_x():
        pieces = split_windows(line, history_series, n_tm, history_dictionary if fast else None)
        v["x"] = Exchange(line, pieces, n_tm)

    @task
    def split_g():
        v["g"] = Exchange(line, split_windows(line, remainder_adjoint, n_tm), n_tm)

    @task
    def select():
        args = (labels, prediction_adjoint.T)
        v["fg"] = line.run(select_body, "select", args, [((LANES, rows), bf16)], limit=4)[0]

    for name in ("x", "g", "rem", "der"):
        tasks["relay_" + name] = lambda name=name: v[name].relay()

    @task
    def merge_rem():
        pieces = v["rem"].pieces()
        v["remainder"] = merge_windows(line, history_series, pieces, -1)

    @task
    def merge_der():
        pieces = v["der"].pieces()
        v["derivative"] = merge_windows(line, remainder_adjoint, pieces, 1)

    @task
    def front_0():
        outs = front(line, 0, v["a0"].slots, v["x"].pieces(), rows)
        v["w1a"], v["w2a"], v["bias"], v["basis_a"], *v["h12"] = outs

    @task
    def rear_0():
        args = (v["b0"].slots, v["h12"][2], v["bias"], v["basis_a"], ())
        outs = rear(line, *args, width, v["h12"])
        v["w3a"], v["w4a"], v["wba"], v["wfa"] = outs[:4]
        v["act"], v["fore"] = outs[4:10], outs[10]
        v["h1a"], v["d1a"], v["h2a"], v["d2a"] = outs[11:]

    @task
    def cast_0():
        outs = backcast(line, 0, v["c"].slots, v["act"][4], v["x"].pieces())
        v["wva"], v["x2"], v["cast"] = outs

    @task
    def front_1():
        outs = front(line, 1, v["a1"].slots, [v["x2"]], rows, v["act"])
        v["w1b"], v["w2b"], v["bias"], v["basis_b"], v["h1"], v["d1"], v["h2"], v["d2"] = outs[:8]
        v["h3a"], v["d3a"], v["h4a"], v["d4a"], v["bta"], v["fta"] = outs[8:]

    @task
    def rear_1():
        args = (v["b1"].slots, v["h2"], v["bias"], v["basis_b"], (v["fore"], labels))
        outs = rear(line, *args, width)
        v["w3b"], v["w4b"], v["wbb"], v["wfb"] = outs[:4]
        v["h3"], v["d3"], v["h4"], v["d4"], v["bt"], v["ft"], v["fore"] = outs[4:]

    @task
    def cast_1():
        outs = backcast(line, 1, v["c"].slots, v["bt"], [v["cast"]])
        v["wvb"], v["rem"] = outs[0], Exchange(line, outs[1:], n_tm)

    @task
    def chain_rear_1():
        weights = (v["wvb"], v["basis_b"], v["wbb"], v["wfb"], v["w4b"])
        v["cr"] = chain_rear(line, v["g"].pieces(), v["fg"], weights, v["d4"], v["d3"], False)

    @task
    def terms_rear_1():
        args = ((*v["cr"][0:3], v["fg"]), (v["bt"], v["h4"], v["ft"]), ())
        v["t1"] = terms_rear(line, 1, *args, False)
        if fast:
            v["t1_core"] = core(v["t1"][1])

    @task
    def chain_front_1():
        weights = (v["w3b"], v["w2b"], v["w1b"])
        outs = chain_front(line, v["cr"][4], weights, v["d2"], v["d1"], None, False)
        v["cf"], v["gh2"] = outs[0:3], outs[3]

    @task
    def terms_front_1():
        more = (v["h3"], v["h2"], v["cr"][3], v["cr"][4])
        args = ((*v["cf"], v["cr"][5]), [v["x2"]], v["h1"], more)
        v["t2"] = terms_front(line, 1, *args, False)
        v["m1"] = Message("m1", v["t1"], v["t2"])

    @task
    def chain_rear_0():
        weights = (v["wva"], v["basis_a"], v["wba"], v["wfa"], v["w4a"])
        gs = [*v["g"].pieces(), v["gh2"]]
        v["cr"] = chain_rear(line, gs, v["fg"], weights, v["d4a"], v["d3a"], False)

    @task
    def terms_rear_0():
        more = (v["h3a"], v["h2a"], v["cr"][3], v["cr"][4])
        args = ((*v["cr"][0:3], v["fg"]), (v["bta"], v["h4a"], v["fta"]), more)
        outs = terms_rear(line, 0, *args, False)
        v["m3"] = Message("m3", outs[0:2], outs[2:4])

    @task
    def chain_front_0():
        weights = (v["w3a"], v["w2a"], v["w1a"])
        outs = chain_front(line, v["cr"][4], weights, v["d2a"], v["d1a"], v["gh2"], False)
        v["cf"], v["der"] = outs[0:3], Exchange(line, outs[3:6], n_tm)

    @task
    def terms_front_0():
        args = ((*v["cf"], v["cr"][5]), v["x"].pieces(), v["h1a"], ())
        v["m4"] = Message("m4", terms_front(line, 0, *args, False))

    for name in ("m1", "m3", "m4"):
        tasks["fold_" + name] = lambda name=name: v[name].fold()
        tasks["settle_" + name] = lambda name=name: v[name].last()

    if not fast:
        masters = (
            affine_kernels,
            affine_offsets,
            expansion_projection,
            history_dictionary,
            prediction_dictionary,
        )
        blocks, bases = shares_plain(*masters, n_tm)
        slots = {"a0": blocks[0][0], "b0": blocks[0][1], "a1": blocks[1][0], "b1": blocks[1][1], "c": bases}
        for name, value in slots.items():
            v[name] = Gather.__new__(Gather)
            v[name].slots = value
    for name in ORDER:
        name, _, us = name.partition(":")
        line.us = float(us) if us else None
        if fast or name.split("_")[0] not in ("cut", "step", "last", "fold", "settle"):
            tasks[name]()
    if fast:
        sums = (*v["m3"].sums, *v["m4"].sums, *v["m1"].sums)
        grads = finish(line, sums, width)
    else:
        m3 = [jnp.concatenate(pair, axis=1) for pair in zip(*v["m3"].packed)]
        records = [(m3, v["m4"].packed[0]), v["m1"].packed]
        grads = gradients_plain(records, n_tm, width)
    return (v["remainder"], v["fore"].T, v["derivative"], *grads)


ORDER = (
    "split_x",
    "cut_a0",
    "cut_b0",
    "step_a0",
    "cut_a1:20",
    "step_b0",
    "step_a0:0.2",
    "cut_b1:0.2",
    "step_b0",
    "relay_x",
    "last_a0:0",
    "step_a1:0.2",
    "step_a1",
    "cut_c",
    "front_0",
    "last_b0",
    "step_c",
    "split_g:0.2",
    "last_a1:8",
    "step_c",
    "step_b1",
    "rear_0:0.2",
    "last_c",
    "step_b1",
    "select:0.2",
    "cast_0",
    "front_1",
    "last_b1",
    "relay_g",
    "rear_1",
    "cast_1",
    "chain_rear_1",
    "terms_rear_1",
    "chain_front_1:3",
    "terms_front_1",
    "fold_m1:3",
    "chain_rear_0",
    "terms_rear_0:0.2",
    "chain_front_0:1",
    "fold_m3",
    "fold_m1:0",
    "terms_front_0",
    "fold_m4",
    "fold_m3:3",
    "fold_m1",
    "relay_rem",
    "fold_m4",
    "fold_m3",
    "settle_m1:0",
    "relay_der",
    "merge_der",
    "fold_m4",
    "settle_m3",
    "merge_rem",
    "settle_m4",
)


def solution(mesh):
    return jax.shard_map(
        functools.partial(body, mesh.shape["dp"], mesh.shape["tm"]),
        mesh=mesh,
        in_specs=(
            P("dp", "tm"),
            P(("dp", "tm")),
            P(None, None, "dp", None),
            P(None, None, "dp"),
            P(None, None, "dp", None),
            P(None, "dp", "tm"),
            P(None, "dp", None),
            P("dp", "tm"),
            P(("dp", "tm"), None),
        ),
        out_specs=(
            P("dp", "tm"),
            P(("dp", "tm"), None),
            P("dp", "tm"),
            P(None, None, "dp", None),
            P(None, None, "dp"),
            P(None, None, "dp", None),
            P(None, "dp", "tm"),
            P(None, "dp", None),
        ),
        check_vma=False,
    )
```

```python
import functools
import types

import jax
import jax.numpy as jnp
from jax import lax
from jax.experimental import pallas as pl
from jax.experimental.pallas import tpu as pltpu
from jax.sharding import PartitionSpec as P

HOR_Y = 6
HOR_Q = 8
HOR_M = 18
LAYERS = 4
LANES = 128
HALF = 32
GROUPS = 8
FRONT = 2 * HALF + 16
BACK = 4 * HALF
BASIS = 2 * HALF
HOPS = {
    "a0": (4, 2, 1),
    "b0": (4, 2, 1),
    "a1": (4, 2, 1),
    "b1": (4, 2, 1),
    "c": (4, 2, 1),
    "m1": (4, 1, 2),
    "m3": (4, 1, 2),
    "m4": (4, 2, 1),
}


def slot_shares(hops):
    return tuple(sum(bit for i, bit in enumerate(hops) if s >> i & 1) for s in range(GROUPS))


TILE = 512
CHUNK = 256

f32 = jnp.float32
bf16 = jnp.bfloat16
MIB = 1024 * 1024
FLOPS_PER_US = 150_000_000


def mm(a, b):
    return jnp.dot(a, b, preferred_element_type=f32)


def mm_nt(a, b):
    return lax.dot_general(a, b, (((1,), (1,)), ((), ())), preferred_element_type=f32)


def mm_tn(a, b):
    return lax.dot_general(a, b, (((0,), (0,)), ((), ())), preferred_element_type=f32)


def rows_at(start, size, align):
    return pl.ds(pl.multiple_of(start, align), size)


def in_group(labels, width):
    field = lax.broadcasted_iota(jnp.int32, (width, labels.shape[1]), 0)
    group = (
        (field >= HOR_Y).astype(jnp.int32)
        + (field >= HOR_Y + HOR_Q).astype(jnp.int32)
        + (field >= HOR_Y + HOR_Q + HOR_M).astype(jnp.int32)
    )
    return group == labels


def slot_rows(pos, q, s, hops):
    share = pos[0] ^ slot_shares(hops)[s]
    half = pos[1] ^ q
    row = share * (2 * HALF) + half * HALF
    block = share * 2 + half
    window_row = ((block // 4) ^ pos[2]) * LANES + (block % 4) * HALF
    return row, window_row


def slot_at(pos, share, hops):
    r = share ^ pos[0]
    place = {1: 0, 2: 1, 4: 2}
    return sum(((r >> place[bit]) & 1) << i for i, bit in enumerate(hops))


def size_of(shape):
    total = 1
    for extent in shape:
        total *= extent
    return total


class Inputs:
    def __init__(self, refs, copies):
        self.refs, self.copies = refs, copies

    def __getitem__(self, i):
        if isinstance(i, slice):
            return [self[j] for j in range(*i.indices(len(self.refs)))]
        if i in self.copies:
            self.copies.pop(i).wait()
        return self.refs[i]


class Line:
    def __init__(self, pos):
        self.pos, self.token, self.us = pos, None, None

    def batch(self, steps):
        shapes = [out for _, _, _, outs in steps for out in outs]
        args = [arg for _, _, arg_list, _ in steps for arg in arg_list]

        def body(pos, ins, outs, scratch):
            i = o = 0
            for _, run, arg_list, out_list in steps:
                run(pos, Inputs(ins.refs[i : i + len(arg_list)], {}), outs[o : o + len(out_list)], ())
                i, o = i + len(arg_list), o + len(out_list)

        name = "_and_".join(step[0] for step in steps)
        results = self.run(body, name, args, shapes, limit=6)
        split = []
        for _, _, _, out_list in steps:
            split.append(results[: len(out_list)])
            results = results[len(out_list) :]
        return split

    def run(self, body, name, args, outs, scratch=(), fetch=(), save=(), limit=12, after=(), us=0.5, stay=(), out_stays=False):
        token = [] if self.token is None else [self.token]
        extra = [*after, *token]
        fetch, save = list(fetch), list(save)
        n_in, n_out, n_extra = len(args), len(outs), len(extra)
        n_fetch, n_save = len(fetch), len(save)

        def kernel(pos_ref, *refs):
            refs = list(refs)
            given, refs = refs[:n_in], refs[n_in + n_extra :]
            results, refs = refs[:n_out], refs[n_out:]
            saved, refs = refs[:n_save], refs[n_save:]
            if out_stays:
                refs.pop(0)[...] = jnp.zeros((8, LANES), f32)
            landing, refs = refs[:n_fetch], refs[n_fetch:]
            sems = refs.pop() if n_fetch + n_save else None
            inputs, copies, leaving = list(given), {}, []
            for at, (i, buf) in enumerate(zip(fetch, landing)):
                copies[i] = pltpu.make_async_copy(given[i], buf, sems.at[at])
                copies[i].start()
                inputs[i] = buf
            for at, (i, dst) in enumerate(zip(save, saved)):
                leaving.append(pltpu.make_async_copy(given[i], dst, sems.at[n_fetch + at]))
                leaving[-1].start()
            body(pos_ref, Inputs(inputs, copies), results, refs)
            for copy in (*copies.values(), *leaving):
                copy.wait()

        vmem, hbm = pl.BlockSpec(memory_space=pltpu.VMEM), pl.BlockSpec(memory_space=pltpu.HBM)
        anywhere = pl.BlockSpec(memory_space=pl.ANY)
        place = pltpu.HBM if out_stays else jax.ShapeDtypeStruct
        shapes = [place(shape, dtype) for shape, dtype in outs]
        placed = [
            pltpu.with_memory_space_constraint(a, pltpu.HBM) if i in fetch or i in stay else a
            for i, a in enumerate(args)
        ]
        shapes += [pltpu.HBM(args[i].shape, args[i].dtype) for i in save]
        mark = [jax.ShapeDtypeStruct((8, LANES), f32)] if out_stays else []
        sems = [pltpu.SemaphoreType.DMA((n_fetch + n_save,))] if n_fetch + n_save else []
        results = list(pl.pallas_call(
            kernel,
            name=name,
            out_shape=shapes + mark,
            in_specs=[pl.BlockSpec(memory_space=pltpu.SMEM)]
            + [hbm if i in fetch or i in stay else vmem for i in range(n_in)]
            + [anywhere] * n_extra,
            out_specs=[hbm if out_stays else vmem] * n_out + [hbm] * n_save + [vmem] * len(mark),
            scratch_shapes=[pltpu.VMEM(args[i].shape, args[i].dtype) for i in fetch]
            + list(scratch)
            + sems,
            compiler_params=pltpu.CompilerParams(vmem_limit_bytes=limit * MIB),
            cost_estimate=pl.CostEstimate(
                flops=int((us if self.us is None else self.us) * FLOPS_PER_US),
                bytes_accessed=1,
                transcendentals=0,
            ),
        )(self.pos, *placed, *extra))
        if out_stays:
            self.token = results.pop()
        else:
            self.token = min(results, key=lambda a: a.size * a.dtype.itemsize)
        return results


def swap(x, axis, bit, size):
    return lax.ppermute(x, axis, [(i, i ^ bit) for i in range(size)])


class Exchange:
    def __init__(self, line, pieces, n_tm):
        self.line, self.n_tm = line, n_tm
        self.own, near, far = pieces
        self.far = swap(far, "tm", 2, n_tm)
        self.near = swap(near, "tm", 1, n_tm)

    def relay(self):
        (across,) = yield "relay", relay_body, (self.far,), [(self.far.shape[1:], bf16)]
        self.across = swap(across, "tm", 1, self.n_tm)

    def pieces(self):
        return [self.own, self.near, self.far, self.across]


def relay_body(pos, ins, outs, scratch):
    outs[0][...] = ins[0][1]


def flat(refs):
    return [ref if len(ref.shape) == 2 else ref.at[0] for ref in refs]


def split_body(with_basis, pos, ins, outs, scratch):
    landing, sems = scratch
    rows = landing.shape[1]
    copies = []
    for r in range(4):
        copies.append(pltpu.make_async_copy(ins[0].at[pos[2] ^ r], landing.at[r], sems.at[r]))
    for r in (2, 3, 1, 0):
        copies[r].start()
    if with_basis:
        for k in range(2):
            at = slice(rows + 2 * HALF * k, rows + 2 * HALF * (k + 1))
            value = ins[1][k].astype(bf16)
            for out in (outs[1], outs[2].at[0], outs[2].at[1]):
                out[at, :] = value
    for r in (2, 3, 1, 0):
        copies[r].wait()
        out = outs[2].at[r - 2] if r >= 2 else outs[r]
        out[0:rows, :] = landing[r].astype(bf16)


def piece_shapes(rows, more=0):
    sent = rows + more
    return [((rows, LANES), bf16), ((sent, LANES), bf16), ((2, sent, LANES), bf16)]


def split_windows(line, array, parts, basis=None):
    shape = (parts, array.shape[0] // parts, LANES)
    args = (array.reshape(shape),) if basis is None else (array.reshape(shape), basis)
    return line.run(
        functools.partial(split_body, basis is not None),
        "split_windows",
        args,
        piece_shapes(shape[1], 0 if basis is None else 2 * basis.shape[1]),
        [pltpu.VMEM(shape, f32), pltpu.SemaphoreType.DMA((parts,))],
        stay=(0,),
        limit=8,
        us=2.0,
    )


def merge_body(sign, pos, ins, outs, scratch):
    base, pieces = ins[0], flat(ins[1:5])
    leaving, sems = scratch
    parts = len(pieces)
    arrive, leave = [], []
    for r in range(parts):
        at = pos[2] ^ r
        leave.append(pltpu.make_async_copy(leaving.at[r], outs[0].at[at], sems.at[parts + r]))
    for r, piece in enumerate(pieces):
        value = piece[...].astype(f32)
        own = base[pos[2] ^ r]
        leaving[r] = own - value if sign < 0 else own + value
        leave[r].start()
    for copy in leave:
        copy.wait()


def merge_windows(line, base, pieces, sign):
    parts = len(pieces)
    shape = (parts, base.shape[0] // parts, LANES)
    out = line.run(
        functools.partial(merge_body, sign),
        "merge_windows",
        (base.reshape(shape), *pieces),
        [(shape, f32)],
        [pltpu.VMEM(shape, f32), pltpu.SemaphoreType.DMA((2 * parts,))],
        stay=(),
        out_stays=True,
        limit=12,
        us=3.5,
    )[0]
    return out.reshape(base.shape)


def activate(p):
    t = jnp.tanh(p)
    u = 1.0 + t
    h = p * u
    return h.astype(bf16), u + h * (1.0 - t)


def columns(refs, at):
    if len(refs) == 1:
        return refs[0][at, :]
    return jnp.concatenate([ref[at, :] for ref in refs], axis=1)


def put_pieces(refs, at, value):
    for r in range(4):
        ref = refs[2].at[r - 2] if r >= 2 else refs[r]
        ref[at, :] = value[:, r * LANES : (r + 1) * LANES]


def chunks(rows):
    return [slice(at, at + CHUNK) for at in range(0, rows, CHUNK)]


def front_body(n_x, hops, pos, ins, bufs, scratch):
    w1, w2, bias, basis, h1, d1, h2, d2 = bufs
    total = jnp.zeros((16, 2 * LANES), f32)
    for q in range(2):
        for s in range(GROUPS):
            ref, i = ins[2 * q + s // 4], s % 4
            row, window_row = slot_rows(pos, q, s, hops)
            w1[rows_at(window_row, HALF, HALF), :] = ref[i, 0:HALF, :] * 0.5
            w2[rows_at(row, HALF, HALF), :] = ref[i, HALF : 2 * HALF, :] * 0.5
            low = ref[i, 2 * HALF : FRONT, 0:LANES]
            high = ref[i, 2 * HALF : FRONT, LANES : 2 * LANES]
            basis[rows_at(row, 16, 16), :] = low
            basis[rows_at(row + 16, 16, 16), :] = high
            if q == 0:
                total += ref[i, 2 * HALF : FRONT, 2 * LANES :].astype(f32)
    bias[:, 0 : 2 * LANES] = total[0:8] * 0.5
    bias[:, 2 * LANES :] = total[8:16] * 0.5
    xs = flat(ins[4 : 4 + n_x])
    for at in chunks(h1.shape[0]):
        h, d = activate(mm(columns(xs, at), w1[...]) + bias[0:1, :])
        h1[at, :] = h
        d1[at, :] = d.astype(bf16)
    for at in chunks(h1.shape[0]):
        h, d = activate(mm(h1[at, :], w2[...]) + bias[1:2, :])
        h2[at, :] = h
        d2[at, :] = d.astype(bf16)


def front(line, k, slots, xs, rows, leaving=()):
    square = ((512, 512), bf16)
    hidden = ((rows, 512), bf16)
    args = (*slots, *xs, *leaving)
    return line.run(
        functools.partial(front_body, len(xs), HOPS["a" + str(k)]),
        "front",
        args,
        [square, square, ((8, 512), f32), ((512, LANES), bf16), hidden, hidden, hidden, hidden],
        save=range(len(args) - len(leaving), len(args)),
        limit=6,
        us=4.0,
    )


def rear_body(last, hops, pos, ins, bufs, scratch):
    w3, w4, wb, wf, h3, d3, h4, d4, bt, ft, fore_out = bufs
    for q in range(2):
        for s in range(GROUPS):
            ref, i = ins[2 * q + s // 4], s % 4
            row, _ = slot_rows(pos, q, s, hops)
            for m, w in enumerate((w3, w4, wb, wf)):
                part = ref[i, m * HALF : (m + 1) * HALF, :]
                w[rows_at(row, HALF, HALF), :] = part * 0.5 if m < 2 else part
    bias, h2, basis = ins[4], ins[5], ins[6]
    steps = chunks(h3.shape[0])
    for at in steps:
        h, d = activate(mm(h2[at, :], w3[...]) + bias[2:3, :])
        h3[at, :] = h
        d3[at, :] = d.astype(bf16)
    for at in steps:
        h, d = activate(mm(h3[at, :], w4[...]) + bias[3:4, :])
        h4[at, :] = h
        d4[at, :] = (0.5 * d).astype(bf16)
    for at in steps:
        bt[at, :] = mm(h4[at, :], wb[...]).astype(bf16)
    for at in steps:
        ft[at, :] = mm(h4[at, :], wf[...]).astype(bf16)
    width = fore_out.shape[0]
    for at in steps:
        fore = mm(ft[at, :], basis[...]).T[0:width, :]
        if last:
            fore = ins[7][:, at] + fore
            fore = jnp.where(in_group(ins[8][0:1, at], width), fore, 0.0)
        fore_out[:, at] = fore


def rear(line, slots, h2, bias, basis, extra, width, leaving=()):
    rows = h2.shape[0]
    square = ((512, 512), bf16)
    hidden = ((rows, 512), bf16)
    args = (*slots, bias, h2, basis, *extra, *leaving)
    return line.run(
        functools.partial(rear_body, bool(extra), HOPS["b1" if extra else "b0"]),
        "rear",
        args,
        [square] * 4 + [hidden] * 6 + [((width, rows), f32)],
        save=range(len(args) - len(leaving), len(args)),
        limit=6,
        us=6.5,
    )


def cast_body(k, pos, ins, bufs, scratch):
    wv = bufs[0]
    for q in range(2):
        for s in range(GROUPS):
            ref, i = ins[2 * q + s // 4], s % 4
            row, _ = slot_rows(pos, q, s, HOPS["c"])
            for r in range(4):
                part = ref[i, k * HALF : (k + 1) * HALF, r * LANES : (r + 1) * LANES]
                at = r ^ q
                wv[rows_at(row, HALF, HALF), at * LANES : (at + 1) * LANES] = part
    bt = ins[4]
    for at in chunks(bt.shape[0]):
        cast = mm(bt[at, :], wv[...])
        if k == 0:
            bufs[1][at, :] = (columns(flat(ins[5:9]), at).astype(f32) - cast).astype(bf16)
            bufs[2][at, :] = cast
        else:
            put_pieces(bufs[1:4], at, (cast + ins[5][at, :]).astype(bf16))


def backcast(line, k, slots, bt, extra, leaving=()):
    rows = bt.shape[0]
    hidden = (rows, 512)
    outs = [(hidden, bf16), (hidden, f32)] if k == 0 else piece_shapes(rows)
    return line.run(
        functools.partial(cast_body, k),
        "backcast",
        (*slots, bt, *extra, *leaving),
        [((512, 512), bf16)] + outs,
        save=range(5 + len(extra), 5 + len(extra) + len(leaving)),
        limit=6,
        us=1.5,
    )


def row_sum(value):
    return jnp.sum(value.astype(f32), axis=0, keepdims=True)


def pack_pair(packed, rows, lanes, slot, first, second, pos):
    keep, send = packed
    lower = pos[1] == 0
    first, second = first.astype(bf16), second.astype(bf16)
    keep[slot, rows, lanes] = jnp.where(lower, first, second)
    send[slot, rows, lanes] = jnp.where(lower, second, first)


def pack_rows(packed, at, value, pos, hops):
    for share in range(GROUPS):
        row = share * 2 * HALF
        pack_pair(
            packed,
            slice(at, at + HALF),
            slice(None),
            slot_at(pos, share, hops),
            value[row : row + HALF, :],
            value[row + HALF : row + 2 * HALF, :],
            pos,
        )


def chain_rear_body(n_g, pos, ins, outs, scratch):
    g, g_back, g_fore, g4, g3, bias = outs
    wv, basis, wb, wf, w4 = ins[n_g + 1 : n_g + 6]
    gs, fg = flat(ins[0:4]) + ins[4:n_g], ins[n_g]
    steps = chunks(g.shape[0])
    for at in steps:
        value = columns(gs[:4], at)
        if n_g == 5:
            value = (value.astype(f32) + gs[4][at, :].astype(f32)).astype(bf16)
        g[at, :] = -value
        g_back[at, :] = mm_nt(g[at, :], wv[...]).astype(bf16)
    for at in steps:
        g_fore[at, :] = mm_nt(fg[:, at].T, basis[...]).astype(bf16)
    d4 = ins[n_g + 6]
    b3 = b4 = jnp.zeros((1, 512), f32)
    for at in steps:
        gh = mm_nt(g_back[at, :], wb[...]) + mm_nt(g_fore[at, :], wf[...])
        value = (gh * d4[at, :].astype(f32)).astype(bf16)
        g4[at, :] = value
        b4 += row_sum(value)
    d3 = ins[n_g + 7]
    for at in steps:
        gh = mm_nt(g4[at, :], w4[...])
        value = (gh * d3[at, :].astype(f32)).astype(bf16)
        g3[at, :] = value
        b3 += row_sum(value)
    bias[...] = jnp.concatenate([b3, b4, jnp.zeros((6, 512), f32)], axis=0)


def chain_rear(line, gs, fg, weights, d4, d3, fetch):
    rows = fg.shape[1]
    n = len(gs) + 1 + len(weights)
    return line.run(
        functools.partial(chain_rear_body, len(gs)),
        "chain_rear",
        (*gs, fg, *weights, d4, d3),
        [((rows, 512), bf16)] * 5 + [((8, 512), f32)],
        fetch=(n, n + 1) if fetch else (),
        limit=10 if fetch else 6,
        us=7.0,
    )


def chain_front_body(last, pos, ins, outs, scratch):
    g2, g1, bias = outs[:3]
    g3, w3, w2, w1 = ins[0:4]
    steps = chunks(g1.shape[0])
    b1 = b2 = jnp.zeros((1, 512), f32)
    d2 = ins[4]
    for at in steps:
        gh = mm_nt(g3[at, :], w3[...])
        value = (gh * d2[at, :].astype(f32)).astype(bf16)
        g2[at, :] = value
        b2 += row_sum(value)
    d1 = ins[5]
    for at in steps:
        gh = mm_nt(g2[at, :], w2[...])
        value = (gh * d1[at, :].astype(f32)).astype(bf16)
        g1[at, :] = value
        b1 += row_sum(value)
    for at in steps:
        gh = (2.0 * mm_nt(g1[at, :], w1[...])).astype(bf16)
        if last:
            gh = (gh.astype(f32) + ins[6][at, :].astype(f32)).astype(bf16)
            put_pieces(outs[3:6], at, gh)
        else:
            outs[3][at, :] = gh
    bias[...] = jnp.concatenate([b1, b2, jnp.zeros((6, 512), f32)], axis=0)


def chain_front(line, g3, weights, d2, d1, gh2, fetch):
    rows = g3.shape[0]
    last = gh2 is not None
    outs = piece_shapes(rows) if last else [((rows, 512), bf16)]
    return line.run(
        functools.partial(chain_front_body, last),
        "chain_front",
        (g3, *weights, d2, d1, *([gh2] if last else [])),
        [((rows, 512), bf16)] * 2 + [((8, 512), f32)] + outs,
        fetch=(4, 5) if fetch else (),
        limit=10 if fetch else 6,
        us=4.5,
    )


def message_rows(k):
    first = {"B": 0, "F": HALF, "V": 2 * HALF, "U": 3 * HALF}
    second = {"L2": 0, "L1": HALF, "bias": 2 * HALF}
    sizes = [3 * HALF + 16, 2 * HALF + 16]
    at = 1 if k else 0
    for name in ("L4", "L3"):
        (first, second)[at][name] = sizes[at]
        sizes[at] += HALF
    return first, second, sizes


def whole_rows(ref):
    return slice(0, ref.shape[0])


def terms_rear_body(k, pos, ins, outs, scratch):
    packed, second = outs[0:2], outs[2:4]
    at, _, _ = message_rows(k)
    hops = HOPS["m1" if k else "m3"]
    g, g_back, g_fore, fg = ins[0:4]
    bt = ins[4]
    value = mm_tn(bt[...], g[...])
    for share in range(GROUPS):
        slot = slot_at(pos, share, hops)
        for r in range(4):
            for j in range(2):
                row, lane = (2 * share + j) * HALF, (2 * j + r // 2) * LANES
                part = value[row : row + HALF, r * LANES : (r + 1) * LANES].astype(bf16)
                packed[r % 2][slot, at["V"] : at["V"] + HALF, lane : lane + LANES] = part
    h4 = ins[5]
    pack_rows(packed, at["B"], mm_tn(h4[...], g_back[...]), pos, hops)
    pack_rows(packed, at["F"], mm_tn(h4[...], g_fore[...]), pos, hops)
    ft = ins[6]
    value = mm(fg[...], ft[...]).T
    rows = slice(at["U"], at["U"] + 16)
    for share in range(GROUPS):
        row, slot = share * 2 * HALF, slot_at(pos, share, hops)
        for j in range(2):
            lanes = slice(j * LANES, (j + 1) * LANES)
            low = value[row + 16 * j : row + 16 * (j + 1), :]
            high = value[row + HALF + 16 * j : row + HALF + 16 * (j + 1), :]
            pack_pair(packed, rows, lanes, slot, low, high, pos)
        for out in packed:
            out[slot, rows, 2 * LANES :] = jnp.zeros((16, 2 * LANES), bf16)
    if "L4" in at:
        h3, h2, g4, g3 = ins[7], ins[8], ins[9], ins[10]
        pack_rows(second, 0, mm_tn(h3[...], g4[...]), pos, hops)
        pack_rows(second, HALF, mm_tn(h2[...], g3[...]), pos, hops)


def terms_rear(line, k, grads, hidden, more, fetch):
    args = (*grads, *hidden, *more)
    heights = (3 * HALF + 16, 2 * HALF)
    outs = [((GROUPS, height, 512), bf16) for height in heights[: 2 if more else 1] for _ in range(2)]
    return line.run(
        functools.partial(terms_rear_body, k),
        "terms_rear",
        args,
        outs,
        fetch=[i for i in range(4, min(9, len(args)))] if fetch else (),
        limit=16 if fetch else 6,
        us=4.5 if k else 8.0,
    )


def terms_front_body(k, n_x, pos, ins, packed, scratch):
    _, at, _ = message_rows(k)
    hops = HOPS["m1" if k else "m4"]
    g2, g1, low_bias, high_bias = ins[0:4]
    bias = jnp.concatenate([low_bias[0:2, :], high_bias[0:2, :], jnp.zeros((4, 512), f32)], axis=0)
    bias = jnp.concatenate([bias[:, 0 : 2 * LANES], bias[:, 2 * LANES :]], axis=0).astype(bf16)
    rows = slice(at["bias"], at["bias"] + 16)
    for s in range(GROUPS):
        for out in packed:
            out[s, rows, 0 : 2 * LANES] = jnp.zeros((16, 2 * LANES), bf16)
            out[s, rows, 2 * LANES :] = bias
    xs = flat(ins[4 : 4 + n_x])
    value = mm_tn(columns(xs, whole_rows(g1)), g1[...])
    for r in range(4):
        for i in range(2):
            row = r * LANES + i * 2 * HALF
            pack_pair(
                packed,
                slice(at["L1"], at["L1"] + HALF),
                slice(None),
                slot_at(pos, (pos[2] ^ r) * 2 + i, hops),
                value[row : row + HALF, :],
                value[row + HALF : row + 2 * HALF, :],
                pos,
            )
    h1 = ins[4 + n_x]
    pack_rows(packed, at["L2"], mm_tn(h1[...], g2[...]), pos, hops)
    if "L4" in at:
        h3, h2, g4, g3 = ins[5 + n_x : 9 + n_x]
        pack_rows(packed, at["L4"], mm_tn(h3[...], g4[...]), pos, hops)
        pack_rows(packed, at["L3"], mm_tn(h2[...], g3[...]), pos, hops)


def terms_front(line, k, grads, xs, h1, more, fetch):
    args = (*grads, *xs, h1, *more)
    out = ((GROUPS, message_rows(k)[2][1], 512), bf16)
    return line.run(
        functools.partial(terms_front_body, k, len(xs)),
        "terms_front",
        args,
        [out, out],
        fetch=(4 + len(xs),) if fetch else (),
        limit=8,
        us=5.5 if k else 3.0,
    )


def pack_misc(basis, offsets):
    lead = basis.shape[:-2]
    offsets = jnp.concatenate([offsets, jnp.zeros_like(offsets)], axis=-2)
    return jnp.concatenate(
        [
            basis[..., 0:16, :],
            basis[..., 16:32, :],
            jnp.concatenate([offsets[..., 0 : 2 * LANES], offsets[..., 2 * LANES :]], axis=-2),
        ],
        axis=-1,
    ).reshape(*lead, 16, 512)


def select_body(pos, ins, outs, scratch):
    labels, adjoint = ins[0], ins[1]
    width = adjoint.shape[0]
    for at in chunks(adjoint.shape[1]):
        value = jnp.where(in_group(labels[0:1, at], width), adjoint[:, at], 0.0)
        outs[0][0:width, at] = value.astype(bf16)
    outs[0][width:, :] = jnp.zeros((LANES - width, adjoint.shape[1]), bf16)


def cut_body(pos, ins, outs, scratch):
    kernels, projection, basis, offsets = ins[0:4]
    rows_in, pair_in, basis_in, sems = scratch
    half = rows_at(pos[1] * HALF, HALF, HALF)
    copies = []
    for k in range(2):
        copies += [
            pltpu.make_async_copy(kernels.at[k, :, half, :], rows_in.at[k], sems.at[k, 0]),
            pltpu.make_async_copy(basis.at[k, half, :], basis_in.at[k], sems.at[k, 1]),
            pltpu.make_async_copy(projection.at[k, :, half, :], pair_in.at[k], sems.at[k, 2]),
        ]
    for copy in copies:
        copy.start()
    rows, width = slice(2 * HALF, FRONT), basis.shape[2]
    for k in range(2):
        front, back = outs[2 * k : 2 * k + 2]
        front[0, rows, :] = jnp.zeros((16, 512), bf16)
        own = jnp.concatenate([offsets[k], jnp.zeros_like(offsets[k])], axis=0)
        own = jnp.concatenate([jnp.where(pos[0] % 4 == i, own, 0.0) for i in range(4)], axis=1)
        own = jnp.concatenate([jnp.where(pos[0] // 4 == i, own, 0.0) for i in range(2)], axis=0)
        front[0, rows, 2 * LANES :] = own.astype(bf16)
    for copy in copies:
        copy.wait()
    for k in range(2):
        front, back = outs[2 * k : 2 * k + 2]
        for j in range(2):
            part = basis_in[k, 16 * j : 16 * (j + 1), :]
            front[0, rows, j * LANES : j * LANES + width] = part.astype(bf16)
        for i in range(2):
            at = slice(i * HALF, (i + 1) * HALF)
            front[0, at, :] = rows_in[k, i].astype(bf16)
            back[0, at, :] = rows_in[k, 2 + i].astype(bf16)
            back[0, (2 + i) * HALF : (3 + i) * HALF, :] = pair_in[k, i].astype(bf16)


def cut_basis_body(pos, ins, outs, scratch):
    own, near, far, across = ins[0:4]
    first = near.shape[0] - 4 * HALF
    for k in range(2):
        at = first + 2 * HALF * k + pos[1] * HALF
        parts = [own[k, rows_at(pos[1] * HALF, HALF, HALF), :].astype(bf16)]
        parts += [ref[rows_at(at, HALF, HALF), :] for ref in (near, far.at[0], across)]
        outs[0][0, k * HALF : (k + 1) * HALF, :] = jnp.concatenate(parts, axis=1)


def join_body(pos, ins, outs, scratch):
    at = 0
    for ref in ins[0 : len(ins.refs)]:
        outs[0][at : at + ref.shape[0]] = ref[...]
        at += ref.shape[0]


def join(*parts):
    count = sum(part.shape[0] for part in parts)
    return "join", join_body, parts, [((count, *parts[0].shape[1:]), bf16)]


def fold_body(n, pos, ins, outs, scratch):
    at = 0
    for kept, arrived in zip(ins[0 : len(ins.refs) : 2], ins[1 : len(ins.refs) : 2]):
        rows = slice(at, at + kept.shape[1])
        at += kept.shape[1]
        for s in range(2 * n):
            total = kept[s].astype(f32) + arrived[s].astype(f32)
            if s < n:
                outs[0][s, rows, :] = total
            else:
                outs[1][s - n, rows, :] = total.astype(bf16)


def fold(*terms):
    n = terms[0].shape[0] // 2
    shape = (n, sum(term.shape[1] for term in terms[::2]), terms[0].shape[2])
    return "fold", functools.partial(fold_body, n), terms, [(shape, f32), (shape, bf16)]


def settle_body(pos, ins, outs, scratch):
    outs[0][...] = (ins[0][0] + ins[1][0].astype(f32)).astype(bf16)


def settle(kept, arrived):
    return "settle", settle_body, (kept, arrived), [(kept.shape[1:], bf16)]


def finish_body(width, pos, ins, outs, scratch):
    kernels, bias_out, projection, history_basis, forecast_basis = outs
    lower = pos[1] == 0
    for k in range(2):
        first, second, sizes = message_rows(k)
        places = {}
        for m, rows in enumerate((first, second)):
            one = 0 if k else 4 * m
            own, core, far, across = ins[8 * k + one : 8 * k + one + 4]
            for name, at in rows.items():
                places[name] = (own, core, far, across, at + (sizes[0] if k and m else 0))

        def both(name, height):
            own, core, far, across, at = places[name]
            rows = slice(at, at + height)
            mine = own[rows, :].astype(f32) + far[rows, :].astype(f32)
            other = core[rows, :].astype(f32) + across[rows, :].astype(f32)
            return jnp.where(lower, mine, other), jnp.where(lower, other, mine), mine

        targets = [("B", projection, 0), ("F", projection, 1)]
        targets += [("L" + str(layer + 1), kernels, layer) for layer in range(LAYERS)]
        for name, out, index in targets:
            a, b, _ = both(name, HALF)
            out[k, index, 0:HALF, :] = a
            out[k, index, HALF : 2 * HALF, :] = b
        own, _, far, _, at = places["V"]
        for j in range(2):
            lanes = slice(2 * j * LANES, (2 * j + 1) * LANES)
            theirs = slice((2 * j + 1) * LANES, (2 * j + 2) * LANES)
            rows = slice(at, at + HALF)
            total = own[rows, lanes].astype(f32) + far[rows, theirs].astype(f32)
            history_basis[k, j * HALF : (j + 1) * HALF, :] = total
        a, b, _ = both("U", 16)
        for j, value in enumerate((a, b)):
            for i in range(2):
                row = j * HALF + i * 16
                part = value[:, i * LANES : i * LANES + width]
                forecast_basis[k, row : row + 16, :] = part
        _, _, mine = both("bias", 16)
        total = jnp.zeros(bias_out.shape[1:], f32)
        for share in range(GROUPS):
            row, lane = 8 * (share // 4), 2 * LANES + (share % 4) * 2 * HALF
            part = mine[row : row + LAYERS, lane : lane + 2 * HALF]
            total = total + jnp.where(pos[0] == share, part, 0.0)
        bias_out[k] = total


def finish(line, sums, width):
    share = 2 * HALF
    return line.run(
        functools.partial(finish_body, width),
        "finish",
        sums,
        [
            ((2, LAYERS, share, 512), f32),
            ((2, LAYERS, share), f32),
            ((2, 2, share, 512), f32),
            ((2, share, LANES), f32),
            ((2, share, width), f32),
        ],
        limit=8,
    )


def slots_of(x, hops):
    x = x.reshape(GROUPS, 2, HALF, x.shape[-1]).swapaxes(0, 1)
    return x[:, jnp.array(slot_shares(hops))]


def in_order(x, hops):
    shares = slot_shares(hops)
    return x[:, jnp.array([shares.index(share) for share in range(GROUPS)])]


def flat_rows(x):
    return x.swapaxes(0, 1).reshape(2 * GROUPS * HALF, x.shape[-1])


def four(x):
    return x[0, 0:4], x[0, 4:8], x[1, 0:4], x[1, 4:8]


def shares_plain(kernels, offsets, projection, history_basis, forecast_basis, n_tm):
    tm = lax.axis_index("tm")

    def gather(x, axis, over="dp"):
        return lax.all_gather(x.astype(bf16), over, axis=axis, tiled=True)

    order = [jnp.bitwise_xor(tm, r) for r in range(n_tm)]
    out, bases = [], []
    for k in range(kernels.shape[0]):
        w = gather(kernels[k], 1)
        b = gather(offsets[k], 1)
        p = gather(projection[k], 1)
        u = gather(forecast_basis[k], 0)
        u = jnp.pad(u, ((0, 0), (0, LANES - u.shape[-1])))
        v = gather(gather(history_basis[k], 0), 1, "tm")
        v = jnp.concatenate(
            [lax.dynamic_slice_in_dim(v, at * LANES, LANES, 1) for at in order], axis=1
        )
        v = slots_of(v, HOPS["c"])
        other = [v[1, ..., (r ^ 1) * LANES : ((r ^ 1) + 1) * LANES] for r in range(4)]
        v = jnp.stack([v[0], jnp.concatenate(other, axis=-1)])
        offs = jnp.zeros((2, GROUPS, LAYERS, 512), bf16).at[0, 0].set(b)
        front_hops, back_hops = HOPS["a" + str(k)], HOPS["b" + str(k)]
        misc = pack_misc(slots_of(u, front_hops), offs)
        first = [slots_of(x, front_hops) for x in (w[0], w[1])] + [misc]
        first = jnp.concatenate(first, axis=2)
        second = jnp.concatenate([slots_of(x, back_hops) for x in (w[2], w[3], p[0], p[1])], axis=2)
        out.append((four(first), four(second)))
        bases.append(v)
    return out, four(jnp.concatenate(bases, axis=2))


def gradients_plain(records, n_tm, width):
    def reduce(x, axis):
        return lax.psum_scatter(
            lax.psum(x.astype(bf16), "tm").astype(f32), "dp", scatter_dimension=axis, tiled=True
        )

    results = [[], [], [], [], []]
    for k, messages in enumerate(records):
        pieces = {}
        for m, message in enumerate(messages):
            message = jnp.stack(message)
            hops = HOPS["m1" if k else ("m3", "m4")[m]]
            for name, at in message_rows(k)[m].items():
                height = 16 if name in ("U", "bias") else HALF
                pieces[name] = in_order(message[:, :, at : at + height, :], hops)
        square = {name: flat_rows(pieces[name]) for name in ("L1", "L2", "L3", "L4", "B", "F")}
        results[0].append(reduce(jnp.stack([square["L" + str(i)] for i in range(1, 5)]), 1))
        bias = pieces["bias"][0, 0]
        bias = jnp.concatenate([bias[0:4, 2 * LANES :], bias[8:12, 2 * LANES :]], axis=1)
        results[1].append(reduce(bias, 1))
        results[2].append(reduce(jnp.stack([square["B"], square["F"]]), 1))
        v = pieces["V"]
        v = jnp.concatenate([v[..., 0 : 2 * LANES], v[..., 2 * LANES :]], axis=2)
        v = v.reshape(2, 2 * GROUPS * HALF, 2, LANES)
        blocks = [v[r % 2, :, r // 2] for r in range(4)]
        total = blocks[0].astype(f32)
        for r in range(1, n_tm):
            total = total + swap(blocks[r], "tm", r, n_tm).astype(f32)
        results[3].append(lax.psum_scatter(total, "dp", scatter_dimension=0, tiled=True))
        u = pieces["U"]
        u = jnp.concatenate([u[..., 0:LANES], u[..., LANES : 2 * LANES]], axis=2)
        results[4].append(reduce(flat_rows(u), 0)[:, 0:width])
    return [jnp.stack(x) for x in results]


def body(
    n_dp,
    n_tm,
    history_series,
    frequency_labels,
    affine_kernels,
    affine_offsets,
    expansion_projection,
    history_dictionary,
    prediction_dictionary,
    remainder_adjoint,
    prediction_adjoint,
):
    dp = lax.axis_index("dp")
    tm = lax.axis_index("tm")
    fast = n_dp == GROUPS
    zero = jnp.zeros((), jnp.int32)
    pos = jnp.stack([dp if fast else zero, tm % 2 if fast else zero, tm]).astype(jnp.int32)
    line = Line(pos)
    width = prediction_adjoint.shape[1]
    rows = frequency_labels.shape[0]
    labels = frequency_labels.reshape(1, rows)

    def hop(x, bit):
        return swap(x, "dp", bit, n_dp)

    def core(x):
        return swap(x, "tm", 1, n_tm)

    class Gather:
        def __init__(self, own, name):
            self.x, self.hops = own, list(HOPS[name])
            self.arriving = hop(own, self.hops.pop(0))

        def step(self):
            (self.x,) = yield join(self.x, self.arriving)
            self.arriving = hop(self.x, self.hops.pop(0))
            if not self.hops:
                self.low_core = core(self.x)

        def last(self):
            (high,) = yield join(self.arriving)
            self.slots = self.x, high, self.low_core, core(high)

    class Message:
        def __init__(self, name, *packed):
            self.packed, self.terms, self.hops = packed, [], list(HOPS[name])
            if fast:
                for kept, sent in packed:
                    self.terms += [kept, core(sent)]

        def fold(self):
            kept, out = yield fold(*self.terms)
            self.terms = [kept, hop(out, self.hops.pop())]

        def last(self):
            (own,) = yield settle(*self.terms)
            self.sums = [own] + [swap(own, "tm", r, n_tm) for r in (1, 2, 3)]

    v = types.SimpleNamespace()
    t = types.SimpleNamespace()

    def task(run):
        setattr(t, run.__name__, run)
        return run

    @task
    def cut():
        args = (affine_kernels, expansion_projection, prediction_dictionary, affine_offsets)
        scratch = [
            pltpu.VMEM((2, LAYERS, HALF, 512), f32),
            pltpu.VMEM((2, 2, HALF, 512), f32),
            pltpu.VMEM((2, HALF, width), f32),
            pltpu.SemaphoreType.DMA((2, 3)),
        ]
        outs = [((1, FRONT, 512), bf16), ((1, BACK, 512), bf16)] * 2
        chunks = line.run(cut_body, "cut", args, outs, scratch, stay=(0, 1, 2), limit=4)
        names = ("a0", "b0", "a1", "b1")
        v.a0, v.b0, v.a1, v.b1 = (Gather(x, name) for x, name in zip(chunks, names))

    @task
    def cut_c():
        args = (history_dictionary, *v.x.pieces()[1:])
        (own,) = yield "cut_basis", cut_basis_body, args, [((1, BASIS, 512), bf16)]
        v.c = Gather(own, "c")

    for name in ("a0", "b0", "a1", "b1", "c"):
        setattr(t, "step_" + name, lambda name=name: getattr(v, name).step())
        setattr(t, "last_" + name, lambda name=name: getattr(v, name).last())

    @task
    def split_x():
        pieces = split_windows(line, history_series, n_tm, history_dictionary if fast else None)
        v.x = Exchange(line, pieces, n_tm)

    @task
    def split_g():
        v.g = Exchange(line, split_windows(line, remainder_adjoint, n_tm), n_tm)

    @task
    def select():
        out = [((LANES, rows), bf16)]
        (v.fg,) = yield "select", select_body, (labels, prediction_adjoint.T), out

    for name in ("x", "g", "rem", "der"):
        setattr(t, "relay_" + name, lambda name=name: getattr(v, name).relay())

    @task
    def merge_rem():
        pieces = v.rem.pieces()
        v.remainder = merge_windows(line, history_series, pieces, -1)

    @task
    def merge_der():
        pieces = v.der.pieces()
        v.derivative = merge_windows(line, remainder_adjoint, pieces, 1)

    @task
    def front_0():
        outs = front(line, 0, v.a0.slots, v.x.pieces(), rows)
        v.w1a, v.w2a, v.bias, v.basis_a, *v.h12 = outs

    @task
    def rear_0():
        args = (v.b0.slots, v.h12[2], v.bias, v.basis_a, ())
        outs = rear(line, *args, width, v.h12)
        v.w3a, v.w4a, v.wba, v.wfa = outs[:4]
        v.act, v.fore = outs[4:10], outs[10]
        v.h1a, v.d1a, v.h2a, v.d2a = outs[11:]

    @task
    def cast_0():
        outs = backcast(line, 0, v.c.slots, v.act[4], v.x.pieces(), v.act[0:2])
        v.wva, v.x2, v.cast, v.h3a, v.d3a = outs

    @task
    def front_1():
        outs = front(line, 1, v.a1.slots, [v.x2], rows, v.act[2:5])
        v.w1b, v.w2b, v.bias, v.basis_b, v.h1, v.d1, v.h2, v.d2 = outs[:8]
        v.h4a, v.d4a, v.bta = outs[8:]

    @task
    def rear_1():
        args = (v.b1.slots, v.h2, v.bias, v.basis_b, (v.fore, labels))
        outs = rear(line, *args, width, v.act[5:6])
        v.w3b, v.w4b, v.wbb, v.wfb = outs[:4]
        v.h3, v.d3, v.h4, v.d4, v.bt, v.ft, v.fore, v.fta = outs[4:]

    @task
    def cast_1():
        outs = backcast(line, 1, v.c.slots, v.bt, [v.cast])
        v.wvb, v.rem = outs[0], Exchange(line, outs[1:], n_tm)

    @task
    def chain_rear_1():
        weights = (v.wvb, v.basis_b, v.wbb, v.wfb, v.w4b)
        v.cr = chain_rear(line, v.g.pieces(), v.fg, weights, v.d4, v.d3, False)

    @task
    def terms_rear_1():
        args = ((*v.cr[0:3], v.fg), (v.bt, v.h4, v.ft), ())
        v.t1 = terms_rear(line, 1, *args, False)

    @task
    def chain_front_1():
        weights = (v.w3b, v.w2b, v.w1b)
        outs = chain_front(line, v.cr[4], weights, v.d2, v.d1, None, False)
        v.cf, v.gh2 = outs[0:3], outs[3]

    @task
    def terms_front_1():
        more = (v.h3, v.h2, v.cr[3], v.cr[4])
        args = ((*v.cf, v.cr[5]), [v.x2], v.h1, more)
        v.t2 = terms_front(line, 1, *args, False)
        v.m1 = Message("m1", v.t1, v.t2)

    @task
    def chain_rear_0():
        weights = (v.wva, v.basis_a, v.wba, v.wfa, v.w4a)
        gs = [*v.g.pieces(), v.gh2]
        v.cr = chain_rear(line, gs, v.fg, weights, v.d4a, v.d3a, False)

    @task
    def terms_rear_0():
        more = (v.h3a, v.h2a, v.cr[3], v.cr[4])
        args = ((*v.cr[0:3], v.fg), (v.bta, v.h4a, v.fta), more)
        outs = terms_rear(line, 0, *args, False)
        v.m3 = Message("m3", outs[0:2], outs[2:4])

    @task
    def chain_front_0():
        weights = (v.w3a, v.w2a, v.w1a)
        outs = chain_front(line, v.cr[4], weights, v.d2a, v.d1a, v.gh2, False)
        v.cf, v.der = outs[0:3], Exchange(line, outs[3:6], n_tm)

    @task
    def terms_front_0():
        args = ((*v.cf, v.cr[5]), v.x.pieces(), v.h1a, ())
        v.m4 = Message("m4", terms_front(line, 0, *args, False))

    for name in ("m1", "m3", "m4"):
        setattr(t, "fold_" + name, lambda name=name: getattr(v, name).fold())
        setattr(t, "settle_" + name, lambda name=name: getattr(v, name).last())

    if not fast:
        masters = (
            affine_kernels,
            affine_offsets,
            expansion_projection,
            history_dictionary,
            prediction_dictionary,
        )
        blocks, bases = shares_plain(*masters, n_tm)
        v.a0, v.b0, v.a1, v.b1, v.c = (Gather.__new__(Gather) for _ in range(5))
        v.a0.slots, v.b0.slots = blocks[0]
        v.a1.slots, v.b1.slots = blocks[1]
        v.c.slots = bases
        for name in vars(t):
            if name.startswith(("cut", "step", "last", "fold", "settle")):
                setattr(t, name, lambda: None)
    for us, *runs in order(t):
        line.us = us
        steps = [step for step in [run() for run in runs] if step is not None]
        if steps:
            for step, result in zip(steps, line.batch([next(step) for step in steps])):
                try:
                    step.send(result)
                except StopIteration:
                    pass
    if fast:
        sums = (*v.m3.sums, *v.m4.sums, *v.m1.sums)
        grads = finish(line, sums, width)
    else:
        m3 = [jnp.concatenate(pair, axis=1) for pair in zip(*v.m3.packed)]
        records = [(m3, v.m4.packed[0]), v.m1.packed]
        grads = gradients_plain(records, n_tm, width)
    return (v.remainder, v.fore.T, v.derivative, *grads)


def order(t):
    return (
        (0, t.split_x),
        (None, t.cut),
        (None, t.step_a0),
        (3, t.step_b0),
        (3, t.step_a0),
        (None, t.step_a1),
        (None, t.last_a0),
        (None, t.relay_x),
        (0.2, t.step_b0),
        (0.2, t.cut_c),
        (None, t.front_0),
        (None, t.step_a1, t.step_c),
        (0.2, t.step_c),
        (20, t.last_b0),
        (None, t.split_g),
        (8, t.step_b1),
        (20, t.last_a1),
        (None, t.rear_0),
        (None, t.step_b1),
        (3, t.last_c),
        (1, t.cast_0),
        (8, t.select),
        (None, t.front_1),
        (None, t.last_b1),
        (None, t.relay_g),
        (1, t.rear_1),
        (None, t.cast_1),
        (1, t.chain_rear_1),
        (8, t.terms_rear_1),
        (20, t.chain_front_1),
        (0, t.terms_front_1),
        (None, t.fold_m1),
        (None, t.chain_rear_0),
        (None, t.terms_rear_0),
        (20, t.chain_front_0),
        (1, t.relay_rem),
        (None, t.fold_m3),
        (None, t.fold_m1),
        (20, t.terms_front_0),
        (None, t.merge_rem),
        (1, t.fold_m4),
        (0.2, t.fold_m3),
        (20, t.fold_m1),
        (None, t.fold_m4),
        (20, t.settle_m1, t.fold_m3, t.relay_der),
        (None, t.merge_der),
        (None, t.settle_m3, t.fold_m4),
        (0.2, t.settle_m4),
    )


def solution(mesh):
    return jax.shard_map(
        functools.partial(body, mesh.shape["dp"], mesh.shape["tm"]),
        mesh=mesh,
        in_specs=(
            P("dp", "tm"),
            P(("dp", "tm")),
            P(None, None, "dp", None),
            P(None, None, "dp"),
            P(None, None, "dp", None),
            P(None, "dp", "tm"),
            P(None, "dp", None),
            P("dp", "tm"),
            P(("dp", "tm"), None),
        ),
        out_specs=(
            P("dp", "tm"),
            P(("dp", "tm"), None),
            P("dp", "tm"),
            P(None, None, "dp", None),
            P(None, None, "dp"),
            P(None, None, "dp", None),
            P(None, "dp", "tm"),
            P(None, "dp", None),
        ),
        check_vma=False,
    )
```

```python
import functools
import types

import jax
import jax.numpy as jnp
from jax import lax
from jax.experimental import pallas as pl
from jax.experimental.pallas import tpu as pltpu
from jax.sharding import PartitionSpec as P

HOR_Y = 6
HOR_Q = 8
HOR_M = 18
LAYERS = 4
LANES = 128
HALF = 32
GROUPS = 8
FRONT = 2 * HALF + 16
BACK = 4 * HALF
BASIS = 2 * HALF
HOPS = {
    "a0": (4, 2, 1),
    "b0": (4, 2, 1),
    "a1": (4, 2, 1),
    "b1": (4, 2, 1),
    "c": (4, 2, 1),
    "m1": (4, 1, 2),
    "m3": (4, 1, 2),
    "m4": (4, 2, 1),
}


def slot_shares(hops):
    return tuple(sum(bit for i, bit in enumerate(hops) if s >> i & 1) for s in range(GROUPS))


TILE = 512
CHUNK = 256

f32 = jnp.float32
bf16 = jnp.bfloat16
MIB = 1024 * 1024
FLOPS_PER_US = 150_000_000


def mm(a, b):
    return jnp.dot(a, b, preferred_element_type=f32)


def mm_nt(a, b):
    return lax.dot_general(a, b, (((1,), (1,)), ((), ())), preferred_element_type=f32)


def mm_tn(a, b):
    return lax.dot_general(a, b, (((0,), (0,)), ((), ())), preferred_element_type=f32)


def rows_at(start, size, align):
    return pl.ds(pl.multiple_of(start, align), size)


def in_group(labels, width):
    field = lax.broadcasted_iota(jnp.int32, (width, labels.shape[1]), 0)
    group = (
        (field >= HOR_Y).astype(jnp.int32)
        + (field >= HOR_Y + HOR_Q).astype(jnp.int32)
        + (field >= HOR_Y + HOR_Q + HOR_M).astype(jnp.int32)
    )
    return group == labels


def slot_rows(pos, q, s, hops):
    share = pos[0] ^ slot_shares(hops)[s]
    half = pos[1] ^ q
    row = share * (2 * HALF) + half * HALF
    block = share * 2 + half
    window_row = ((block // 4) ^ pos[2]) * LANES + (block % 4) * HALF
    return row, window_row


def slot_at(pos, share, hops):
    r = share ^ pos[0]
    place = {1: 0, 2: 1, 4: 2}
    return sum(((r >> place[bit]) & 1) << i for i, bit in enumerate(hops))


def size_of(shape):
    total = 1
    for extent in shape:
        total *= extent
    return total


class Inputs:
    def __init__(self, refs, copies):
        self.refs, self.copies = refs, copies

    def __getitem__(self, i):
        if isinstance(i, slice):
            return [self[j] for j in range(*i.indices(len(self.refs)))]
        if i in self.copies:
            self.copies.pop(i).wait()
        return self.refs[i]


class Line:
    def __init__(self, pos):
        self.pos, self.token, self.us = pos, None, None

    def batch(self, steps):
        shapes = [out for _, _, _, outs in steps for out in outs]
        args = [arg for _, _, arg_list, _ in steps for arg in arg_list]

        def body(pos, ins, outs, scratch):
            i = o = 0
            for _, run, arg_list, out_list in steps:
                run(pos, Inputs(ins.refs[i : i + len(arg_list)], {}), outs[o : o + len(out_list)], ())
                i, o = i + len(arg_list), o + len(out_list)

        name = "_and_".join(step[0] for step in steps)
        where = any(step[0] == "cut_basis" for step in steps)
        results = self.run(body, name, args, shapes, limit=6, where=where)
        split = []
        for _, _, _, out_list in steps:
            split.append(results[: len(out_list)])
            results = results[len(out_list) :]
        return split

    def run(self, body, name, args, outs, scratch=(), fetch=(), save=(), limit=12, after=(), us=0.5, stay=(), out_stays=False, where=True):
        token = [] if self.token is None else [self.token]
        extra = [*after, *token]
        fetch, save = list(fetch), list(save)
        n_in, n_out, n_extra = len(args), len(outs), len(extra)
        n_fetch, n_save = len(fetch), len(save)

        def kernel(*refs):
            refs = list(refs)
            pos_ref = self.pos() if where else None
            given, refs = refs[:n_in], refs[n_in + n_extra :]
            results, refs = refs[:n_out], refs[n_out:]
            saved, refs = refs[:n_save], refs[n_save:]
            if out_stays:
                refs.pop(0)[...] = jnp.zeros((8, LANES), f32)
            landing, refs = refs[:n_fetch], refs[n_fetch:]
            sems = refs.pop() if n_fetch + n_save else None
            inputs, copies, leaving = list(given), {}, []
            for at, (i, buf) in enumerate(zip(fetch, landing)):
                copies[i] = pltpu.make_async_copy(given[i], buf, sems.at[at])
                copies[i].start()
                inputs[i] = buf
            for at, (i, dst) in enumerate(zip(save, saved)):
                leaving.append(pltpu.make_async_copy(given[i], dst, sems.at[n_fetch + at]))
                leaving[-1].start()
            body(pos_ref, Inputs(inputs, copies), results, refs)
            for copy in (*copies.values(), *leaving):
                copy.wait()

        vmem, hbm = pl.BlockSpec(memory_space=pltpu.VMEM), pl.BlockSpec(memory_space=pltpu.HBM)
        anywhere = pl.BlockSpec(memory_space=pl.ANY)
        place = pltpu.HBM if out_stays else jax.ShapeDtypeStruct
        shapes = [place(shape, dtype) for shape, dtype in outs]
        placed = [
            pltpu.with_memory_space_constraint(a, pltpu.HBM) if i in fetch or i in stay else a
            for i, a in enumerate(args)
        ]
        shapes += [pltpu.HBM(args[i].shape, args[i].dtype) for i in save]
        mark = [jax.ShapeDtypeStruct((8, LANES), f32)] if out_stays else []
        sems = [pltpu.SemaphoreType.DMA((n_fetch + n_save,))] if n_fetch + n_save else []
        results = list(pl.pallas_call(
            kernel,
            name=name,
            out_shape=shapes + mark,
            in_specs=[hbm if i in fetch or i in stay else vmem for i in range(n_in)]
            + [anywhere] * n_extra,
            out_specs=[hbm if out_stays else vmem] * n_out + [hbm] * n_save + [vmem] * len(mark),
            scratch_shapes=[pltpu.VMEM(args[i].shape, args[i].dtype) for i in fetch]
            + list(scratch)
            + sems,
            compiler_params=pltpu.CompilerParams(vmem_limit_bytes=limit * MIB),
            cost_estimate=pl.CostEstimate(
                flops=int((us if self.us is None else self.us) * FLOPS_PER_US),
                bytes_accessed=1,
                transcendentals=0,
            ),
        )(*placed, *extra))
        if out_stays:
            self.token = results.pop()
        else:
            self.token = min(results, key=lambda a: a.size * a.dtype.itemsize)
        return results


def swap(x, axis, bit, size):
    return lax.ppermute(x, axis, [(i, i ^ bit) for i in range(size)])


class Exchange:
    def __init__(self, line, pieces, n_tm):
        self.line, self.n_tm = line, n_tm
        self.own, near, far = pieces
        self.far = swap(far, "tm", 2, n_tm)
        self.near = swap(near, "tm", 1, n_tm)

    def relay(self):
        (across,) = yield "relay", relay_body, (self.far,), [(self.far.shape[1:], bf16)]
        self.across = swap(across, "tm", 1, self.n_tm)

    def pieces(self):
        return [self.own, self.near, self.far, self.across]


def relay_body(pos, ins, outs, scratch):
    outs[0][...] = ins[0][1]


def flat(refs):
    return [ref if len(ref.shape) == 2 else ref.at[0] for ref in refs]


def split_body(with_basis, pos, ins, outs, scratch):
    landing, sems = scratch[0:2]
    rows = landing.shape[1]
    copies = []
    for r in range(4):
        copies.append(pltpu.make_async_copy(ins[0].at[pos[2] ^ r], landing.at[r], sems.at[r]))
    if with_basis:
        basis = scratch[2]
        basis_copy = pltpu.make_async_copy(ins[1], basis, sems.at[4])
        basis_copy.start()
    for r in (2, 3, 1, 0):
        copies[r].start()
    if with_basis:
        basis_copy.wait()
        for k in range(2):
            at = slice(rows + 2 * HALF * k, rows + 2 * HALF * (k + 1))
            value = basis[k].astype(bf16)
            for out in (outs[1], outs[2].at[0], outs[2].at[1]):
                out[at, :] = value
    for r in (2, 3, 1, 0):
        copies[r].wait()
        out = outs[2].at[r - 2] if r >= 2 else outs[r]
        out[0:rows, :] = landing[r].astype(bf16)


def piece_shapes(rows, more=0):
    sent = rows + more
    return [((rows, LANES), bf16), ((sent, LANES), bf16), ((2, sent, LANES), bf16)]


def split_windows(line, array, parts, basis=None):
    shape = (parts, array.shape[0] // parts, LANES)
    args = (array.reshape(shape),) if basis is None else (array.reshape(shape), basis)
    return line.run(
        functools.partial(split_body, basis is not None),
        "split_windows",
        args,
        piece_shapes(shape[1], 0 if basis is None else 2 * basis.shape[1]),
        [pltpu.VMEM(shape, f32), pltpu.SemaphoreType.DMA((parts + 1,))]
        + [pltpu.VMEM(a.shape, f32) for a in args[1:]],
        stay=range(len(args)),
        limit=8,
        us=2.0,
    )


def merge_body(sign, pos, ins, outs, scratch):
    base, pieces = ins[0], flat(ins[1:5])
    leaving, sems = scratch
    parts = len(pieces)
    arrive, leave = [], []
    for r in range(parts):
        at = pos[2] ^ r
        leave.append(pltpu.make_async_copy(leaving.at[r], outs[0].at[at], sems.at[parts + r]))
    for r, piece in enumerate(pieces):
        value = piece[...].astype(f32)
        own = base[pos[2] ^ r]
        leaving[r] = own - value if sign < 0 else own + value
        leave[r].start()
    for copy in leave:
        copy.wait()


def merge_windows(line, base, pieces, sign):
    parts = len(pieces)
    shape = (parts, base.shape[0] // parts, LANES)
    out = line.run(
        functools.partial(merge_body, sign),
        "merge_windows",
        (base.reshape(shape), *pieces),
        [(shape, f32)],
        [pltpu.VMEM(shape, f32), pltpu.SemaphoreType.DMA((2 * parts,))],
        stay=(),
        out_stays=True,
        limit=12,
        us=3.5,
    )[0]
    return out.reshape(base.shape)


def activate(p):
    t = jnp.tanh(p)
    u = 1.0 + t
    h = p * u
    return h.astype(bf16), u + h * (1.0 - t)


def columns(refs, at):
    if len(refs) == 1:
        return refs[0][at, :]
    return jnp.concatenate([ref[at, :] for ref in refs], axis=1)


def put_pieces(refs, at, value):
    for r in range(4):
        ref = refs[2].at[r - 2] if r >= 2 else refs[r]
        ref[at, :] = value[:, r * LANES : (r + 1) * LANES]


def chunks(rows):
    return [slice(at, at + CHUNK) for at in range(0, rows, CHUNK)]


def front_body(n_x, hops, pos, ins, bufs, scratch):
    w1, w2, bias, basis, h1, d1, h2, d2 = bufs
    total = jnp.zeros((16, 2 * LANES), f32)
    for q in range(2):
        for s in range(GROUPS):
            ref, i = ins[2 * q + s // 4], s % 4
            row, window_row = slot_rows(pos, q, s, hops)
            w1[rows_at(window_row, HALF, HALF), :] = ref[i, 0:HALF, :] * 0.5
            w2[rows_at(row, HALF, HALF), :] = ref[i, HALF : 2 * HALF, :] * 0.5
            low = ref[i, 2 * HALF : FRONT, 0:LANES]
            high = ref[i, 2 * HALF : FRONT, LANES : 2 * LANES]
            basis[rows_at(row, 16, 16), :] = low
            basis[rows_at(row + 16, 16, 16), :] = high
            if q == 0:
                total += ref[i, 2 * HALF : FRONT, 2 * LANES :].astype(f32)
    bias[:, 0 : 2 * LANES] = total[0:8] * 0.5
    bias[:, 2 * LANES :] = total[8:16] * 0.5
    xs = flat(ins[4 : 4 + n_x])
    for at in chunks(h1.shape[0]):
        h, d = activate(mm(columns(xs, at), w1[...]) + bias[0:1, :])
        h1[at, :] = h
        d1[at, :] = d.astype(bf16)
    for at in chunks(h1.shape[0]):
        h, d = activate(mm(h1[at, :], w2[...]) + bias[1:2, :])
        h2[at, :] = h
        d2[at, :] = d.astype(bf16)


def front(line, k, slots, xs, rows, leaving=()):
    square = ((512, 512), bf16)
    hidden = ((rows, 512), bf16)
    args = (*slots, *xs, *leaving)
    return line.run(
        functools.partial(front_body, len(xs), HOPS["a" + str(k)]),
        "front",
        args,
        [square, square, ((8, 512), f32), ((512, LANES), bf16), hidden, hidden, hidden, hidden],
        save=range(len(args) - len(leaving), len(args)),
        limit=6,
        us=4.0,
    )


def rear_body(last, hops, pos, ins, bufs, scratch):
    w3, w4, wb, wf, h3, d3, h4, d4, bt, ft, fore_out = bufs
    for q in range(2):
        for s in range(GROUPS):
            ref, i = ins[2 * q + s // 4], s % 4
            row, _ = slot_rows(pos, q, s, hops)
            for m, w in enumerate((w3, w4, wb, wf)):
                part = ref[i, m * HALF : (m + 1) * HALF, :]
                w[rows_at(row, HALF, HALF), :] = part * 0.5 if m < 2 else part
    bias, h2, basis = ins[4], ins[5], ins[6]
    steps = chunks(h3.shape[0])
    for at in steps:
        h, d = activate(mm(h2[at, :], w3[...]) + bias[2:3, :])
        h3[at, :] = h
        d3[at, :] = d.astype(bf16)
    for at in steps:
        h, d = activate(mm(h3[at, :], w4[...]) + bias[3:4, :])
        h4[at, :] = h
        d4[at, :] = (0.5 * d).astype(bf16)
    for at in steps:
        bt[at, :] = mm(h4[at, :], wb[...]).astype(bf16)
    for at in steps:
        ft[at, :] = mm(h4[at, :], wf[...]).astype(bf16)
    width = fore_out.shape[0]
    for at in steps:
        fore = mm(ft[at, :], basis[...]).T[0:width, :]
        if last:
            fore = ins[7][:, at] + fore
            fore = jnp.where(in_group(ins[8][0:1, at], width), fore, 0.0)
        fore_out[:, at] = fore


def rear(line, slots, h2, bias, basis, extra, width, leaving=()):
    rows = h2.shape[0]
    square = ((512, 512), bf16)
    hidden = ((rows, 512), bf16)
    args = (*slots, bias, h2, basis, *extra, *leaving)
    return line.run(
        functools.partial(rear_body, bool(extra), HOPS["b1" if extra else "b0"]),
        "rear",
        args,
        [square] * 4 + [hidden] * 6 + [((width, rows), f32)],
        save=range(len(args) - len(leaving), len(args)),
        limit=6,
        us=6.5,
    )


def cast_body(k, pos, ins, bufs, scratch):
    wv = bufs[0]
    for q in range(2):
        for s in range(GROUPS):
            ref, i = ins[2 * q + s // 4], s % 4
            row, _ = slot_rows(pos, q, s, HOPS["c"])
            for r in range(4):
                part = ref[i, k * HALF : (k + 1) * HALF, r * LANES : (r + 1) * LANES]
                at = r ^ q
                wv[rows_at(row, HALF, HALF), at * LANES : (at + 1) * LANES] = part
    bt = ins[4]
    for at in chunks(bt.shape[0]):
        cast = mm(bt[at, :], wv[...])
        if k == 0:
            bufs[1][at, :] = (columns(flat(ins[5:9]), at).astype(f32) - cast).astype(bf16)
            bufs[2][at, :] = cast
        else:
            put_pieces(bufs[1:4], at, (cast + ins[5][at, :]).astype(bf16))


def backcast(line, k, slots, bt, extra, leaving=()):
    rows = bt.shape[0]
    hidden = (rows, 512)
    outs = [(hidden, bf16), (hidden, f32)] if k == 0 else piece_shapes(rows)
    return line.run(
        functools.partial(cast_body, k),
        "backcast",
        (*slots, bt, *extra, *leaving),
        [((512, 512), bf16)] + outs,
        save=range(5 + len(extra), 5 + len(extra) + len(leaving)),
        limit=6,
        us=1.5,
    )


def row_sum(value):
    return jnp.sum(value.astype(f32), axis=0, keepdims=True)


def pack_pair(packed, rows, lanes, slot, first, second, pos):
    keep, send = packed
    lower = pos[1] == 0
    first, second = first.astype(bf16), second.astype(bf16)
    keep[slot, rows, lanes] = jnp.where(lower, first, second)
    send[slot, rows, lanes] = jnp.where(lower, second, first)


def pack_rows(packed, at, value, pos, hops):
    for share in range(GROUPS):
        row = share * 2 * HALF
        pack_pair(
            packed,
            slice(at, at + HALF),
            slice(None),
            slot_at(pos, share, hops),
            value[row : row + HALF, :],
            value[row + HALF : row + 2 * HALF, :],
            pos,
        )


def chain_rear_body(n_g, pos, ins, outs, scratch):
    g, g_back, g_fore, g4, g3, bias = outs
    wv, basis, wb, wf, w4 = ins[n_g + 1 : n_g + 6]
    gs, fg = flat(ins[0:4]) + ins[4:n_g], ins[n_g]
    steps = chunks(g.shape[0])
    for at in steps:
        value = columns(gs[:4], at)
        if n_g == 5:
            value = (value.astype(f32) + gs[4][at, :].astype(f32)).astype(bf16)
        g[at, :] = -value
        g_back[at, :] = mm_nt(g[at, :], wv[...]).astype(bf16)
    for at in steps:
        g_fore[at, :] = mm_nt(fg[:, at].T, basis[...]).astype(bf16)
    d4 = ins[n_g + 6]
    b3 = b4 = jnp.zeros((1, 512), f32)
    for at in steps:
        gh = mm_nt(g_back[at, :], wb[...]) + mm_nt(g_fore[at, :], wf[...])
        value = (gh * d4[at, :].astype(f32)).astype(bf16)
        g4[at, :] = value
        b4 += row_sum(value)
    d3 = ins[n_g + 7]
    for at in steps:
        gh = mm_nt(g4[at, :], w4[...])
        value = (gh * d3[at, :].astype(f32)).astype(bf16)
        g3[at, :] = value
        b3 += row_sum(value)
    bias[...] = jnp.concatenate([b3, b4, jnp.zeros((6, 512), f32)], axis=0)


def chain_rear(line, gs, fg, weights, d4, d3, fetch):
    rows = fg.shape[1]
    n = len(gs) + 1 + len(weights)
    return line.run(
        functools.partial(chain_rear_body, len(gs)),
        "chain_rear",
        (*gs, fg, *weights, d4, d3),
        [((rows, 512), bf16)] * 5 + [((8, 512), f32)],
        fetch=(n, n + 1) if fetch else (),
        limit=10 if fetch else 6,
        where=False,
        us=7.0,
    )


def chain_front_body(last, pos, ins, outs, scratch):
    g2, g1, bias = outs[:3]
    g3, w3, w2, w1 = ins[0:4]
    steps = chunks(g1.shape[0])
    b1 = b2 = jnp.zeros((1, 512), f32)
    d2 = ins[4]
    for at in steps:
        gh = mm_nt(g3[at, :], w3[...])
        value = (gh * d2[at, :].astype(f32)).astype(bf16)
        g2[at, :] = value
        b2 += row_sum(value)
    d1 = ins[5]
    for at in steps:
        gh = mm_nt(g2[at, :], w2[...])
        value = (gh * d1[at, :].astype(f32)).astype(bf16)
        g1[at, :] = value
        b1 += row_sum(value)
    for at in steps:
        gh = (2.0 * mm_nt(g1[at, :], w1[...])).astype(bf16)
        if last:
            gh = (gh.astype(f32) + ins[6][at, :].astype(f32)).astype(bf16)
            put_pieces(outs[3:6], at, gh)
        else:
            outs[3][at, :] = gh
    bias[...] = jnp.concatenate([b1, b2, jnp.zeros((6, 512), f32)], axis=0)


def chain_front(line, g3, weights, d2, d1, gh2, fetch):
    rows = g3.shape[0]
    last = gh2 is not None
    outs = piece_shapes(rows) if last else [((rows, 512), bf16)]
    return line.run(
        functools.partial(chain_front_body, last),
        "chain_front",
        (g3, *weights, d2, d1, *([gh2] if last else [])),
        [((rows, 512), bf16)] * 2 + [((8, 512), f32)] + outs,
        fetch=(4, 5) if fetch else (),
        limit=10 if fetch else 6,
        where=False,
        us=4.5,
    )


def message_rows(k):
    first = {"B": 0, "F": HALF, "V": 2 * HALF, "U": 3 * HALF}
    second = {"L2": 0, "L1": HALF, "bias": 2 * HALF}
    sizes = [3 * HALF + 16, 2 * HALF + 16]
    at = 1 if k else 0
    for name in ("L4", "L3"):
        (first, second)[at][name] = sizes[at]
        sizes[at] += HALF
    return first, second, sizes


def whole_rows(ref):
    return slice(0, ref.shape[0])


def terms_rear_body(k, pos, ins, outs, scratch):
    packed, second = outs[0:2], outs[2:4]
    at, _, _ = message_rows(k)
    hops = HOPS["m1" if k else "m3"]
    g, g_back, g_fore, fg = ins[0:4]
    bt = ins[4]
    value = mm_tn(bt[...], g[...])
    for share in range(GROUPS):
        slot = slot_at(pos, share, hops)
        for r in range(4):
            for j in range(2):
                row, lane = (2 * share + j) * HALF, (2 * j + r // 2) * LANES
                part = value[row : row + HALF, r * LANES : (r + 1) * LANES].astype(bf16)
                packed[r % 2][slot, at["V"] : at["V"] + HALF, lane : lane + LANES] = part
    h4 = ins[5]
    pack_rows(packed, at["B"], mm_tn(h4[...], g_back[...]), pos, hops)
    pack_rows(packed, at["F"], mm_tn(h4[...], g_fore[...]), pos, hops)
    ft = ins[6]
    value = mm(fg[...], ft[...]).T
    rows = slice(at["U"], at["U"] + 16)
    for share in range(GROUPS):
        row, slot = share * 2 * HALF, slot_at(pos, share, hops)
        for j in range(2):
            lanes = slice(j * LANES, (j + 1) * LANES)
            low = value[row + 16 * j : row + 16 * (j + 1), :]
            high = value[row + HALF + 16 * j : row + HALF + 16 * (j + 1), :]
            pack_pair(packed, rows, lanes, slot, low, high, pos)
        for out in packed:
            out[slot, rows, 2 * LANES :] = jnp.zeros((16, 2 * LANES), bf16)
    if "L4" in at:
        h3, h2, g4, g3 = ins[7], ins[8], ins[9], ins[10]
        pack_rows(second, 0, mm_tn(h3[...], g4[...]), pos, hops)
        pack_rows(second, HALF, mm_tn(h2[...], g3[...]), pos, hops)


def terms_rear(line, k, grads, hidden, more, fetch):
    args = (*grads, *hidden, *more)
    heights = (3 * HALF + 16, 2 * HALF)
    outs = [((GROUPS, height, 512), bf16) for height in heights[: 2 if more else 1] for _ in range(2)]
    return line.run(
        functools.partial(terms_rear_body, k),
        "terms_rear",
        args,
        outs,
        fetch=[i for i in range(4, min(9, len(args)))] if fetch else (),
        limit=16 if fetch else 6,
        us=4.5 if k else 8.0,
    )


def terms_front_body(k, n_x, pos, ins, packed, scratch):
    _, at, _ = message_rows(k)
    hops = HOPS["m1" if k else "m4"]
    g2, g1, low_bias, high_bias = ins[0:4]
    bias = jnp.concatenate([low_bias[0:2, :], high_bias[0:2, :], jnp.zeros((4, 512), f32)], axis=0)
    bias = jnp.concatenate([bias[:, 0 : 2 * LANES], bias[:, 2 * LANES :]], axis=0).astype(bf16)
    rows = slice(at["bias"], at["bias"] + 16)
    for s in range(GROUPS):
        for out in packed:
            out[s, rows, 0 : 2 * LANES] = jnp.zeros((16, 2 * LANES), bf16)
            out[s, rows, 2 * LANES :] = bias
    xs = flat(ins[4 : 4 + n_x])
    value = mm_tn(columns(xs, whole_rows(g1)), g1[...])
    for r in range(4):
        for i in range(2):
            row = r * LANES + i * 2 * HALF
            pack_pair(
                packed,
                slice(at["L1"], at["L1"] + HALF),
                slice(None),
                slot_at(pos, (pos[2] ^ r) * 2 + i, hops),
                value[row : row + HALF, :],
                value[row + HALF : row + 2 * HALF, :],
                pos,
            )
    h1 = ins[4 + n_x]
    pack_rows(packed, at["L2"], mm_tn(h1[...], g2[...]), pos, hops)
    if "L4" in at:
        h3, h2, g4, g3 = ins[5 + n_x : 9 + n_x]
        pack_rows(packed, at["L4"], mm_tn(h3[...], g4[...]), pos, hops)
        pack_rows(packed, at["L3"], mm_tn(h2[...], g3[...]), pos, hops)


def terms_front(line, k, grads, xs, h1, more, fetch):
    args = (*grads, *xs, h1, *more)
    out = ((GROUPS, message_rows(k)[2][1], 512), bf16)
    return line.run(
        functools.partial(terms_front_body, k, len(xs)),
        "terms_front",
        args,
        [out, out],
        fetch=(4 + len(xs),) if fetch else (),
        limit=8,
        us=5.5 if k else 3.0,
    )


def pack_misc(basis, offsets):
    lead = basis.shape[:-2]
    offsets = jnp.concatenate([offsets, jnp.zeros_like(offsets)], axis=-2)
    return jnp.concatenate(
        [
            basis[..., 0:16, :],
            basis[..., 16:32, :],
            jnp.concatenate([offsets[..., 0 : 2 * LANES], offsets[..., 2 * LANES :]], axis=-2),
        ],
        axis=-1,
    ).reshape(*lead, 16, 512)


def select_body(pos, ins, outs, scratch):
    labels, adjoint = ins[0], ins[1]
    width = adjoint.shape[0]
    for at in chunks(adjoint.shape[1]):
        value = jnp.where(in_group(labels[0:1, at], width), adjoint[:, at], 0.0)
        outs[0][0:width, at] = value.astype(bf16)
    outs[0][width:, :] = jnp.zeros((LANES - width, adjoint.shape[1]), bf16)


def cut_body(pos, ins, outs, scratch):
    kernels, projection, basis, offsets = ins[0:4]
    rows_in, pair_in, basis_in, offsets_in, sems = scratch
    offsets_copy = pltpu.make_async_copy(offsets, offsets_in, sems.at[0, 3])
    offsets_copy.start()
    half = rows_at(pos[1] * HALF, HALF, HALF)
    copies = []
    for k in range(2):
        copies += [
            pltpu.make_async_copy(kernels.at[k, :, half, :], rows_in.at[k], sems.at[k, 0]),
            pltpu.make_async_copy(basis.at[k, half, :], basis_in.at[k], sems.at[k, 1]),
            pltpu.make_async_copy(projection.at[k, :, half, :], pair_in.at[k], sems.at[k, 2]),
        ]
    for copy in copies:
        copy.start()
    rows, width = slice(2 * HALF, FRONT), basis.shape[2]
    offsets_copy.wait()
    for k in range(2):
        front, back = outs[2 * k : 2 * k + 2]
        front[0, rows, :] = jnp.zeros((16, 512), bf16)
        own = jnp.concatenate([offsets_in[k], jnp.zeros_like(offsets_in[k])], axis=0)
        own = jnp.concatenate([jnp.where(pos[0] % 4 == i, own, 0.0) for i in range(4)], axis=1)
        own = jnp.concatenate([jnp.where(pos[0] // 4 == i, own, 0.0) for i in range(2)], axis=0)
        front[0, rows, 2 * LANES :] = own.astype(bf16)
    for copy in copies:
        copy.wait()
    for k in range(2):
        front, back = outs[2 * k : 2 * k + 2]
        for j in range(2):
            part = basis_in[k, 16 * j : 16 * (j + 1), :]
            front[0, rows, j * LANES : j * LANES + width] = part.astype(bf16)
        for i in range(2):
            at = slice(i * HALF, (i + 1) * HALF)
            front[0, at, :] = rows_in[k, i].astype(bf16)
            back[0, at, :] = rows_in[k, 2 + i].astype(bf16)
            back[0, (2 + i) * HALF : (3 + i) * HALF, :] = pair_in[k, i].astype(bf16)


def cut_basis_body(pos, ins, outs, scratch):
    own, near, far, across = ins[0:4]
    first = near.shape[0] - 4 * HALF
    for k in range(2):
        at = first + 2 * HALF * k + pos[1] * HALF
        parts = [own[k, rows_at(pos[1] * HALF, HALF, HALF), :].astype(bf16)]
        parts += [ref[rows_at(at, HALF, HALF), :] for ref in (near, far.at[0], across)]
        outs[0][0, k * HALF : (k + 1) * HALF, :] = jnp.concatenate(parts, axis=1)


def join_body(pos, ins, outs, scratch):
    at = 0
    for ref in ins[0 : len(ins.refs)]:
        outs[0][at : at + ref.shape[0]] = ref[...]
        at += ref.shape[0]


def join(*parts):
    count = sum(part.shape[0] for part in parts)
    return "join", join_body, parts, [((count, *parts[0].shape[1:]), bf16)]


def fold_body(n, pos, ins, outs, scratch):
    at = 0
    for kept, arrived in zip(ins[0 : len(ins.refs) : 2], ins[1 : len(ins.refs) : 2]):
        rows = slice(at, at + kept.shape[1])
        at += kept.shape[1]
        for s in range(2 * n):
            total = kept[s].astype(f32) + arrived[s].astype(f32)
            if s < n:
                outs[0][s, rows, :] = total
            else:
                outs[1][s - n, rows, :] = total.astype(bf16)


def fold(*terms):
    n = terms[0].shape[0] // 2
    shape = (n, sum(term.shape[1] for term in terms[::2]), terms[0].shape[2])
    return "fold", functools.partial(fold_body, n), terms, [(shape, f32), (shape, bf16)]


def settle_body(pos, ins, outs, scratch):
    outs[0][...] = (ins[0][0] + ins[1][0].astype(f32)).astype(bf16)


def settle(kept, arrived):
    return "settle", settle_body, (kept, arrived), [(kept.shape[1:], bf16)]


def finish_body(width, pos, ins, outs, scratch):
    kernels, bias_out, projection, history_basis, forecast_basis = outs
    lower = pos[1] == 0
    for k in range(2):
        first, second, sizes = message_rows(k)
        places = {}
        for m, rows in enumerate((first, second)):
            one = 0 if k else 4 * m
            own, core, far, across = ins[8 * k + one : 8 * k + one + 4]
            for name, at in rows.items():
                places[name] = (own, core, far, across, at + (sizes[0] if k and m else 0))

        def both(name, height):
            own, core, far, across, at = places[name]
            rows = slice(at, at + height)
            mine = own[rows, :].astype(f32) + far[rows, :].astype(f32)
            other = core[rows, :].astype(f32) + across[rows, :].astype(f32)
            return jnp.where(lower, mine, other), jnp.where(lower, other, mine), mine

        targets = [("B", projection, 0), ("F", projection, 1)]
        targets += [("L" + str(layer + 1), kernels, layer) for layer in range(LAYERS)]
        for name, out, index in targets:
            a, b, _ = both(name, HALF)
            out[k, index, 0:HALF, :] = a
            out[k, index, HALF : 2 * HALF, :] = b
        own, _, far, _, at = places["V"]
        for j in range(2):
            lanes = slice(2 * j * LANES, (2 * j + 1) * LANES)
            theirs = slice((2 * j + 1) * LANES, (2 * j + 2) * LANES)
            rows = slice(at, at + HALF)
            total = own[rows, lanes].astype(f32) + far[rows, theirs].astype(f32)
            history_basis[k, j * HALF : (j + 1) * HALF, :] = total
        a, b, _ = both("U", 16)
        for j, value in enumerate((a, b)):
            for i in range(2):
                row = j * HALF + i * 16
                part = value[:, i * LANES : i * LANES + width]
                forecast_basis[k, row : row + 16, :] = part
        _, _, mine = both("bias", 16)
        total = jnp.zeros(bias_out.shape[1:], f32)
        for share in range(GROUPS):
            row, lane = 8 * (share // 4), 2 * LANES + (share % 4) * 2 * HALF
            part = mine[row : row + LAYERS, lane : lane + 2 * HALF]
            total = total + jnp.where(pos[0] == share, part, 0.0)
        bias_out[k] = total


def finish(line, sums, width):
    share = 2 * HALF
    return line.run(
        functools.partial(finish_body, width),
        "finish",
        sums,
        [
            ((2, LAYERS, share, 512), f32),
            ((2, LAYERS, share), f32),
            ((2, 2, share, 512), f32),
            ((2, share, LANES), f32),
            ((2, share, width), f32),
        ],
        limit=8,
    )


def slots_of(x, hops):
    x = x.reshape(GROUPS, 2, HALF, x.shape[-1]).swapaxes(0, 1)
    return x[:, jnp.array(slot_shares(hops))]


def in_order(x, hops):
    shares = slot_shares(hops)
    return x[:, jnp.array([shares.index(share) for share in range(GROUPS)])]


def flat_rows(x):
    return x.swapaxes(0, 1).reshape(2 * GROUPS * HALF, x.shape[-1])


def four(x):
    return x[0, 0:4], x[0, 4:8], x[1, 0:4], x[1, 4:8]


def shares_plain(kernels, offsets, projection, history_basis, forecast_basis, n_tm):
    tm = lax.axis_index("tm")

    def gather(x, axis, over="dp"):
        return lax.all_gather(x.astype(bf16), over, axis=axis, tiled=True)

    order = [jnp.bitwise_xor(tm, r) for r in range(n_tm)]
    out, bases = [], []
    for k in range(kernels.shape[0]):
        w = gather(kernels[k], 1)
        b = gather(offsets[k], 1)
        p = gather(projection[k], 1)
        u = gather(forecast_basis[k], 0)
        u = jnp.pad(u, ((0, 0), (0, LANES - u.shape[-1])))
        v = gather(gather(history_basis[k], 0), 1, "tm")
        v = jnp.concatenate(
            [lax.dynamic_slice_in_dim(v, at * LANES, LANES, 1) for at in order], axis=1
        )
        v = slots_of(v, HOPS["c"])
        other = [v[1, ..., (r ^ 1) * LANES : ((r ^ 1) + 1) * LANES] for r in range(4)]
        v = jnp.stack([v[0], jnp.concatenate(other, axis=-1)])
        offs = jnp.zeros((2, GROUPS, LAYERS, 512), bf16).at[0, 0].set(b)
        front_hops, back_hops = HOPS["a" + str(k)], HOPS["b" + str(k)]
        misc = pack_misc(slots_of(u, front_hops), offs)
        first = [slots_of(x, front_hops) for x in (w[0], w[1])] + [misc]
        first = jnp.concatenate(first, axis=2)
        second = jnp.concatenate([slots_of(x, back_hops) for x in (w[2], w[3], p[0], p[1])], axis=2)
        out.append((four(first), four(second)))
        bases.append(v)
    return out, four(jnp.concatenate(bases, axis=2))


def gradients_plain(records, n_tm, width):
    def reduce(x, axis):
        return lax.psum_scatter(
            lax.psum(x.astype(bf16), "tm").astype(f32), "dp", scatter_dimension=axis, tiled=True
        )

    results = [[], [], [], [], []]
    for k, messages in enumerate(records):
        pieces = {}
        for m, message in enumerate(messages):
            message = jnp.stack(message)
            hops = HOPS["m1" if k else ("m3", "m4")[m]]
            for name, at in message_rows(k)[m].items():
                height = 16 if name in ("U", "bias") else HALF
                pieces[name] = in_order(message[:, :, at : at + height, :], hops)
        square = {name: flat_rows(pieces[name]) for name in ("L1", "L2", "L3", "L4", "B", "F")}
        results[0].append(reduce(jnp.stack([square["L" + str(i)] for i in range(1, 5)]), 1))
        bias = pieces["bias"][0, 0]
        bias = jnp.concatenate([bias[0:4, 2 * LANES :], bias[8:12, 2 * LANES :]], axis=1)
        results[1].append(reduce(bias, 1))
        results[2].append(reduce(jnp.stack([square["B"], square["F"]]), 1))
        v = pieces["V"]
        v = jnp.concatenate([v[..., 0 : 2 * LANES], v[..., 2 * LANES :]], axis=2)
        v = v.reshape(2, 2 * GROUPS * HALF, 2, LANES)
        blocks = [v[r % 2, :, r // 2] for r in range(4)]
        total = blocks[0].astype(f32)
        for r in range(1, n_tm):
            total = total + swap(blocks[r], "tm", r, n_tm).astype(f32)
        results[3].append(lax.psum_scatter(total, "dp", scatter_dimension=0, tiled=True))
        u = pieces["U"]
        u = jnp.concatenate([u[..., 0:LANES], u[..., LANES : 2 * LANES]], axis=2)
        results[4].append(reduce(flat_rows(u), 0)[:, 0:width])
    return [jnp.stack(x) for x in results]


def body(
    n_dp,
    n_tm,
    history_series,
    frequency_labels,
    affine_kernels,
    affine_offsets,
    expansion_projection,
    history_dictionary,
    prediction_dictionary,
    remainder_adjoint,
    prediction_adjoint,
):
    fast = n_dp == GROUPS

    def pos():
        tm = lax.axis_index("tm")
        return (lax.axis_index("dp"), tm % 2, tm) if fast else (0, 0, tm)

    line = Line(pos)
    width = prediction_adjoint.shape[1]
    rows = frequency_labels.shape[0]
    labels = frequency_labels.reshape(1, rows)

    def hop(x, bit):
        return swap(x, "dp", bit, n_dp)

    def core(x):
        return swap(x, "tm", 1, n_tm)

    class Gather:
        def __init__(self, own, name):
            self.x, self.hops = own, list(HOPS[name])
            self.arriving = hop(own, self.hops.pop(0))

        def step(self):
            (self.x,) = yield join(self.x, self.arriving)
            self.arriving = hop(self.x, self.hops.pop(0))
            if not self.hops:
                self.low_core = core(self.x)

        def last(self):
            (high,) = yield join(self.arriving)
            self.slots = self.x, high, self.low_core, core(high)

    class Message:
        def __init__(self, name, *packed):
            self.packed, self.terms, self.hops = packed, [], list(HOPS[name])
            if fast:
                for kept, sent in packed:
                    self.terms += [kept, core(sent)]

        def fold(self):
            kept, out = yield fold(*self.terms)
            self.terms = [kept, hop(out, self.hops.pop())]

        def last(self):
            (own,) = yield settle(*self.terms)
            self.sums = [own] + [swap(own, "tm", r, n_tm) for r in (1, 2, 3)]

    v = types.SimpleNamespace()
    t = types.SimpleNamespace()

    def task(run):
        setattr(t, run.__name__, run)
        return run

    @task
    def cut():
        args = (affine_kernels, expansion_projection, prediction_dictionary, affine_offsets)
        scratch = [
            pltpu.VMEM((2, LAYERS, HALF, 512), f32),
            pltpu.VMEM((2, 2, HALF, 512), f32),
            pltpu.VMEM((2, HALF, width), f32),
            pltpu.VMEM(affine_offsets.shape, f32),
            pltpu.SemaphoreType.DMA((2, 4)),
        ]
        outs = [((1, FRONT, 512), bf16), ((1, BACK, 512), bf16)] * 2
        chunks = line.run(cut_body, "cut", args, outs, scratch, stay=(0, 1, 2, 3), limit=4)
        names = ("a0", "b0", "a1", "b1")
        v.a0, v.b0, v.a1, v.b1 = (Gather(x, name) for x, name in zip(chunks, names))

    @task
    def cut_c():
        args = (history_dictionary, *v.x.pieces()[1:])
        (own,) = yield "cut_basis", cut_basis_body, args, [((1, BASIS, 512), bf16)]
        v.c = Gather(own, "c")

    for name in ("a0", "b0", "a1", "b1", "c"):
        setattr(t, "step_" + name, lambda name=name: getattr(v, name).step())
        setattr(t, "last_" + name, lambda name=name: getattr(v, name).last())

    @task
    def split_x():
        pieces = split_windows(line, history_series, n_tm, history_dictionary if fast else None)
        v.x = Exchange(line, pieces, n_tm)

    @task
    def split_g():
        v.g = Exchange(line, split_windows(line, remainder_adjoint, n_tm), n_tm)

    @task
    def select():
        out = [((LANES, rows), bf16)]
        (v.fg,) = yield "select", select_body, (labels, prediction_adjoint.T), out

    for name in ("x", "g", "rem", "der"):
        setattr(t, "relay_" + name, lambda name=name: getattr(v, name).relay())

    @task
    def merge_rem():
        pieces = v.rem.pieces()
        v.remainder = merge_windows(line, history_series, pieces, -1)

    @task
    def merge_der():
        pieces = v.der.pieces()
        v.derivative = merge_windows(line, remainder_adjoint, pieces, 1)

    @task
    def front_0():
        outs = front(line, 0, v.a0.slots, v.x.pieces(), rows)
        v.w1a, v.w2a, v.bias, v.basis_a, *v.h12 = outs

    @task
    def rear_0():
        args = (v.b0.slots, v.h12[2], v.bias, v.basis_a, ())
        outs = rear(line, *args, width)
        v.w3a, v.w4a, v.wba, v.wfa = outs[:4]
        v.act, v.fore = outs[4:10], outs[10]
        v.h1a, v.d1a, v.h2a, v.d2a = v.h12

    @task
    def cast_0():
        outs = backcast(line, 0, v.c.slots, v.act[4], v.x.pieces(), v.act[0:2])
        v.wva, v.x2, v.cast, v.h3a, v.d3a = outs

    @task
    def front_1():
        outs = front(line, 1, v.a1.slots, [v.x2], rows, v.act[2:5])
        v.w1b, v.w2b, v.bias, v.basis_b, v.h1, v.d1, v.h2, v.d2 = outs[:8]
        v.h4a, v.d4a, v.bta = outs[8:]

    @task
    def rear_1():
        args = (v.b1.slots, v.h2, v.bias, v.basis_b, (v.fore, labels))
        outs = rear(line, *args, width, v.act[5:6])
        v.w3b, v.w4b, v.wbb, v.wfb = outs[:4]
        v.h3, v.d3, v.h4, v.d4, v.bt, v.ft, v.fore, v.fta = outs[4:]

    @task
    def cast_1():
        outs = backcast(line, 1, v.c.slots, v.bt, [v.cast])
        v.wvb, v.rem = outs[0], Exchange(line, outs[1:], n_tm)

    @task
    def chain_rear_1():
        weights = (v.wvb, v.basis_b, v.wbb, v.wfb, v.w4b)
        v.cr = chain_rear(line, v.g.pieces(), v.fg, weights, v.d4, v.d3, False)

    @task
    def terms_rear_1():
        args = ((*v.cr[0:3], v.fg), (v.bt, v.h4, v.ft), ())
        v.t1 = terms_rear(line, 1, *args, False)

    @task
    def chain_front_1():
        weights = (v.w3b, v.w2b, v.w1b)
        outs = chain_front(line, v.cr[4], weights, v.d2, v.d1, None, False)
        v.cf, v.gh2 = outs[0:3], outs[3]

    @task
    def terms_front_1():
        more = (v.h3, v.h2, v.cr[3], v.cr[4])
        args = ((*v.cf, v.cr[5]), [v.x2], v.h1, more)
        v.t2 = terms_front(line, 1, *args, False)
        v.m1 = Message("m1", v.t1, v.t2)

    @task
    def chain_rear_0():
        weights = (v.wva, v.basis_a, v.wba, v.wfa, v.w4a)
        gs = [*v.g.pieces(), v.gh2]
        v.cr = chain_rear(line, gs, v.fg, weights, v.d4a, v.d3a, False)

    @task
    def terms_rear_0():
        more = (v.h3a, v.h2a, v.cr[3], v.cr[4])
        args = ((*v.cr[0:3], v.fg), (v.bta, v.h4a, v.fta), more)
        outs = terms_rear(line, 0, *args, False)
        v.m3 = Message("m3", outs[0:2], outs[2:4])

    @task
    def chain_front_0():
        weights = (v.w3a, v.w2a, v.w1a)
        outs = chain_front(line, v.cr[4], weights, v.d2a, v.d1a, v.gh2, False)
        v.cf, v.der = outs[0:3], Exchange(line, outs[3:6], n_tm)

    @task
    def terms_front_0():
        args = ((*v.cf, v.cr[5]), v.x.pieces(), v.h1a, ())
        v.m4 = Message("m4", terms_front(line, 0, *args, False))

    for name in ("m1", "m3", "m4"):
        setattr(t, "fold_" + name, lambda name=name: getattr(v, name).fold())
        setattr(t, "settle_" + name, lambda name=name: getattr(v, name).last())

    if not fast:
        masters = (
            affine_kernels,
            affine_offsets,
            expansion_projection,
            history_dictionary,
            prediction_dictionary,
        )
        blocks, bases = shares_plain(*masters, n_tm)
        v.a0, v.b0, v.a1, v.b1, v.c = (Gather.__new__(Gather) for _ in range(5))
        v.a0.slots, v.b0.slots = blocks[0]
        v.a1.slots, v.b1.slots = blocks[1]
        v.c.slots = bases
        for name in vars(t):
            if name.startswith(("cut", "step", "last", "fold", "settle")):
                setattr(t, name, lambda: None)
    for us, *runs in order(t):
        line.us = us
        steps = [step for step in [run() for run in runs] if step is not None]
        if steps:
            for step, result in zip(steps, line.batch([next(step) for step in steps])):
                try:
                    step.send(result)
                except StopIteration:
                    pass
    if fast:
        sums = (*v.m3.sums, *v.m4.sums, *v.m1.sums)
        grads = finish(line, sums, width)
    else:
        m3 = [jnp.concatenate(pair, axis=1) for pair in zip(*v.m3.packed)]
        records = [(m3, v.m4.packed[0]), v.m1.packed]
        grads = gradients_plain(records, n_tm, width)
    return (v.remainder, v.fore.T, v.derivative, *grads)


def order(t):
    return (
        (0, t.split_x),
        (None, t.cut),
        (None, t.step_a0),
        (3, t.step_b0),
        (3, t.step_a0),
        (None, t.step_a1),
        (None, t.last_a0),
        (None, t.relay_x),
        (0.2, t.step_b0),
        (0.2, t.cut_c),
        (None, t.front_0),
        (None, t.step_a1, t.step_c),
        (0.2, t.step_c),
        (20, t.last_b0),
        (None, t.split_g),
        (8, t.step_b1),
        (20, t.last_a1),
        (None, t.rear_0),
        (None, t.step_b1),
        (3, t.last_c),
        (1, t.cast_0),
        (8, t.select),
        (None, t.front_1),
        (None, t.last_b1),
        (None, t.relay_g),
        (1, t.rear_1),
        (None, t.cast_1),
        (1, t.chain_rear_1),
        (8, t.terms_rear_1),
        (20, t.chain_front_1),
        (0, t.terms_front_1),
        (None, t.fold_m1),
        (None, t.chain_rear_0),
        (None, t.terms_rear_0),
        (20, t.chain_front_0),
        (1, t.relay_rem),
        (None, t.fold_m3),
        (None, t.fold_m1),
        (20, t.terms_front_0),
        (None, t.merge_rem),
        (1, t.fold_m4),
        (0.2, t.fold_m3),
        (20, t.fold_m1),
        (None, t.fold_m4),
        (20, t.settle_m1, t.fold_m3, t.relay_der),
        (None, t.merge_der),
        (None, t.settle_m3, t.fold_m4),
        (0.2, t.settle_m4),
    )


def solution(mesh):
    return jax.shard_map(
        functools.partial(body, mesh.shape["dp"], mesh.shape["tm"]),
        mesh=mesh,
        in_specs=(
            P("dp", "tm"),
            P(("dp", "tm")),
            P(None, None, "dp", None),
            P(None, None, "dp"),
            P(None, None, "dp", None),
            P(None, "dp", "tm"),
            P(None, "dp", None),
            P("dp", "tm"),
            P(("dp", "tm"), None),
        ),
        out_specs=(
            P("dp", "tm"),
            P(("dp", "tm"), None),
            P("dp", "tm"),
            P(None, None, "dp", None),
            P(None, None, "dp"),
            P(None, None, "dp", None),
            P(None, "dp", "tm"),
            P(None, "dp", None),
        ),
        check_vma=False,
    )
```

```python
import functools
import types

import jax
import jax.numpy as jnp
from jax import lax
from jax.experimental import pallas as pl
from jax.experimental.pallas import tpu as pltpu
from jax.sharding import PartitionSpec as P

HOR_Y = 6
HOR_Q = 8
HOR_M = 18
LAYERS = 4
LANES = 128
HALF = 32
GROUPS = 8
FRONT = 2 * HALF + 16
BACK = 4 * HALF
BASIS = 2 * HALF
HOPS = {
    "a0": (4, 2, 1),
    "b0": (4, 2, 1),
    "a1": (4, 2, 1),
    "b1": (4, 2, 1),
    "c": (4, 2, 1),
    "m1": (4, 1, 2),
    "m3": (4, 1, 2),
    "m4": (4, 2, 1),
}


def slot_shares(hops):
    return tuple(sum(bit for i, bit in enumerate(hops) if s >> i & 1) for s in range(GROUPS))


TILE = 512
CHUNK = 256

f32 = jnp.float32
bf16 = jnp.bfloat16
MIB = 1024 * 1024
FLOPS_PER_US = 150_000_000


def mm(a, b):
    return jnp.dot(a, b, preferred_element_type=f32)


def mm_nt(a, b):
    return lax.dot_general(a, b, (((1,), (1,)), ((), ())), preferred_element_type=f32)


def mm_tn(a, b):
    return lax.dot_general(a, b, (((0,), (0,)), ((), ())), preferred_element_type=f32)


def rows_at(start, size, align):
    return pl.ds(pl.multiple_of(start, align), size)


def in_group(labels, width):
    field = lax.broadcasted_iota(jnp.int32, (width, labels.shape[1]), 0)
    group = (
        (field >= HOR_Y).astype(jnp.int32)
        + (field >= HOR_Y + HOR_Q).astype(jnp.int32)
        + (field >= HOR_Y + HOR_Q + HOR_M).astype(jnp.int32)
    )
    return group == labels


def slot_rows(pos, q, s, hops):
    share = pos[0] ^ slot_shares(hops)[s]
    half = pos[1] ^ q
    row = share * (2 * HALF) + half * HALF
    block = share * 2 + half
    window_row = ((block // 4) ^ pos[2]) * LANES + (block % 4) * HALF
    return row, window_row


def slot_at(pos, share, hops):
    r = share ^ pos[0]
    place = {1: 0, 2: 1, 4: 2}
    return sum(((r >> place[bit]) & 1) << i for i, bit in enumerate(hops))


def size_of(shape):
    total = 1
    for extent in shape:
        total *= extent
    return total


class Inputs:
    def __init__(self, refs, copies):
        self.refs, self.copies = refs, copies

    def __getitem__(self, i):
        if isinstance(i, slice):
            return [self[j] for j in range(*i.indices(len(self.refs)))]
        if i in self.copies:
            self.copies.pop(i).wait()
        return self.refs[i]


class Line:
    def __init__(self, pos):
        self.pos, self.token, self.us = pos, None, None

    def batch(self, steps):
        shapes = [out for _, _, _, outs in steps for out in outs]
        args = [arg for _, _, arg_list, _ in steps for arg in arg_list]

        def body(pos, ins, outs, scratch):
            i = o = 0
            for _, run, arg_list, out_list in steps:
                run(pos, Inputs(ins.refs[i : i + len(arg_list)], {}), outs[o : o + len(out_list)], ())
                i, o = i + len(arg_list), o + len(out_list)

        name = "_and_".join(step[0] for step in steps)
        where = any(step[0] == "cut_basis" for step in steps)
        results = self.run(body, name, args, shapes, limit=6, where=where)
        split = []
        for _, _, _, out_list in steps:
            split.append(results[: len(out_list)])
            results = results[len(out_list) :]
        return split

    def run(self, body, name, args, outs, scratch=(), fetch=(), save=(), limit=12, after=(), us=0.5, stay=(), out_stays=False, where=True):
        token = [] if self.token is None else [self.token]
        extra = [*after, *token]
        fetch, save = list(fetch), list(save)
        n_in, n_out, n_extra = len(args), len(outs), len(extra)
        n_fetch, n_save = len(fetch), len(save)

        def kernel(*refs):
            refs = list(refs)
            pos_ref = self.pos() if where else None
            given, refs = refs[:n_in], refs[n_in + n_extra :]
            results, refs = refs[:n_out], refs[n_out:]
            saved, refs = refs[:n_save], refs[n_save:]
            if out_stays:
                refs.pop(0)[...] = jnp.zeros((8, LANES), f32)
            landing, refs = refs[:n_fetch], refs[n_fetch:]
            sems = refs.pop() if n_fetch + n_save else None
            inputs, copies, leaving = list(given), {}, []
            for at, (i, buf) in enumerate(zip(fetch, landing)):
                copies[i] = pltpu.make_async_copy(given[i], buf, sems.at[at])
                copies[i].start()
                inputs[i] = buf
            for at, (i, dst) in enumerate(zip(save, saved)):
                leaving.append(pltpu.make_async_copy(given[i], dst, sems.at[n_fetch + at]))
                leaving[-1].start()
            body(pos_ref, Inputs(inputs, copies), results, refs)
            for copy in (*copies.values(), *leaving):
                copy.wait()

        vmem, hbm = pl.BlockSpec(memory_space=pltpu.VMEM), pl.BlockSpec(memory_space=pltpu.HBM)
        anywhere = pl.BlockSpec(memory_space=pl.ANY)
        place = pltpu.HBM if out_stays else jax.ShapeDtypeStruct
        shapes = [place(shape, dtype) for shape, dtype in outs]
        placed = [
            pltpu.with_memory_space_constraint(a, pltpu.HBM) if i in fetch or i in stay else a
            for i, a in enumerate(args)
        ]
        shapes += [pltpu.HBM(args[i].shape, args[i].dtype) for i in save]
        mark = [jax.ShapeDtypeStruct((8, LANES), f32)] if out_stays else []
        sems = [pltpu.SemaphoreType.DMA((n_fetch + n_save,))] if n_fetch + n_save else []
        results = list(pl.pallas_call(
            kernel,
            name=name,
            out_shape=shapes + mark,
            in_specs=[hbm if i in fetch or i in stay else vmem for i in range(n_in)]
            + [anywhere] * n_extra,
            out_specs=[hbm if out_stays else vmem] * n_out + [hbm] * n_save + [vmem] * len(mark),
            scratch_shapes=[pltpu.VMEM(args[i].shape, args[i].dtype) for i in fetch]
            + list(scratch)
            + sems,
            compiler_params=pltpu.CompilerParams(vmem_limit_bytes=limit * MIB),
            cost_estimate=pl.CostEstimate(
                flops=int((us if self.us is None else self.us) * FLOPS_PER_US),
                bytes_accessed=1,
                transcendentals=0,
            ),
        )(*placed, *extra))
        if out_stays:
            self.token = results.pop()
        else:
            self.token = min(results, key=lambda a: a.size * a.dtype.itemsize)
        return results


def swap(x, axis, bit, size):
    return lax.ppermute(x, axis, [(i, i ^ bit) for i in range(size)])


class Exchange:
    def __init__(self, line, pieces, n_tm):
        self.line, self.n_tm = line, n_tm
        self.own, near, far = pieces
        self.far = swap(far, "tm", 2, n_tm)
        self.near = swap(near, "tm", 1, n_tm)

    def relay(self):
        (across,) = yield "relay", relay_body, (self.far,), [(self.far.shape[1:], bf16)]
        self.across = swap(across, "tm", 1, self.n_tm)

    def pieces(self):
        return [self.own, self.near, self.far, self.across]


def relay_body(pos, ins, outs, scratch):
    outs[0][...] = ins[0][1]


def flat(refs):
    return [ref if len(ref.shape) == 2 else ref.at[0] for ref in refs]


def split_body(with_basis, pos, ins, outs, scratch):
    landing, sems = scratch[0:2]
    rows = landing.shape[1]
    copies = []
    for r in range(4):
        copies.append(pltpu.make_async_copy(ins[0].at[pos[2] ^ r], landing.at[r], sems.at[r]))
    if with_basis:
        basis = scratch[2]
        basis_copy = pltpu.make_async_copy(ins[1], basis, sems.at[4])
        basis_copy.start()
    for r in (2, 3, 1, 0):
        copies[r].start()
    if with_basis:
        basis_copy.wait()
        for k in range(2):
            at = slice(rows + 2 * HALF * k, rows + 2 * HALF * (k + 1))
            value = basis[k].astype(bf16)
            for out in (outs[1], outs[2].at[0], outs[2].at[1]):
                out[at, :] = value
    for r in (2, 3, 1, 0):
        copies[r].wait()
        out = outs[2].at[r - 2] if r >= 2 else outs[r]
        out[0:rows, :] = landing[r].astype(bf16)


def piece_shapes(rows, more=0):
    sent = rows + more
    return [((rows, LANES), bf16), ((sent, LANES), bf16), ((2, sent, LANES), bf16)]


def split_windows(line, array, parts, basis=None):
    shape = (parts, array.shape[0] // parts, LANES)
    args = (array.reshape(shape),) if basis is None else (array.reshape(shape), basis)
    return line.run(
        functools.partial(split_body, basis is not None),
        "split_windows",
        args,
        piece_shapes(shape[1], 0 if basis is None else 2 * basis.shape[1]),
        [pltpu.VMEM(shape, f32), pltpu.SemaphoreType.DMA((parts + 1,))]
        + [pltpu.VMEM(a.shape, f32) for a in args[1:]],
        stay=range(len(args)),
        limit=8,
        us=2.0,
    )


def merge_body(sign, pos, ins, outs, scratch):
    base, pieces = ins[0], flat(ins[1:5])
    leaving, sems = scratch
    parts = len(pieces)
    arrive, leave = [], []
    for r in range(parts):
        at = pos[2] ^ r
        leave.append(pltpu.make_async_copy(leaving.at[r], outs[0].at[at], sems.at[parts + r]))
    for r, piece in enumerate(pieces):
        value = piece[...].astype(f32)
        own = base[pos[2] ^ r]
        leaving[r] = own - value if sign < 0 else own + value
        leave[r].start()
    for copy in leave:
        copy.wait()


def merge_windows(line, base, pieces, sign):
    parts = len(pieces)
    shape = (parts, base.shape[0] // parts, LANES)
    out = line.run(
        functools.partial(merge_body, sign),
        "merge_windows",
        (base.reshape(shape), *pieces),
        [(shape, f32)],
        [pltpu.VMEM(shape, f32), pltpu.SemaphoreType.DMA((2 * parts,))],
        stay=(),
        out_stays=True,
        limit=12,
        us=3.5,
    )[0]
    return out.reshape(base.shape)


def activate(p):
    t = jnp.tanh(p)
    u = 1.0 + t
    h = p * u
    return h.astype(bf16), u + h * (1.0 - t)


def columns(refs, at):
    if len(refs) == 1:
        return refs[0][at, :]
    return jnp.concatenate([ref[at, :] for ref in refs], axis=1)


def put_pieces(refs, at, value):
    for r in range(4):
        ref = refs[2].at[r - 2] if r >= 2 else refs[r]
        ref[at, :] = value[:, r * LANES : (r + 1) * LANES]


def chunks(rows):
    return [slice(at, at + CHUNK) for at in range(0, rows, CHUNK)]


def front_body(n_x, hops, pos, ins, bufs, scratch):
    w1, w2, bias, basis, h1, d1, h2, d2 = bufs
    total = jnp.zeros((16, 2 * LANES), f32)
    for q in range(2):
        for s in range(GROUPS):
            ref, i = ins[2 * q + s // 4], s % 4
            row, window_row = slot_rows(pos, q, s, hops)
            w1[rows_at(window_row, HALF, HALF), :] = ref[i, 0:HALF, :] * 0.5
            w2[rows_at(row, HALF, HALF), :] = ref[i, HALF : 2 * HALF, :] * 0.5
            low = ref[i, 2 * HALF : FRONT, 0:LANES]
            high = ref[i, 2 * HALF : FRONT, LANES : 2 * LANES]
            basis[rows_at(row, 16, 16), :] = low
            basis[rows_at(row + 16, 16, 16), :] = high
            if q == 0:
                total += ref[i, 2 * HALF : FRONT, 2 * LANES :].astype(f32)
    bias[:, 0 : 2 * LANES] = total[0:8] * 0.5
    bias[:, 2 * LANES :] = total[8:16] * 0.5
    xs = flat(ins[4 : 4 + n_x])
    for at in chunks(h1.shape[0]):
        h, d = activate(mm(columns(xs, at), w1[...]) + bias[0:1, :])
        h1[at, :] = h
        d1[at, :] = d.astype(bf16)
    for at in chunks(h1.shape[0]):
        h, d = activate(mm(h1[at, :], w2[...]) + bias[1:2, :])
        h2[at, :] = h
        d2[at, :] = d.astype(bf16)


def front(line, k, slots, xs, rows, leaving=()):
    square = ((512, 512), bf16)
    hidden = ((rows, 512), bf16)
    args = (*slots, *xs, *leaving)
    return line.run(
        functools.partial(front_body, len(xs), HOPS["a" + str(k)]),
        "front",
        args,
        [square, square, ((8, 512), f32), ((512, LANES), bf16), hidden, hidden, hidden, hidden],
        save=range(len(args) - len(leaving), len(args)),
        limit=6,
        us=4.0,
    )


def rear_body(last, hops, pos, ins, bufs, scratch):
    w3, w4, wb, wf, h3, d3, h4, d4, bt, ft, fore_out = bufs
    for q in range(2):
        for s in range(GROUPS):
            ref, i = ins[2 * q + s // 4], s % 4
            row, _ = slot_rows(pos, q, s, hops)
            for m, w in enumerate((w3, w4, wb, wf)):
                part = ref[i, m * HALF : (m + 1) * HALF, :]
                w[rows_at(row, HALF, HALF), :] = part * 0.5 if m < 2 else part
    bias, h2, basis = ins[4], ins[5], ins[6]
    steps = chunks(h3.shape[0])
    for at in steps:
        h, d = activate(mm(h2[at, :], w3[...]) + bias[2:3, :])
        h3[at, :] = h
        d3[at, :] = d.astype(bf16)
    for at in steps:
        h, d = activate(mm(h3[at, :], w4[...]) + bias[3:4, :])
        h4[at, :] = h
        d4[at, :] = (0.5 * d).astype(bf16)
    for at in steps:
        bt[at, :] = mm(h4[at, :], wb[...]).astype(bf16)
    for at in steps:
        ft[at, :] = mm(h4[at, :], wf[...]).astype(bf16)
    width = fore_out.shape[0]
    for at in steps:
        fore = mm(ft[at, :], basis[...]).T[0:width, :]
        if last:
            fore = ins[7][:, at] + fore
            fore = jnp.where(in_group(ins[8][0:1, at], width), fore, 0.0)
        fore_out[:, at] = fore


def rear(line, slots, h2, bias, basis, extra, width, leaving=()):
    rows = h2.shape[0]
    square = ((512, 512), bf16)
    hidden = ((rows, 512), bf16)
    args = (*slots, bias, h2, basis, *extra, *leaving)
    return line.run(
        functools.partial(rear_body, bool(extra), HOPS["b1" if extra else "b0"]),
        "rear",
        args,
        [square] * 4 + [hidden] * 6 + [((width, rows), f32)],
        save=range(len(args) - len(leaving), len(args)),
        limit=6,
        us=6.5,
    )


def cast_body(k, pos, ins, bufs, scratch):
    wv = bufs[0]
    for q in range(2):
        for s in range(GROUPS):
            ref, i = ins[2 * q + s // 4], s % 4
            row, _ = slot_rows(pos, q, s, HOPS["c"])
            for r in range(4):
                part = ref[i, k * HALF : (k + 1) * HALF, r * LANES : (r + 1) * LANES]
                at = r ^ q
                wv[rows_at(row, HALF, HALF), at * LANES : (at + 1) * LANES] = part
    bt = ins[4]
    for at in chunks(bt.shape[0]):
        cast = mm(bt[at, :], wv[...])
        if k == 0:
            bufs[1][at, :] = (columns(flat(ins[5:9]), at).astype(f32) - cast).astype(bf16)
            bufs[2][at, :] = cast
        else:
            put_pieces(bufs[1:4], at, (cast + ins[5][at, :]).astype(bf16))


def backcast(line, k, slots, bt, extra, leaving=()):
    rows = bt.shape[0]
    hidden = (rows, 512)
    outs = [(hidden, bf16), (hidden, f32)] if k == 0 else piece_shapes(rows)
    return line.run(
        functools.partial(cast_body, k),
        "backcast",
        (*slots, bt, *extra, *leaving),
        [((512, 512), bf16)] + outs,
        save=range(5 + len(extra), 5 + len(extra) + len(leaving)),
        limit=6,
        us=1.5,
    )


def row_sum(value):
    return jnp.sum(value.astype(f32), axis=0, keepdims=True)


def pack_pair(packed, rows, lanes, slot, first, second, pos):
    keep, send = packed
    lower = pos[1] == 0
    first, second = first.astype(bf16), second.astype(bf16)
    keep[slot, rows, lanes] = jnp.where(lower, first, second)
    send[slot, rows, lanes] = jnp.where(lower, second, first)


def pack_rows(packed, at, value, pos, hops):
    for share in range(GROUPS):
        row = share * 2 * HALF
        pack_pair(
            packed,
            slice(at, at + HALF),
            slice(None),
            slot_at(pos, share, hops),
            value[row : row + HALF, :],
            value[row + HALF : row + 2 * HALF, :],
            pos,
        )


def chain_rear_body(n_g, pos, ins, outs, scratch):
    g, g_back, g_fore, g4, g3, bias = outs
    wv, basis, wb, wf, w4 = ins[n_g + 1 : n_g + 6]
    gs, fg = flat(ins[0:4]) + ins[4:n_g], ins[n_g]
    steps = chunks(g.shape[0])
    for at in steps:
        value = columns(gs[:4], at)
        if n_g == 5:
            value = (value.astype(f32) + gs[4][at, :].astype(f32)).astype(bf16)
        g[at, :] = -value
        g_back[at, :] = mm_nt(g[at, :], wv[...]).astype(bf16)
    for at in steps:
        g_fore[at, :] = mm_nt(fg[:, at].T, basis[...]).astype(bf16)
    d4 = ins[n_g + 6]
    b3 = b4 = jnp.zeros((1, 512), f32)
    for at in steps:
        gh = mm_nt(g_back[at, :], wb[...]) + mm_nt(g_fore[at, :], wf[...])
        value = (gh * d4[at, :].astype(f32)).astype(bf16)
        g4[at, :] = value
        b4 += row_sum(value)
    d3 = ins[n_g + 7]
    for at in steps:
        gh = mm_nt(g4[at, :], w4[...])
        value = (gh * d3[at, :].astype(f32)).astype(bf16)
        g3[at, :] = value
        b3 += row_sum(value)
    bias[...] = jnp.concatenate([b3, b4, jnp.zeros((6, 512), f32)], axis=0)


def chain_rear(line, gs, fg, weights, d4, d3, fetch):
    rows = fg.shape[1]
    n = len(gs) + 1 + len(weights)
    return line.run(
        functools.partial(chain_rear_body, len(gs)),
        "chain_rear",
        (*gs, fg, *weights, d4, d3),
        [((rows, 512), bf16)] * 5 + [((8, 512), f32)],
        fetch=(n, n + 1) if fetch else (),
        limit=10 if fetch else 6,
        where=False,
        us=7.0,
    )


def chain_front_body(last, pos, ins, outs, scratch):
    g2, g1, bias = outs[:3]
    g3, w3, w2, w1 = ins[0:4]
    steps = chunks(g1.shape[0])
    b1 = b2 = jnp.zeros((1, 512), f32)
    d2 = ins[4]
    for at in steps:
        gh = mm_nt(g3[at, :], w3[...])
        value = (gh * d2[at, :].astype(f32)).astype(bf16)
        g2[at, :] = value
        b2 += row_sum(value)
    d1 = ins[5]
    for at in steps:
        gh = mm_nt(g2[at, :], w2[...])
        value = (gh * d1[at, :].astype(f32)).astype(bf16)
        g1[at, :] = value
        b1 += row_sum(value)
    for at in steps:
        gh = (2.0 * mm_nt(g1[at, :], w1[...])).astype(bf16)
        if last:
            gh = (gh.astype(f32) + ins[6][at, :].astype(f32)).astype(bf16)
            put_pieces(outs[3:6], at, gh)
        else:
            outs[3][at, :] = gh
    bias[...] = jnp.concatenate([b1, b2, jnp.zeros((6, 512), f32)], axis=0)


def chain_front(line, g3, weights, d2, d1, gh2, fetch):
    rows = g3.shape[0]
    last = gh2 is not None
    outs = piece_shapes(rows) if last else [((rows, 512), bf16)]
    return line.run(
        functools.partial(chain_front_body, last),
        "chain_front",
        (g3, *weights, d2, d1, *([gh2] if last else [])),
        [((rows, 512), bf16)] * 2 + [((8, 512), f32)] + outs,
        fetch=(4, 5) if fetch else (),
        limit=10 if fetch else 6,
        where=False,
        us=4.5,
    )


def message_rows(k):
    first = {"B": 0, "F": HALF, "V": 2 * HALF, "U": 3 * HALF}
    second = {"L2": 0, "L1": HALF, "bias": 2 * HALF}
    sizes = [3 * HALF + 16, 2 * HALF + 16]
    at = 1 if k else 0
    for name in ("L4", "L3"):
        (first, second)[at][name] = sizes[at]
        sizes[at] += HALF
    return first, second, sizes


def whole_rows(ref):
    return slice(0, ref.shape[0])


def terms_rear_body(k, pos, ins, outs, scratch):
    packed, second = outs[0:2], outs[2:4]
    at, _, _ = message_rows(k)
    hops = HOPS["m1" if k else "m3"]
    g, g_back, g_fore, fg = ins[0:4]
    bt = ins[4]
    value = mm_tn(bt[...], g[...])
    for share in range(GROUPS):
        slot = slot_at(pos, share, hops)
        for r in range(4):
            for j in range(2):
                row, lane = (2 * share + j) * HALF, (2 * j + r // 2) * LANES
                part = value[row : row + HALF, r * LANES : (r + 1) * LANES].astype(bf16)
                packed[r % 2][slot, at["V"] : at["V"] + HALF, lane : lane + LANES] = part
    h4 = ins[5]
    pack_rows(packed, at["B"], mm_tn(h4[...], g_back[...]), pos, hops)
    pack_rows(packed, at["F"], mm_tn(h4[...], g_fore[...]), pos, hops)
    ft = ins[6]
    value = mm(fg[...], ft[...]).T
    rows = slice(at["U"], at["U"] + 16)
    for share in range(GROUPS):
        row, slot = share * 2 * HALF, slot_at(pos, share, hops)
        for j in range(2):
            lanes = slice(j * LANES, (j + 1) * LANES)
            low = value[row + 16 * j : row + 16 * (j + 1), :]
            high = value[row + HALF + 16 * j : row + HALF + 16 * (j + 1), :]
            pack_pair(packed, rows, lanes, slot, low, high, pos)
        for out in packed:
            out[slot, rows, 2 * LANES :] = jnp.zeros((16, 2 * LANES), bf16)
    if "L4" in at:
        h3, h2, g4, g3 = ins[7], ins[8], ins[9], ins[10]
        pack_rows(second, 0, mm_tn(h3[...], g4[...]), pos, hops)
        pack_rows(second, HALF, mm_tn(h2[...], g3[...]), pos, hops)


def terms_rear(line, k, grads, hidden, more, fetch):
    args = (*grads, *hidden, *more)
    heights = (3 * HALF + 16, 2 * HALF)
    outs = [((GROUPS, height, 512), bf16) for height in heights[: 2 if more else 1] for _ in range(2)]
    return line.run(
        functools.partial(terms_rear_body, k),
        "terms_rear",
        args,
        outs,
        fetch=[i for i in range(4, min(9, len(args)))] if fetch else (),
        limit=16 if fetch else 6,
        us=4.5 if k else 8.0,
    )


def terms_front_body(k, n_x, pos, ins, packed, scratch):
    _, at, _ = message_rows(k)
    hops = HOPS["m1" if k else "m4"]
    g2, g1, low_bias, high_bias = ins[0:4]
    bias = jnp.concatenate([low_bias[0:2, :], high_bias[0:2, :], jnp.zeros((4, 512), f32)], axis=0)
    bias = jnp.concatenate([bias[:, 0 : 2 * LANES], bias[:, 2 * LANES :]], axis=0).astype(bf16)
    rows = slice(at["bias"], at["bias"] + 16)
    for s in range(GROUPS):
        for out in packed:
            out[s, rows, 0 : 2 * LANES] = jnp.zeros((16, 2 * LANES), bf16)
            out[s, rows, 2 * LANES :] = bias
    xs = flat(ins[4 : 4 + n_x])
    value = mm_tn(columns(xs, whole_rows(g1)), g1[...])
    for r in range(4):
        for i in range(2):
            row = r * LANES + i * 2 * HALF
            pack_pair(
                packed,
                slice(at["L1"], at["L1"] + HALF),
                slice(None),
                slot_at(pos, (pos[2] ^ r) * 2 + i, hops),
                value[row : row + HALF, :],
                value[row + HALF : row + 2 * HALF, :],
                pos,
            )
    h1 = ins[4 + n_x]
    pack_rows(packed, at["L2"], mm_tn(h1[...], g2[...]), pos, hops)
    if "L4" in at:
        h3, h2, g4, g3 = ins[5 + n_x : 9 + n_x]
        pack_rows(packed, at["L4"], mm_tn(h3[...], g4[...]), pos, hops)
        pack_rows(packed, at["L3"], mm_tn(h2[...], g3[...]), pos, hops)


def terms_front(line, k, grads, xs, h1, more, fetch):
    args = (*grads, *xs, h1, *more)
    out = ((GROUPS, message_rows(k)[2][1], 512), bf16)
    return line.run(
        functools.partial(terms_front_body, k, len(xs)),
        "terms_front",
        args,
        [out, out],
        fetch=(4 + len(xs),) if fetch else (),
        limit=8,
        us=5.5 if k else 3.0,
    )


def pack_misc(basis, offsets):
    lead = basis.shape[:-2]
    offsets = jnp.concatenate([offsets, jnp.zeros_like(offsets)], axis=-2)
    return jnp.concatenate(
        [
            basis[..., 0:16, :],
            basis[..., 16:32, :],
            jnp.concatenate([offsets[..., 0 : 2 * LANES], offsets[..., 2 * LANES :]], axis=-2),
        ],
        axis=-1,
    ).reshape(*lead, 16, 512)


def select_body(pos, ins, outs, scratch):
    labels, adjoint = ins[0], ins[1]
    width = adjoint.shape[0]
    for at in chunks(adjoint.shape[1]):
        value = jnp.where(in_group(labels[0:1, at], width), adjoint[:, at], 0.0)
        outs[0][0:width, at] = value.astype(bf16)
    outs[0][width:, :] = jnp.zeros((LANES - width, adjoint.shape[1]), bf16)


def cut_body(pos, ins, outs, scratch):
    kernels, projection, basis, offsets = ins[0:4]
    rows_in, pair_in, basis_in, offsets_in, sems = scratch
    offsets_copy = pltpu.make_async_copy(offsets, offsets_in, sems.at[0, 3])
    offsets_copy.start()
    half = rows_at(pos[1] * HALF, HALF, HALF)
    copies = []
    for k in range(2):
        copies += [
            pltpu.make_async_copy(kernels.at[k, :, half, :], rows_in.at[k], sems.at[k, 0]),
            pltpu.make_async_copy(basis.at[k, half, :], basis_in.at[k], sems.at[k, 1]),
            pltpu.make_async_copy(projection.at[k, :, half, :], pair_in.at[k], sems.at[k, 2]),
        ]
    for copy in copies:
        copy.start()
    rows, width = slice(2 * HALF, FRONT), basis.shape[2]
    offsets_copy.wait()
    for k in range(2):
        front, back = outs[2 * k : 2 * k + 2]
        front[0, rows, :] = jnp.zeros((16, 512), bf16)
        own = jnp.concatenate([offsets_in[k], jnp.zeros_like(offsets_in[k])], axis=0)
        own = jnp.concatenate([jnp.where(pos[0] % 4 == i, own, 0.0) for i in range(4)], axis=1)
        own = jnp.concatenate([jnp.where(pos[0] // 4 == i, own, 0.0) for i in range(2)], axis=0)
        front[0, rows, 2 * LANES :] = own.astype(bf16)
    for copy in copies:
        copy.wait()
    for k in range(2):
        front, back = outs[2 * k : 2 * k + 2]
        for j in range(2):
            part = basis_in[k, 16 * j : 16 * (j + 1), :]
            front[0, rows, j * LANES : j * LANES + width] = part.astype(bf16)
        for i in range(2):
            at = slice(i * HALF, (i + 1) * HALF)
            front[0, at, :] = rows_in[k, i].astype(bf16)
            back[0, at, :] = rows_in[k, 2 + i].astype(bf16)
            back[0, (2 + i) * HALF : (3 + i) * HALF, :] = pair_in[k, i].astype(bf16)


def cut_basis_body(pos, ins, outs, scratch):
    own, near, far, across = ins[0:4]
    first = near.shape[0] - 4 * HALF
    for k in range(2):
        at = first + 2 * HALF * k + pos[1] * HALF
        parts = [own[k, rows_at(pos[1] * HALF, HALF, HALF), :].astype(bf16)]
        parts += [ref[rows_at(at, HALF, HALF), :] for ref in (near, far.at[0], across)]
        outs[0][0, k * HALF : (k + 1) * HALF, :] = jnp.concatenate(parts, axis=1)


def join_body(pos, ins, outs, scratch):
    at = 0
    for ref in ins[0 : len(ins.refs)]:
        outs[0][at : at + ref.shape[0]] = ref[...]
        at += ref.shape[0]


def join(*parts):
    count = sum(part.shape[0] for part in parts)
    return "join", join_body, parts, [((count, *parts[0].shape[1:]), bf16)]


def fold_body(n, pos, ins, outs, scratch):
    at = 0
    for kept, arrived in zip(ins[0 : len(ins.refs) : 2], ins[1 : len(ins.refs) : 2]):
        rows = slice(at, at + kept.shape[1])
        at += kept.shape[1]
        for s in range(2 * n):
            total = kept[s].astype(f32) + arrived[s].astype(f32)
            if s < n:
                outs[0][s, rows, :] = total
            else:
                outs[1][s - n, rows, :] = total.astype(bf16)


def fold(*terms):
    n = terms[0].shape[0] // 2
    shape = (n, sum(term.shape[1] for term in terms[::2]), terms[0].shape[2])
    return "fold", functools.partial(fold_body, n), terms, [(shape, f32), (shape, bf16)]


def settle_body(pos, ins, outs, scratch):
    outs[0][...] = (ins[0][0] + ins[1][0].astype(f32)).astype(bf16)


def settle(kept, arrived):
    return "settle", settle_body, (kept, arrived), [(kept.shape[1:], bf16)]


def finish_body(width, pos, ins, outs, scratch):
    kernels, bias_out, projection, history_basis, forecast_basis = outs
    lower = pos[1] == 0
    for k in range(2):
        first, second, sizes = message_rows(k)
        places = {}
        for m, rows in enumerate((first, second)):
            one = 0 if k else 4 * m
            own, core, far, across = ins[8 * k + one : 8 * k + one + 4]
            for name, at in rows.items():
                places[name] = (own, core, far, across, at + (sizes[0] if k and m else 0))

        def both(name, height):
            own, core, far, across, at = places[name]
            rows = slice(at, at + height)
            mine = own[rows, :].astype(f32) + far[rows, :].astype(f32)
            other = core[rows, :].astype(f32) + across[rows, :].astype(f32)
            return jnp.where(lower, mine, other), jnp.where(lower, other, mine), mine

        targets = [("B", projection, 0), ("F", projection, 1)]
        targets += [("L" + str(layer + 1), kernels, layer) for layer in range(LAYERS)]
        for name, out, index in targets:
            a, b, _ = both(name, HALF)
            out[k, index, 0:HALF, :] = a
            out[k, index, HALF : 2 * HALF, :] = b
        own, _, far, _, at = places["V"]
        for j in range(2):
            lanes = slice(2 * j * LANES, (2 * j + 1) * LANES)
            theirs = slice((2 * j + 1) * LANES, (2 * j + 2) * LANES)
            rows = slice(at, at + HALF)
            total = own[rows, lanes].astype(f32) + far[rows, theirs].astype(f32)
            history_basis[k, j * HALF : (j + 1) * HALF, :] = total
        a, b, _ = both("U", 16)
        for j, value in enumerate((a, b)):
            for i in range(2):
                row = j * HALF + i * 16
                part = value[:, i * LANES : i * LANES + width]
                forecast_basis[k, row : row + 16, :] = part
        _, _, mine = both("bias", 16)
        total = jnp.zeros(bias_out.shape[1:], f32)
        for share in range(GROUPS):
            row, lane = 8 * (share // 4), 2 * LANES + (share % 4) * 2 * HALF
            part = mine[row : row + LAYERS, lane : lane + 2 * HALF]
            total = total + jnp.where(pos[0] == share, part, 0.0)
        bias_out[k] = total


def finish(line, sums, width):
    share = 2 * HALF
    return line.run(
        functools.partial(finish_body, width),
        "finish",
        sums,
        [
            ((2, LAYERS, share, 512), f32),
            ((2, LAYERS, share), f32),
            ((2, 2, share, 512), f32),
            ((2, share, LANES), f32),
            ((2, share, width), f32),
        ],
        limit=8,
    )


def slots_of(x, hops):
    x = x.reshape(GROUPS, 2, HALF, x.shape[-1]).swapaxes(0, 1)
    return x[:, jnp.array(slot_shares(hops))]


def in_order(x, hops):
    shares = slot_shares(hops)
    return x[:, jnp.array([shares.index(share) for share in range(GROUPS)])]


def flat_rows(x):
    return x.swapaxes(0, 1).reshape(2 * GROUPS * HALF, x.shape[-1])


def four(x):
    return x[0, 0:4], x[0, 4:8], x[1, 0:4], x[1, 4:8]


def shares_plain(kernels, offsets, projection, history_basis, forecast_basis, n_tm):
    tm = lax.axis_index("tm")

    def gather(x, axis, over="dp"):
        return lax.all_gather(x.astype(bf16), over, axis=axis, tiled=True)

    order = [jnp.bitwise_xor(tm, r) for r in range(n_tm)]
    out, bases = [], []
    for k in range(kernels.shape[0]):
        w = gather(kernels[k], 1)
        b = gather(offsets[k], 1)
        p = gather(projection[k], 1)
        u = gather(forecast_basis[k], 0)
        u = jnp.pad(u, ((0, 0), (0, LANES - u.shape[-1])))
        v = gather(gather(history_basis[k], 0), 1, "tm")
        v = jnp.concatenate(
            [lax.dynamic_slice_in_dim(v, at * LANES, LANES, 1) for at in order], axis=1
        )
        v = slots_of(v, HOPS["c"])
        other = [v[1, ..., (r ^ 1) * LANES : ((r ^ 1) + 1) * LANES] for r in range(4)]
        v = jnp.stack([v[0], jnp.concatenate(other, axis=-1)])
        offs = jnp.zeros((2, GROUPS, LAYERS, 512), bf16).at[0, 0].set(b)
        front_hops, back_hops = HOPS["a" + str(k)], HOPS["b" + str(k)]
        misc = pack_misc(slots_of(u, front_hops), offs)
        first = [slots_of(x, front_hops) for x in (w[0], w[1])] + [misc]
        first = jnp.concatenate(first, axis=2)
        second = jnp.concatenate([slots_of(x, back_hops) for x in (w[2], w[3], p[0], p[1])], axis=2)
        out.append((four(first), four(second)))
        bases.append(v)
    return out, four(jnp.concatenate(bases, axis=2))


def gradients_plain(records, n_tm, width):
    def reduce(x, axis):
        return lax.psum_scatter(
            lax.psum(x.astype(bf16), "tm").astype(f32), "dp", scatter_dimension=axis, tiled=True
        )

    results = [[], [], [], [], []]
    for k, messages in enumerate(records):
        pieces = {}
        for m, message in enumerate(messages):
            message = jnp.stack(message)
            hops = HOPS["m1" if k else ("m3", "m4")[m]]
            for name, at in message_rows(k)[m].items():
                height = 16 if name in ("U", "bias") else HALF
                pieces[name] = in_order(message[:, :, at : at + height, :], hops)
        square = {name: flat_rows(pieces[name]) for name in ("L1", "L2", "L3", "L4", "B", "F")}
        results[0].append(reduce(jnp.stack([square["L" + str(i)] for i in range(1, 5)]), 1))
        bias = pieces["bias"][0, 0]
        bias = jnp.concatenate([bias[0:4, 2 * LANES :], bias[8:12, 2 * LANES :]], axis=1)
        results[1].append(reduce(bias, 1))
        results[2].append(reduce(jnp.stack([square["B"], square["F"]]), 1))
        v = pieces["V"]
        v = jnp.concatenate([v[..., 0 : 2 * LANES], v[..., 2 * LANES :]], axis=2)
        v = v.reshape(2, 2 * GROUPS * HALF, 2, LANES)
        blocks = [v[r % 2, :, r // 2] for r in range(4)]
        total = blocks[0].astype(f32)
        for r in range(1, n_tm):
            total = total + swap(blocks[r], "tm", r, n_tm).astype(f32)
        results[3].append(lax.psum_scatter(total, "dp", scatter_dimension=0, tiled=True))
        u = pieces["U"]
        u = jnp.concatenate([u[..., 0:LANES], u[..., LANES : 2 * LANES]], axis=2)
        results[4].append(reduce(flat_rows(u), 0)[:, 0:width])
    return [jnp.stack(x) for x in results]


def body(
    n_dp,
    n_tm,
    history_series,
    frequency_labels,
    affine_kernels,
    affine_offsets,
    expansion_projection,
    history_dictionary,
    prediction_dictionary,
    remainder_adjoint,
    prediction_adjoint,
):
    fast = n_dp == GROUPS

    def pos():
        tm = lax.axis_index("tm")
        return (lax.axis_index("dp"), tm % 2, tm) if fast else (0, 0, tm)

    line = Line(pos)
    width = prediction_adjoint.shape[1]
    rows = frequency_labels.shape[0]
    labels = frequency_labels.reshape(1, rows)

    def hop(x, bit):
        return swap(x, "dp", bit, n_dp)

    def core(x):
        return swap(x, "tm", 1, n_tm)

    class Gather:
        def __init__(self, own, name):
            self.x, self.hops = own, list(HOPS[name])
            self.arriving = hop(own, self.hops.pop(0))

        def step(self):
            (self.x,) = yield join(self.x, self.arriving)
            self.arriving = hop(self.x, self.hops.pop(0))
            if not self.hops:
                self.low_core = core(self.x)

        def last(self):
            (high,) = yield join(self.arriving)
            self.slots = self.x, high, self.low_core, core(high)

    class Message:
        def __init__(self, name, *packed):
            self.packed, self.terms, self.hops = packed, [], list(HOPS[name])
            if fast:
                for kept, sent in packed:
                    self.terms += [kept, core(sent)]

        def fold(self):
            kept, out = yield fold(*self.terms)
            self.terms = [kept, hop(out, self.hops.pop())]

        def last(self):
            (own,) = yield settle(*self.terms)
            self.sums = [own] + [swap(own, "tm", r, n_tm) for r in (1, 2, 3)]

    v = types.SimpleNamespace()
    t = types.SimpleNamespace()

    def task(run):
        setattr(t, run.__name__, run)
        return run

    @task
    def cut():
        args = (affine_kernels, expansion_projection, prediction_dictionary, affine_offsets)
        scratch = [
            pltpu.VMEM((2, LAYERS, HALF, 512), f32),
            pltpu.VMEM((2, 2, HALF, 512), f32),
            pltpu.VMEM((2, HALF, width), f32),
            pltpu.VMEM(affine_offsets.shape, f32),
            pltpu.SemaphoreType.DMA((2, 4)),
        ]
        outs = [((1, FRONT, 512), bf16), ((1, BACK, 512), bf16)] * 2
        chunks = line.run(cut_body, "cut", args, outs, scratch, stay=(0, 1, 2, 3), limit=4)
        names = ("a0", "b0", "a1", "b1")
        v.a0, v.b0, v.a1, v.b1 = (Gather(x, name) for x, name in zip(chunks, names))

    @task
    def cut_c():
        args = (history_dictionary, *v.x.pieces()[1:])
        (own,) = yield "cut_basis", cut_basis_body, args, [((1, BASIS, 512), bf16)]
        v.c = Gather(own, "c")

    for name in ("a0", "b0", "a1", "b1", "c"):
        setattr(t, "step_" + name, lambda name=name: getattr(v, name).step())
        setattr(t, "last_" + name, lambda name=name: getattr(v, name).last())

    @task
    def split_x():
        pieces = split_windows(line, history_series, n_tm, history_dictionary if fast else None)
        v.x = Exchange(line, pieces, n_tm)

    @task
    def split_g():
        v.g = Exchange(line, split_windows(line, remainder_adjoint, n_tm), n_tm)

    @task
    def select():
        out = [((LANES, rows), bf16)]
        (v.fg,) = yield "select", select_body, (labels, prediction_adjoint.T), out

    for name in ("x", "g", "rem", "der"):
        setattr(t, "relay_" + name, lambda name=name: getattr(v, name).relay())

    @task
    def merge_rem():
        pieces = v.rem.pieces()
        v.remainder = merge_windows(line, history_series, pieces, -1)

    @task
    def merge_der():
        pieces = v.der.pieces()
        v.derivative = merge_windows(line, remainder_adjoint, pieces, 1)

    @task
    def front_0():
        outs = front(line, 0, v.a0.slots, v.x.pieces(), rows)
        v.w1a, v.w2a, v.bias, v.basis_a, *v.h12 = outs

    @task
    def rear_0():
        args = (v.b0.slots, v.h12[2], v.bias, v.basis_a, ())
        outs = rear(line, *args, width)
        v.w3a, v.w4a, v.wba, v.wfa = outs[:4]
        v.act, v.fore = outs[4:10], outs[10]
        v.h1a, v.d1a, v.h2a, v.d2a = v.h12

    @task
    def cast_0():
        outs = backcast(line, 0, v.c.slots, v.act[4], v.x.pieces(), v.act[0:2])
        v.wva, v.x2, v.cast, v.h3a, v.d3a = outs

    @task
    def front_1():
        outs = front(line, 1, v.a1.slots, [v.x2], rows, v.act[2:5])
        v.w1b, v.w2b, v.bias, v.basis_b, v.h1, v.d1, v.h2, v.d2 = outs[:8]
        v.h4a, v.d4a, v.bta = outs[8:]

    @task
    def rear_1():
        args = (v.b1.slots, v.h2, v.bias, v.basis_b, (v.fore, labels))
        outs = rear(line, *args, width, v.act[5:6])
        v.w3b, v.w4b, v.wbb, v.wfb = outs[:4]
        v.h3, v.d3, v.h4, v.d4, v.bt, v.ft, v.fore, v.fta = outs[4:]

    @task
    def cast_1():
        outs = backcast(line, 1, v.c.slots, v.bt, [v.cast])
        v.wvb, v.rem = outs[0], Exchange(line, outs[1:], n_tm)

    @task
    def chain_rear_1():
        weights = (v.wvb, v.basis_b, v.wbb, v.wfb, v.w4b)
        v.cr = chain_rear(line, v.g.pieces(), v.fg, weights, v.d4, v.d3, False)

    @task
    def terms_rear_1():
        args = ((*v.cr[0:3], v.fg), (v.bt, v.h4, v.ft), ())
        v.t1 = terms_rear(line, 1, *args, False)

    @task
    def chain_front_1():
        weights = (v.w3b, v.w2b, v.w1b)
        outs = chain_front(line, v.cr[4], weights, v.d2, v.d1, None, False)
        v.cf, v.gh2 = outs[0:3], outs[3]

    @task
    def terms_front_1():
        more = (v.h3, v.h2, v.cr[3], v.cr[4])
        args = ((*v.cf, v.cr[5]), [v.x2], v.h1, more)
        v.t2 = terms_front(line, 1, *args, False)
        v.m1 = Message("m1", v.t1, v.t2)

    @task
    def chain_rear_0():
        weights = (v.wva, v.basis_a, v.wba, v.wfa, v.w4a)
        gs = [*v.g.pieces(), v.gh2]
        v.cr = chain_rear(line, gs, v.fg, weights, v.d4a, v.d3a, False)

    @task
    def terms_rear_0():
        more = (v.h3a, v.h2a, v.cr[3], v.cr[4])
        args = ((*v.cr[0:3], v.fg), (v.bta, v.h4a, v.fta), more)
        outs = terms_rear(line, 0, *args, False)
        v.m3 = Message("m3", outs[0:2], outs[2:4])

    @task
    def chain_front_0():
        weights = (v.w3a, v.w2a, v.w1a)
        outs = chain_front(line, v.cr[4], weights, v.d2a, v.d1a, v.gh2, False)
        v.cf, v.der = outs[0:3], Exchange(line, outs[3:6], n_tm)

    @task
    def terms_front_0():
        args = ((*v.cf, v.cr[5]), v.x.pieces(), v.h1a, ())
        v.m4 = Message("m4", terms_front(line, 0, *args, False))

    for name in ("m1", "m3", "m4"):
        setattr(t, "fold_" + name, lambda name=name: getattr(v, name).fold())
        setattr(t, "settle_" + name, lambda name=name: getattr(v, name).last())

    if not fast:
        masters = (
            affine_kernels,
            affine_offsets,
            expansion_projection,
            history_dictionary,
            prediction_dictionary,
        )
        blocks, bases = shares_plain(*masters, n_tm)
        v.a0, v.b0, v.a1, v.b1, v.c = (Gather.__new__(Gather) for _ in range(5))
        v.a0.slots, v.b0.slots = blocks[0]
        v.a1.slots, v.b1.slots = blocks[1]
        v.c.slots = bases
        for name in vars(t):
            if name.startswith(("cut", "step", "last", "fold", "settle")):
                setattr(t, name, lambda: None)
    for us, *runs in order(t):
        line.us = us
        steps = [step for step in [run() for run in runs] if step is not None]
        if steps:
            for step, result in zip(steps, line.batch([next(step) for step in steps])):
                try:
                    step.send(result)
                except StopIteration:
                    pass
    if fast:
        sums = (*v.m3.sums, *v.m4.sums, *v.m1.sums)
        grads = finish(line, sums, width)
    else:
        m3 = [jnp.concatenate(pair, axis=1) for pair in zip(*v.m3.packed)]
        records = [(m3, v.m4.packed[0]), v.m1.packed]
        grads = gradients_plain(records, n_tm, width)
    return (v.remainder, v.fore.T, v.derivative, *grads)


def order(t):
    return (
        (None, t.split_x),
        (None, t.cut),
        (None, t.step_a0),
        (3, t.step_b0),
        (3, t.step_a0),
        (None, t.last_a0),
        (0, t.step_a1),
        (None, t.relay_x),
        (0.2, t.step_b0),
        (0.2, t.cut_c),
        (None, t.front_0),
        (None, t.step_a1),
        (None, t.step_c),
        (0.2, t.step_c),
        (20, t.last_b0),
        (20, t.split_g),
        (8, t.step_b1),
        (None, t.rear_0),
        (None, t.step_b1),
        (3, t.last_c),
        (20, t.last_a1),
        (None, t.cast_0),
        (8, t.select),
        (None, t.front_1),
        (None, t.last_b1),
        (20, t.relay_g),
        (1, t.rear_1),
        (None, t.cast_1),
        (1, t.chain_rear_1),
        (8, t.terms_rear_1),
        (20, t.chain_front_1),
        (0, t.terms_front_1),
        (None, t.fold_m1),
        (None, t.chain_rear_0),
        (20, t.chain_front_0),
        (None, t.terms_rear_0),
        (1, t.relay_rem),
        (None, t.fold_m3),
        (None, t.fold_m1),
        (20, t.terms_front_0),
        (None, t.merge_rem),
        (1, t.fold_m4),
        (0.2, t.fold_m3),
        (20, t.fold_m1),
        (None, t.fold_m4),
        (None, t.settle_m1),
        (None, t.fold_m3, t.relay_der),
        (None, t.merge_der),
        (None, t.settle_m3),
        (None, t.fold_m4),
        (0.2, t.settle_m4),
    )


def solution(mesh):
    return jax.shard_map(
        functools.partial(body, mesh.shape["dp"], mesh.shape["tm"]),
        mesh=mesh,
        in_specs=(
            P("dp", "tm"),
            P(("dp", "tm")),
            P(None, None, "dp", None),
            P(None, None, "dp"),
            P(None, None, "dp", None),
            P(None, "dp", "tm"),
            P(None, "dp", None),
            P("dp", "tm"),
            P(("dp", "tm"), None),
        ),
        out_specs=(
            P("dp", "tm"),
            P(("dp", "tm"), None),
            P("dp", "tm"),
            P(None, None, "dp", None),
            P(None, None, "dp"),
            P(None, None, "dp", None),
            P(None, "dp", "tm"),
            P(None, "dp", None),
        ),
        check_vma=False,
    )
```

```python
import functools
import types

import jax
import jax.numpy as jnp
from jax import lax
from jax.experimental import pallas as pl
from jax.experimental.pallas import tpu as pltpu
from jax.sharding import PartitionSpec as P

HOR_Y = 6
HOR_Q = 8
HOR_M = 18
LAYERS = 4
LANES = 128
HALF = 32
GROUPS = 8
FRONT = 2 * HALF + 16
BACK = 4 * HALF
BASIS = 2 * HALF
HOPS = {
    "a0": (4, 2, 1),
    "b0": (4, 2, 1),
    "a1": (4, 2, 1),
    "b1": (4, 2, 1),
    "c": (4, 2, 1),
    "m1": (4, 2, 1),
    "m3": (4, 1, 2),
    "m4": (4, 2, 1),
    "m2": (4, 1, 2),
}


def slot_shares(hops):
    return tuple(sum(bit for i, bit in enumerate(hops) if s >> i & 1) for s in range(GROUPS))


TILE = 512
CHUNK = 256

f32 = jnp.float32
bf16 = jnp.bfloat16
MIB = 1024 * 1024
FLOPS_PER_US = 150_000_000


def mm(a, b):
    return jnp.dot(a, b, preferred_element_type=f32)


def mm_nt(a, b):
    return lax.dot_general(a, b, (((1,), (1,)), ((), ())), preferred_element_type=f32)


def mm_tn(a, b):
    return lax.dot_general(a, b, (((0,), (0,)), ((), ())), preferred_element_type=f32)


def rows_at(start, size, align):
    return pl.ds(pl.multiple_of(start, align), size)


def in_group(labels, width):
    field = lax.broadcasted_iota(jnp.int32, (width, labels.shape[1]), 0)
    group = (
        (field >= HOR_Y).astype(jnp.int32)
        + (field >= HOR_Y + HOR_Q).astype(jnp.int32)
        + (field >= HOR_Y + HOR_Q + HOR_M).astype(jnp.int32)
    )
    return group == labels


def slot_rows(pos, q, s, hops):
    share = pos[0] ^ slot_shares(hops)[s]
    half = pos[1] ^ q
    row = share * (2 * HALF) + half * HALF
    block = share * 2 + half
    window_row = ((block // 4) ^ pos[2]) * LANES + (block % 4) * HALF
    return row, window_row


def slot_at(pos, share, hops):
    r = share ^ pos[0]
    place = {1: 0, 2: 1, 4: 2}
    return sum(((r >> place[bit]) & 1) << i for i, bit in enumerate(hops))


def size_of(shape):
    total = 1
    for extent in shape:
        total *= extent
    return total


class Inputs:
    def __init__(self, refs, copies):
        self.refs, self.copies = refs, copies

    def __getitem__(self, i):
        if isinstance(i, slice):
            return [self[j] for j in range(*i.indices(len(self.refs)))]
        if i in self.copies:
            self.copies.pop(i).wait()
        return self.refs[i]


class Line:
    def __init__(self, pos):
        self.pos, self.token, self.us = pos, None, None

    def batch(self, steps):
        shapes = [out for _, _, _, outs in steps for out in outs]
        args = [arg for _, _, arg_list, _ in steps for arg in arg_list]

        def body(pos, ins, outs, scratch):
            i = o = 0
            for _, run, arg_list, out_list in steps:
                run(pos, Inputs(ins.refs[i : i + len(arg_list)], {}), outs[o : o + len(out_list)], ())
                i, o = i + len(arg_list), o + len(out_list)

        name = "_and_".join(step[0] for step in steps)
        where = any(step[0] == "cut_basis" for step in steps)
        results = self.run(body, name, args, shapes, limit=6, where=where)
        split = []
        for _, _, _, out_list in steps:
            split.append(results[: len(out_list)])
            results = results[len(out_list) :]
        return split

    def run(self, body, name, args, outs, scratch=(), fetch=(), save=(), limit=12, after=(), us=0.5, stay=(), out_stays=False, where=True):
        token = [] if self.token is None else [self.token]
        extra = [*after, *token]
        fetch, save = list(fetch), list(save)
        n_in, n_out, n_extra = len(args), len(outs), len(extra)
        n_fetch, n_save = len(fetch), len(save)

        def kernel(*refs):
            refs = list(refs)
            pos_ref = self.pos() if where else None
            given, refs = refs[:n_in], refs[n_in + n_extra :]
            results, refs = refs[:n_out], refs[n_out:]
            saved, refs = refs[:n_save], refs[n_save:]
            if out_stays:
                refs.pop(0)[...] = jnp.zeros((8, LANES), f32)
            landing, refs = refs[:n_fetch], refs[n_fetch:]
            sems = refs.pop() if n_fetch + n_save else None
            inputs, copies, leaving = list(given), {}, []
            for at, (i, buf) in enumerate(zip(fetch, landing)):
                copies[i] = pltpu.make_async_copy(given[i], buf, sems.at[at])
                copies[i].start()
                inputs[i] = buf
            for at, (i, dst) in enumerate(zip(save, saved)):
                leaving.append(pltpu.make_async_copy(given[i], dst, sems.at[n_fetch + at]))
                leaving[-1].start()
            body(pos_ref, Inputs(inputs, copies), results, refs)
            for copy in (*copies.values(), *leaving):
                copy.wait()

        vmem, hbm = pl.BlockSpec(memory_space=pltpu.VMEM), pl.BlockSpec(memory_space=pltpu.HBM)
        anywhere = pl.BlockSpec(memory_space=pl.ANY)
        place = pltpu.HBM if out_stays else jax.ShapeDtypeStruct
        shapes = [place(shape, dtype) for shape, dtype in outs]
        placed = [
            pltpu.with_memory_space_constraint(a, pltpu.HBM) if i in fetch or i in stay else a
            for i, a in enumerate(args)
        ]
        shapes += [pltpu.HBM(args[i].shape, args[i].dtype) for i in save]
        mark = [jax.ShapeDtypeStruct((8, LANES), f32)] if out_stays else []
        sems = [pltpu.SemaphoreType.DMA((n_fetch + n_save,))] if n_fetch + n_save else []
        results = list(pl.pallas_call(
            kernel,
            name=name,
            out_shape=shapes + mark,
            in_specs=[hbm if i in fetch or i in stay else vmem for i in range(n_in)]
            + [anywhere] * n_extra,
            out_specs=[hbm if out_stays else vmem] * n_out + [hbm] * n_save + [vmem] * len(mark),
            scratch_shapes=[pltpu.VMEM(args[i].shape, args[i].dtype) for i in fetch]
            + list(scratch)
            + sems,
            compiler_params=pltpu.CompilerParams(vmem_limit_bytes=limit * MIB),
            cost_estimate=pl.CostEstimate(
                flops=int((us if self.us is None else self.us) * FLOPS_PER_US),
                bytes_accessed=1,
                transcendentals=0,
            ),
        )(*placed, *extra))
        if out_stays:
            self.token = results.pop()
        else:
            self.token = min(results, key=lambda a: a.size * a.dtype.itemsize)
        return results


def swap(x, axis, bit, size):
    return lax.ppermute(x, axis, [(i, i ^ bit) for i in range(size)])


class Exchange:
    def __init__(self, line, pieces, n_tm):
        self.line, self.n_tm = line, n_tm
        self.own, near, far = pieces
        self.far = swap(far, "tm", 2, n_tm)
        self.near = swap(near, "tm", 1, n_tm)

    def relay(self):
        (across,) = yield "relay", relay_body, (self.far,), [(self.far.shape[1:], bf16)]
        self.across = swap(across, "tm", 1, self.n_tm)

    def pieces(self):
        return [self.own, self.near, self.far, self.across]


def relay_body(pos, ins, outs, scratch):
    outs[0][...] = ins[0][1]


def flat(refs):
    return [ref if len(ref.shape) == 2 else ref.at[0] for ref in refs]


def split_body(with_basis, pos, ins, outs, scratch):
    landing, sems = scratch[0:2]
    rows = landing.shape[1]
    copies = []
    for r in range(4):
        copies.append(pltpu.make_async_copy(ins[0].at[pos[2] ^ r], landing.at[r], sems.at[r]))
    if with_basis:
        basis = scratch[2]
        basis_copy = pltpu.make_async_copy(ins[1], basis, sems.at[4])
        basis_copy.start()
    for r in (2, 3, 1, 0):
        copies[r].start()
    if with_basis:
        basis_copy.wait()
        for k in range(2):
            at = slice(rows + 2 * HALF * k, rows + 2 * HALF * (k + 1))
            value = basis[k].astype(bf16)
            for out in (outs[1], outs[2].at[0], outs[2].at[1]):
                out[at, :] = value
    for r in (2, 3, 1, 0):
        copies[r].wait()
        out = outs[2].at[r - 2] if r >= 2 else outs[r]
        out[0:rows, :] = landing[r].astype(bf16)


def piece_shapes(rows, more=0):
    sent = rows + more
    return [((rows, LANES), bf16), ((sent, LANES), bf16), ((2, sent, LANES), bf16)]


def split_windows(line, array, parts, basis=None):
    shape = (parts, array.shape[0] // parts, LANES)
    args = (array.reshape(shape),) if basis is None else (array.reshape(shape), basis)
    return line.run(
        functools.partial(split_body, basis is not None),
        "split_windows",
        args,
        piece_shapes(shape[1], 0 if basis is None else 2 * basis.shape[1]),
        [pltpu.VMEM(shape, f32), pltpu.SemaphoreType.DMA((parts + 1,))]
        + [pltpu.VMEM(a.shape, f32) for a in args[1:]],
        stay=range(len(args)),
        limit=8,
        us=2.0,
    )


def merge_body(sign, pos, ins, outs, scratch):
    base, pieces = ins[0], flat(ins[1:5])
    leaving, sems = scratch
    parts = len(pieces)
    arrive, leave = [], []
    for r in range(parts):
        at = pos[2] ^ r
        leave.append(pltpu.make_async_copy(leaving.at[r], outs[0].at[at], sems.at[parts + r]))
    for r, piece in enumerate(pieces):
        value = piece[...].astype(f32)
        own = base[pos[2] ^ r]
        leaving[r] = own - value if sign < 0 else own + value
        leave[r].start()
    for copy in leave:
        copy.wait()


def merge_windows(line, base, pieces, sign):
    parts = len(pieces)
    shape = (parts, base.shape[0] // parts, LANES)
    out = line.run(
        functools.partial(merge_body, sign),
        "merge_windows",
        (base.reshape(shape), *pieces),
        [(shape, f32)],
        [pltpu.VMEM(shape, f32), pltpu.SemaphoreType.DMA((2 * parts,))],
        stay=(),
        out_stays=True,
        limit=12,
        us=3.5,
    )[0]
    return out.reshape(base.shape)


def activate(p):
    t = jnp.tanh(p)
    u = 1.0 + t
    h = p * u
    return h.astype(bf16), u + h * (1.0 - t)


def columns(refs, at):
    if len(refs) == 1:
        return refs[0][at, :]
    return jnp.concatenate([ref[at, :] for ref in refs], axis=1)


def put_pieces(refs, at, value):
    for r in range(4):
        ref = refs[2].at[r - 2] if r >= 2 else refs[r]
        ref[at, :] = value[:, r * LANES : (r + 1) * LANES]


def chunks(rows):
    return [slice(at, at + CHUNK) for at in range(0, rows, CHUNK)]


def front_body(n_x, hops, pos, ins, bufs, scratch):
    w1, w2, bias, basis, h1, d1, h2, d2 = bufs
    total = jnp.zeros((16, 2 * LANES), f32)
    for q in range(2):
        for s in range(GROUPS):
            ref, i = ins[2 * q + s // 4], s % 4
            row, window_row = slot_rows(pos, q, s, hops)
            w1[rows_at(window_row, HALF, HALF), :] = ref[i, 0:HALF, :] * 0.5
            w2[rows_at(row, HALF, HALF), :] = ref[i, HALF : 2 * HALF, :] * 0.5
            low = ref[i, 2 * HALF : FRONT, 0:LANES]
            high = ref[i, 2 * HALF : FRONT, LANES : 2 * LANES]
            basis[rows_at(row, 16, 16), :] = low
            basis[rows_at(row + 16, 16, 16), :] = high
            if q == 0:
                total += ref[i, 2 * HALF : FRONT, 2 * LANES :].astype(f32)
    bias[:, 0 : 2 * LANES] = total[0:8] * 0.5
    bias[:, 2 * LANES :] = total[8:16] * 0.5
    xs = flat(ins[4 : 4 + n_x])
    for at in chunks(h1.shape[0]):
        h, d = activate(mm(columns(xs, at), w1[...]) + bias[0:1, :])
        h1[at, :] = h
        d1[at, :] = d.astype(bf16)
    for at in chunks(h1.shape[0]):
        h, d = activate(mm(h1[at, :], w2[...]) + bias[1:2, :])
        h2[at, :] = h
        d2[at, :] = d.astype(bf16)


def front(line, k, slots, xs, rows, leaving=()):
    square = ((512, 512), bf16)
    hidden = ((rows, 512), bf16)
    args = (*slots, *xs, *leaving)
    return line.run(
        functools.partial(front_body, len(xs), HOPS["a" + str(k)]),
        "front",
        args,
        [square, square, ((8, 512), f32), ((512, LANES), bf16), hidden, hidden, hidden, hidden],
        save=range(len(args) - len(leaving), len(args)),
        limit=6,
        us=4.0,
    )


def rear_body(last, hops, pos, ins, bufs, scratch):
    w3, w4, wb, wf, h3, d3, h4, d4, bt, ft, fore_out = bufs
    for q in range(2):
        for s in range(GROUPS):
            ref, i = ins[2 * q + s // 4], s % 4
            row, _ = slot_rows(pos, q, s, hops)
            for m, w in enumerate((w3, w4, wb, wf)):
                part = ref[i, m * HALF : (m + 1) * HALF, :]
                w[rows_at(row, HALF, HALF), :] = part * 0.5 if m < 2 else part
    bias, h2, basis = ins[4], ins[5], ins[6]
    steps = chunks(h3.shape[0])
    for at in steps:
        h, d = activate(mm(h2[at, :], w3[...]) + bias[2:3, :])
        h3[at, :] = h
        d3[at, :] = d.astype(bf16)
    for at in steps:
        h, d = activate(mm(h3[at, :], w4[...]) + bias[3:4, :])
        h4[at, :] = h
        d4[at, :] = (0.5 * d).astype(bf16)
    for at in steps:
        bt[at, :] = mm(h4[at, :], wb[...]).astype(bf16)
    for at in steps:
        ft[at, :] = mm(h4[at, :], wf[...]).astype(bf16)
    width = fore_out.shape[0]
    for at in steps:
        fore = mm(ft[at, :], basis[...]).T[0:width, :]
        if last:
            fore = ins[7][:, at] + fore
            fore = jnp.where(in_group(ins[8][0:1, at], width), fore, 0.0)
        fore_out[:, at] = fore


def rear(line, slots, h2, bias, basis, extra, width, leaving=()):
    rows = h2.shape[0]
    square = ((512, 512), bf16)
    hidden = ((rows, 512), bf16)
    args = (*slots, bias, h2, basis, *extra, *leaving)
    return line.run(
        functools.partial(rear_body, bool(extra), HOPS["b1" if extra else "b0"]),
        "rear",
        args,
        [square] * 4 + [hidden] * 6 + [((width, rows), f32)],
        save=range(len(args) - len(leaving), len(args)),
        limit=6,
        us=6.5,
    )


def cast_body(k, pos, ins, bufs, scratch):
    wv = bufs[0]
    for q in range(2):
        for s in range(GROUPS):
            ref, i = ins[2 * q + s // 4], s % 4
            row, _ = slot_rows(pos, q, s, HOPS["c"])
            for r in range(4):
                part = ref[i, k * HALF : (k + 1) * HALF, r * LANES : (r + 1) * LANES]
                at = r ^ q
                wv[rows_at(row, HALF, HALF), at * LANES : (at + 1) * LANES] = part
    bt = ins[4]
    for at in chunks(bt.shape[0]):
        cast = mm(bt[at, :], wv[...])
        if k == 0:
            bufs[1][at, :] = (columns(flat(ins[5:9]), at).astype(f32) - cast).astype(bf16)
            bufs[2][at, :] = cast
        else:
            put_pieces(bufs[1:4], at, (cast + ins[5][at, :]).astype(bf16))


def backcast(line, k, slots, bt, extra, leaving=()):
    rows = bt.shape[0]
    hidden = (rows, 512)
    outs = [(hidden, bf16), (hidden, f32)] if k == 0 else piece_shapes(rows)
    return line.run(
        functools.partial(cast_body, k),
        "backcast",
        (*slots, bt, *extra, *leaving),
        [((512, 512), bf16)] + outs,
        save=range(5 + len(extra), 5 + len(extra) + len(leaving)),
        limit=6,
        us=1.5,
    )


def row_sum(value):
    return jnp.sum(value.astype(f32), axis=0, keepdims=True)


def pack_pair(packed, rows, lanes, slot, first, second, pos):
    keep, send = packed
    lower = pos[1] == 0
    first, second = first.astype(bf16), second.astype(bf16)
    keep[slot, rows, lanes] = jnp.where(lower, first, second)
    send[slot, rows, lanes] = jnp.where(lower, second, first)


def pack_rows(packed, at, value, pos, hops):
    for share in range(GROUPS):
        row = share * 2 * HALF
        pack_pair(
            packed,
            slice(at, at + HALF),
            slice(None),
            slot_at(pos, share, hops),
            value[row : row + HALF, :],
            value[row + HALF : row + 2 * HALF, :],
            pos,
        )


def chain_rear_body(n_g, pos, ins, outs, scratch):
    g, g_back, g_fore, g4, g3, bias = outs
    wv, basis, wb, wf, w4 = ins[n_g + 1 : n_g + 6]
    gs, fg = flat(ins[0:4]) + ins[4:n_g], ins[n_g]
    steps = chunks(g.shape[0])
    for at in steps:
        value = columns(gs[:4], at)
        if n_g == 5:
            value = (value.astype(f32) + gs[4][at, :].astype(f32)).astype(bf16)
        g[at, :] = -value
        g_back[at, :] = mm_nt(g[at, :], wv[...]).astype(bf16)
    for at in steps:
        g_fore[at, :] = mm_nt(fg[:, at].T, basis[...]).astype(bf16)
    d4 = ins[n_g + 6]
    b3 = b4 = jnp.zeros((1, 512), f32)
    for at in steps:
        gh = mm_nt(g_back[at, :], wb[...]) + mm_nt(g_fore[at, :], wf[...])
        value = (gh * d4[at, :].astype(f32)).astype(bf16)
        g4[at, :] = value
        b4 += row_sum(value)
    d3 = ins[n_g + 7]
    for at in steps:
        gh = mm_nt(g4[at, :], w4[...])
        value = (gh * d3[at, :].astype(f32)).astype(bf16)
        g3[at, :] = value
        b3 += row_sum(value)
    bias[...] = jnp.concatenate([b3, b4, jnp.zeros((6, 512), f32)], axis=0)


def chain_rear(line, gs, fg, weights, d4, d3, fetch):
    rows = fg.shape[1]
    n = len(gs) + 1 + len(weights)
    return line.run(
        functools.partial(chain_rear_body, len(gs)),
        "chain_rear",
        (*gs, fg, *weights, d4, d3),
        [((rows, 512), bf16)] * 5 + [((8, 512), f32)],
        fetch=(n, n + 1) if fetch else (),
        limit=10 if fetch else 6,
        where=False,
        us=7.0,
    )


def chain_front_body(last, pos, ins, outs, scratch):
    g2, g1, bias = outs[:3]
    g3, w3, w2, w1 = ins[0:4]
    steps = chunks(g1.shape[0])
    b1 = b2 = jnp.zeros((1, 512), f32)
    d2 = ins[4]
    for at in steps:
        gh = mm_nt(g3[at, :], w3[...])
        value = (gh * d2[at, :].astype(f32)).astype(bf16)
        g2[at, :] = value
        b2 += row_sum(value)
    d1 = ins[5]
    for at in steps:
        gh = mm_nt(g2[at, :], w2[...])
        value = (gh * d1[at, :].astype(f32)).astype(bf16)
        g1[at, :] = value
        b1 += row_sum(value)
    for at in steps:
        gh = (2.0 * mm_nt(g1[at, :], w1[...])).astype(bf16)
        if last:
            gh = (gh.astype(f32) + ins[6][at, :].astype(f32)).astype(bf16)
            put_pieces(outs[3:6], at, gh)
        else:
            outs[3][at, :] = gh
    bias[...] = jnp.concatenate([b1, b2, jnp.zeros((6, 512), f32)], axis=0)


def chain_front(line, g3, weights, d2, d1, gh2, fetch):
    rows = g3.shape[0]
    last = gh2 is not None
    outs = piece_shapes(rows) if last else [((rows, 512), bf16)]
    return line.run(
        functools.partial(chain_front_body, last),
        "chain_front",
        (g3, *weights, d2, d1, *([gh2] if last else [])),
        [((rows, 512), bf16)] * 2 + [((8, 512), f32)] + outs,
        fetch=(4, 5) if fetch else (),
        limit=10 if fetch else 6,
        where=False,
        us=4.5,
    )


def message_rows(k):
    first = {"B": 0, "F": HALF, "V": 2 * HALF, "U": 3 * HALF}
    second = {"L2": 0, "L1": HALF, "bias": 2 * HALF}
    sizes = [3 * HALF + 16, 2 * HALF + 16]
    at = 1 if k else 0
    for name in ("L4", "L3"):
        (first, second)[at][name] = sizes[at]
        sizes[at] += HALF
    return first, second, sizes


REAR_GROUPS = (("B", "F"), ("V", "U"), ("L4", "L3"))
FRONT_GROUPS = (("L2", "L1", "bias"), ("L4", "L3"))


def pairs_of(groups, outs):
    places = {}
    for i, names in enumerate(groups[: len(outs) // 2]):
        at = 0
        for name in names:
            places[name] = outs[2 * i : 2 * i + 2], at
            at += 16 if name in ("U", "bias") else HALF
    return places


def pair_shapes(groups):
    outs = []
    for names in groups:
        height = sum(16 if name in ("U", "bias") else HALF for name in names)
        outs += [((GROUPS, height, 512), bf16)] * 2
    return outs


def whole_rows(ref):
    return slice(0, ref.shape[0])


def terms_rear_body(k, pos, ins, outs, scratch):
    places = pairs_of(REAR_GROUPS, outs)
    hops = HOPS["m1" if k else "m3"]
    g, g_back, g_fore, fg = ins[0:4]
    bt = ins[4]
    value = mm_tn(bt[...], g[...])
    packed, at = places["V"]
    for share in range(GROUPS):
        slot = slot_at(pos, share, hops)
        for r in range(4):
            for j in range(2):
                row, lane = (2 * share + j) * HALF, (2 * j + r // 2) * LANES
                part = value[row : row + HALF, r * LANES : (r + 1) * LANES].astype(bf16)
                packed[r % 2][slot, at : at + HALF, lane : lane + LANES] = part
    h4 = ins[5]
    pack_rows(*places["B"], mm_tn(h4[...], g_back[...]), pos, hops)
    pack_rows(*places["F"], mm_tn(h4[...], g_fore[...]), pos, hops)
    ft = ins[6]
    value = mm(fg[...], ft[...]).T
    packed, at = places["U"]
    rows = slice(at, at + 16)
    for share in range(GROUPS):
        row, slot = share * 2 * HALF, slot_at(pos, share, hops)
        for j in range(2):
            lanes = slice(j * LANES, (j + 1) * LANES)
            low = value[row + 16 * j : row + 16 * (j + 1), :]
            high = value[row + HALF + 16 * j : row + HALF + 16 * (j + 1), :]
            pack_pair(packed, rows, lanes, slot, low, high, pos)
        for out in packed:
            out[slot, rows, 2 * LANES :] = jnp.zeros((16, 2 * LANES), bf16)
    if "L4" in places:
        h3, h2, g4, g3 = ins[7], ins[8], ins[9], ins[10]
        pack_rows(*places["L4"], mm_tn(h3[...], g4[...]), pos, hops)
        pack_rows(*places["L3"], mm_tn(h2[...], g3[...]), pos, hops)


def terms_rear(line, k, grads, hidden, more, fetch):
    args = (*grads, *hidden, *more)
    return line.run(
        functools.partial(terms_rear_body, k),
        "terms_rear",
        args,
        pair_shapes(REAR_GROUPS[: 3 if more else 2]),
        fetch=[i for i in range(4, min(9, len(args)))] if fetch else (),
        limit=16 if fetch else 6,
        us=4.5 if k else 8.0,
    )


def terms_front_body(k, n_x, pos, ins, outs, scratch):
    places = pairs_of(FRONT_GROUPS, outs)
    hops = HOPS["m2" if k else "m4"]
    g2, g1, low_bias, high_bias = ins[0:4]
    bias = jnp.concatenate([low_bias[0:2, :], high_bias[0:2, :], jnp.zeros((4, 512), f32)], axis=0)
    bias = jnp.concatenate([bias[:, 0 : 2 * LANES], bias[:, 2 * LANES :]], axis=0).astype(bf16)
    packed, at = places["bias"]
    rows = slice(at, at + 16)
    for s in range(GROUPS):
        for out in packed:
            out[s, rows, 0 : 2 * LANES] = jnp.zeros((16, 2 * LANES), bf16)
            out[s, rows, 2 * LANES :] = bias
    xs = flat(ins[4 : 4 + n_x])
    value = mm_tn(columns(xs, whole_rows(g1)), g1[...])
    packed, at = places["L1"]
    for r in range(4):
        for i in range(2):
            row = r * LANES + i * 2 * HALF
            pack_pair(
                packed,
                slice(at, at + HALF),
                slice(None),
                slot_at(pos, (pos[2] ^ r) * 2 + i, hops),
                value[row : row + HALF, :],
                value[row + HALF : row + 2 * HALF, :],
                pos,
            )
    h1 = ins[4 + n_x]
    pack_rows(*places["L2"], mm_tn(h1[...], g2[...]), pos, hops)
    if "L4" in places:
        h3, h2, g4, g3 = ins[5 + n_x : 9 + n_x]
        pack_rows(*places["L4"], mm_tn(h3[...], g4[...]), pos, hops)
        pack_rows(*places["L3"], mm_tn(h2[...], g3[...]), pos, hops)


def terms_front(line, k, grads, xs, h1, more, fetch):
    args = (*grads, *xs, h1, *more)
    return line.run(
        functools.partial(terms_front_body, k, len(xs)),
        "terms_front",
        args,
        pair_shapes(FRONT_GROUPS[: 2 if more else 1]),
        fetch=(4 + len(xs),) if fetch else (),
        limit=8,
        us=5.5 if k else 3.0,
    )


def pack_misc(basis, offsets):
    lead = basis.shape[:-2]
    offsets = jnp.concatenate([offsets, jnp.zeros_like(offsets)], axis=-2)
    return jnp.concatenate(
        [
            basis[..., 0:16, :],
            basis[..., 16:32, :],
            jnp.concatenate([offsets[..., 0 : 2 * LANES], offsets[..., 2 * LANES :]], axis=-2),
        ],
        axis=-1,
    ).reshape(*lead, 16, 512)


def select_body(pos, ins, outs, scratch):
    labels, adjoint = ins[0], ins[1]
    width = adjoint.shape[0]
    for at in chunks(adjoint.shape[1]):
        value = jnp.where(in_group(labels[0:1, at], width), adjoint[:, at], 0.0)
        outs[0][0:width, at] = value.astype(bf16)
    outs[0][width:, :] = jnp.zeros((LANES - width, adjoint.shape[1]), bf16)


def cut_body(pos, ins, outs, scratch):
    kernels, projection, basis, offsets = ins[0:4]
    rows_in, pair_in, basis_in, offsets_in, sems = scratch
    offsets_copy = pltpu.make_async_copy(offsets, offsets_in, sems.at[0, 3])
    offsets_copy.start()
    half = rows_at(pos[1] * HALF, HALF, HALF)
    copies = []
    for k in range(2):
        copies += [
            pltpu.make_async_copy(kernels.at[k, :, half, :], rows_in.at[k], sems.at[k, 0]),
            pltpu.make_async_copy(basis.at[k, half, :], basis_in.at[k], sems.at[k, 1]),
            pltpu.make_async_copy(projection.at[k, :, half, :], pair_in.at[k], sems.at[k, 2]),
        ]
    for copy in copies:
        copy.start()
    rows, width = slice(2 * HALF, FRONT), basis.shape[2]
    offsets_copy.wait()
    for k in range(2):
        front, back = outs[2 * k : 2 * k + 2]
        front[0, rows, :] = jnp.zeros((16, 512), bf16)
        own = jnp.concatenate([offsets_in[k], jnp.zeros_like(offsets_in[k])], axis=0)
        own = jnp.concatenate([jnp.where(pos[0] % 4 == i, own, 0.0) for i in range(4)], axis=1)
        own = jnp.concatenate([jnp.where(pos[0] // 4 == i, own, 0.0) for i in range(2)], axis=0)
        front[0, rows, 2 * LANES :] = own.astype(bf16)
    for copy in copies:
        copy.wait()
    for k in range(2):
        front, back = outs[2 * k : 2 * k + 2]
        for j in range(2):
            part = basis_in[k, 16 * j : 16 * (j + 1), :]
            front[0, rows, j * LANES : j * LANES + width] = part.astype(bf16)
        for i in range(2):
            at = slice(i * HALF, (i + 1) * HALF)
            front[0, at, :] = rows_in[k, i].astype(bf16)
            back[0, at, :] = rows_in[k, 2 + i].astype(bf16)
            back[0, (2 + i) * HALF : (3 + i) * HALF, :] = pair_in[k, i].astype(bf16)


def cut_basis_body(pos, ins, outs, scratch):
    own, near, far, across = ins[0:4]
    first = near.shape[0] - 4 * HALF
    for k in range(2):
        at = first + 2 * HALF * k + pos[1] * HALF
        parts = [own[k, rows_at(pos[1] * HALF, HALF, HALF), :].astype(bf16)]
        parts += [ref[rows_at(at, HALF, HALF), :] for ref in (near, far.at[0], across)]
        outs[0][0, k * HALF : (k + 1) * HALF, :] = jnp.concatenate(parts, axis=1)


def join_body(pos, ins, outs, scratch):
    at = 0
    for ref in ins[0 : len(ins.refs)]:
        outs[0][at : at + ref.shape[0]] = ref[...]
        at += ref.shape[0]


def join(*parts):
    count = sum(part.shape[0] for part in parts)
    return "join", join_body, parts, [((count, *parts[0].shape[1:]), bf16)]


def fold_body(n, pos, ins, outs, scratch):
    at = 0
    for kept, arrived in zip(ins[0 : len(ins.refs) : 2], ins[1 : len(ins.refs) : 2]):
        rows = slice(at, at + kept.shape[1])
        at += kept.shape[1]
        for s in range(2 * n):
            total = kept[s].astype(f32) + arrived[s].astype(f32)
            if s < n:
                outs[0][s, rows, :] = total
            else:
                outs[1][s - n, rows, :] = total.astype(bf16)


def fold(*terms):
    n = terms[0].shape[0] // 2
    shape = (n, sum(term.shape[1] for term in terms[::2]), terms[0].shape[2])
    return "fold", functools.partial(fold_body, n), terms, [(shape, f32), (shape, bf16)]


def settle_body(pos, ins, outs, scratch):
    outs[0][...] = (ins[0][0] + ins[1][0].astype(f32)).astype(bf16)


def settle(kept, arrived):
    return "settle", settle_body, (kept, arrived), [(kept.shape[1:], bf16)]


def finish_body(width, pos, ins, outs, scratch):
    kernels, bias_out, projection, history_basis, forecast_basis = outs
    lower = pos[1] == 0
    for k in range(2):
        first, second, _ = message_rows(k)
        places = {}
        for m, rows in enumerate((first, second)):
            own, core, far, across = ins[8 * k + 4 * m : 8 * k + 4 * m + 4]
            for name, at in rows.items():
                places[name] = (own, core, far, across, at)

        def both(name, height):
            own, core, far, across, at = places[name]
            rows = slice(at, at + height)
            mine = own[rows, :].astype(f32) + far[rows, :].astype(f32)
            other = core[rows, :].astype(f32) + across[rows, :].astype(f32)
            return jnp.where(lower, mine, other), jnp.where(lower, other, mine), mine

        targets = [("B", projection, 0), ("F", projection, 1)]
        targets += [("L" + str(layer + 1), kernels, layer) for layer in range(LAYERS)]
        for name, out, index in targets:
            a, b, _ = both(name, HALF)
            out[k, index, 0:HALF, :] = a
            out[k, index, HALF : 2 * HALF, :] = b
        own, _, far, _, at = places["V"]
        for j in range(2):
            lanes = slice(2 * j * LANES, (2 * j + 1) * LANES)
            theirs = slice((2 * j + 1) * LANES, (2 * j + 2) * LANES)
            rows = slice(at, at + HALF)
            total = own[rows, lanes].astype(f32) + far[rows, theirs].astype(f32)
            history_basis[k, j * HALF : (j + 1) * HALF, :] = total
        a, b, _ = both("U", 16)
        for j, value in enumerate((a, b)):
            for i in range(2):
                row = j * HALF + i * 16
                part = value[:, i * LANES : i * LANES + width]
                forecast_basis[k, row : row + 16, :] = part
        _, _, mine = both("bias", 16)
        total = jnp.zeros(bias_out.shape[1:], f32)
        for share in range(GROUPS):
            row, lane = 8 * (share // 4), 2 * LANES + (share % 4) * 2 * HALF
            part = mine[row : row + LAYERS, lane : lane + 2 * HALF]
            total = total + jnp.where(pos[0] == share, part, 0.0)
        bias_out[k] = total


def finish(line, sums, width):
    share = 2 * HALF
    return line.run(
        functools.partial(finish_body, width),
        "finish",
        sums,
        [
            ((2, LAYERS, share, 512), f32),
            ((2, LAYERS, share), f32),
            ((2, 2, share, 512), f32),
            ((2, share, LANES), f32),
            ((2, share, width), f32),
        ],
        limit=8,
    )


def slots_of(x, hops):
    x = x.reshape(GROUPS, 2, HALF, x.shape[-1]).swapaxes(0, 1)
    return x[:, jnp.array(slot_shares(hops))]


def in_order(x, hops):
    shares = slot_shares(hops)
    return x[:, jnp.array([shares.index(share) for share in range(GROUPS)])]


def flat_rows(x):
    return x.swapaxes(0, 1).reshape(2 * GROUPS * HALF, x.shape[-1])


def four(x):
    return x[0, 0:4], x[0, 4:8], x[1, 0:4], x[1, 4:8]


def shares_plain(kernels, offsets, projection, history_basis, forecast_basis, n_tm):
    tm = lax.axis_index("tm")

    def gather(x, axis, over="dp"):
        return lax.all_gather(x.astype(bf16), over, axis=axis, tiled=True)

    order = [jnp.bitwise_xor(tm, r) for r in range(n_tm)]
    out, bases = [], []
    for k in range(kernels.shape[0]):
        w = gather(kernels[k], 1)
        b = gather(offsets[k], 1)
        p = gather(projection[k], 1)
        u = gather(forecast_basis[k], 0)
        u = jnp.pad(u, ((0, 0), (0, LANES - u.shape[-1])))
        v = gather(gather(history_basis[k], 0), 1, "tm")
        v = jnp.concatenate(
            [lax.dynamic_slice_in_dim(v, at * LANES, LANES, 1) for at in order], axis=1
        )
        v = slots_of(v, HOPS["c"])
        other = [v[1, ..., (r ^ 1) * LANES : ((r ^ 1) + 1) * LANES] for r in range(4)]
        v = jnp.stack([v[0], jnp.concatenate(other, axis=-1)])
        offs = jnp.zeros((2, GROUPS, LAYERS, 512), bf16).at[0, 0].set(b)
        front_hops, back_hops = HOPS["a" + str(k)], HOPS["b" + str(k)]
        misc = pack_misc(slots_of(u, front_hops), offs)
        first = [slots_of(x, front_hops) for x in (w[0], w[1])] + [misc]
        first = jnp.concatenate(first, axis=2)
        second = jnp.concatenate([slots_of(x, back_hops) for x in (w[2], w[3], p[0], p[1])], axis=2)
        out.append((four(first), four(second)))
        bases.append(v)
    return out, four(jnp.concatenate(bases, axis=2))


def gradients_plain(records, n_tm, width):
    def reduce(x, axis):
        return lax.psum_scatter(
            lax.psum(x.astype(bf16), "tm").astype(f32), "dp", scatter_dimension=axis, tiled=True
        )

    results = [[], [], [], [], []]
    for k, messages in enumerate(records):
        pieces = {}
        for m, message in enumerate(messages):
            message = jnp.stack([jnp.concatenate(message[half::2], axis=1) for half in range(2)])
            hops = HOPS[(("m3", "m4"), ("m1", "m2"))[k][m]]
            for name, at in message_rows(k)[m].items():
                height = 16 if name in ("U", "bias") else HALF
                pieces[name] = in_order(message[:, :, at : at + height, :], hops)
        square = {name: flat_rows(pieces[name]) for name in ("L1", "L2", "L3", "L4", "B", "F")}
        results[0].append(reduce(jnp.stack([square["L" + str(i)] for i in range(1, 5)]), 1))
        bias = pieces["bias"][0, 0]
        bias = jnp.concatenate([bias[0:4, 2 * LANES :], bias[8:12, 2 * LANES :]], axis=1)
        results[1].append(reduce(bias, 1))
        results[2].append(reduce(jnp.stack([square["B"], square["F"]]), 1))
        v = pieces["V"]
        v = jnp.concatenate([v[..., 0 : 2 * LANES], v[..., 2 * LANES :]], axis=2)
        v = v.reshape(2, 2 * GROUPS * HALF, 2, LANES)
        blocks = [v[r % 2, :, r // 2] for r in range(4)]
        total = blocks[0].astype(f32)
        for r in range(1, n_tm):
            total = total + swap(blocks[r], "tm", r, n_tm).astype(f32)
        results[3].append(lax.psum_scatter(total, "dp", scatter_dimension=0, tiled=True))
        u = pieces["U"]
        u = jnp.concatenate([u[..., 0:LANES], u[..., LANES : 2 * LANES]], axis=2)
        results[4].append(reduce(flat_rows(u), 0)[:, 0:width])
    return [jnp.stack(x) for x in results]


def body(
    n_dp,
    n_tm,
    history_series,
    frequency_labels,
    affine_kernels,
    affine_offsets,
    expansion_projection,
    history_dictionary,
    prediction_dictionary,
    remainder_adjoint,
    prediction_adjoint,
):
    fast = n_dp == GROUPS

    def pos():
        tm = lax.axis_index("tm")
        return (lax.axis_index("dp"), tm % 2, tm) if fast else (0, 0, tm)

    line = Line(pos)
    width = prediction_adjoint.shape[1]
    rows = frequency_labels.shape[0]
    labels = frequency_labels.reshape(1, rows)

    def hop(x, bit):
        return swap(x, "dp", bit, n_dp)

    def core(x):
        return swap(x, "tm", 1, n_tm)

    class Gather:
        def __init__(self, own, name):
            self.x, self.hops = own, list(HOPS[name])
            self.arriving = hop(own, self.hops.pop(0))

        def step(self):
            (self.x,) = yield join(self.x, self.arriving)
            self.arriving = hop(self.x, self.hops.pop(0))
            if not self.hops:
                self.low_core = core(self.x)

        def last(self):
            (high,) = yield join(self.arriving)
            self.slots = self.x, high, self.low_core, core(high)

    class Message:
        def __init__(self, name, *packed):
            self.packed, self.terms, self.hops = packed, [], list(HOPS[name])
            if fast:
                for kept, sent in zip(packed[::2], packed[1::2]):
                    self.terms += [kept, core(sent)]

        def fold(self):
            kept, out = yield fold(*self.terms)
            self.terms = [kept, hop(out, self.hops.pop())]

        def last(self):
            (own,) = yield settle(*self.terms)
            self.sums = [own] + [swap(own, "tm", r, n_tm) for r in (1, 2, 3)]

    v = types.SimpleNamespace()
    t = types.SimpleNamespace()

    def task(run):
        setattr(t, run.__name__, run)
        return run

    @task
    def cut():
        args = (affine_kernels, expansion_projection, prediction_dictionary, affine_offsets)
        scratch = [
            pltpu.VMEM((2, LAYERS, HALF, 512), f32),
            pltpu.VMEM((2, 2, HALF, 512), f32),
            pltpu.VMEM((2, HALF, width), f32),
            pltpu.VMEM(affine_offsets.shape, f32),
            pltpu.SemaphoreType.DMA((2, 4)),
        ]
        outs = [((1, FRONT, 512), bf16), ((1, BACK, 512), bf16)] * 2
        chunks = line.run(cut_body, "cut", args, outs, scratch, stay=(0, 1, 2, 3), limit=4)
        names = ("a0", "b0", "a1", "b1")
        v.a0, v.b0, v.a1, v.b1 = (Gather(x, name) for x, name in zip(chunks, names))

    @task
    def cut_c():
        args = (history_dictionary, *v.x.pieces()[1:])
        (own,) = yield "cut_basis", cut_basis_body, args, [((1, BASIS, 512), bf16)]
        v.c = Gather(own, "c")

    for name in ("a0", "b0", "a1", "b1", "c"):
        setattr(t, "step_" + name, lambda name=name: getattr(v, name).step())
        setattr(t, "last_" + name, lambda name=name: getattr(v, name).last())

    @task
    def split_x():
        pieces = split_windows(line, history_series, n_tm, history_dictionary if fast else None)
        v.x = Exchange(line, pieces, n_tm)

    @task
    def split_g():
        v.g = Exchange(line, split_windows(line, remainder_adjoint, n_tm), n_tm)

    @task
    def select():
        out = [((LANES, rows), bf16)]
        (v.fg,) = yield "select", select_body, (labels, prediction_adjoint.T), out

    for name in ("x", "g", "rem", "der"):
        setattr(t, "relay_" + name, lambda name=name: getattr(v, name).relay())

    @task
    def merge_rem():
        pieces = v.rem.pieces()
        v.remainder = merge_windows(line, history_series, pieces, -1)

    @task
    def merge_der():
        pieces = v.der.pieces()
        v.derivative = merge_windows(line, remainder_adjoint, pieces, 1)

    @task
    def front_0():
        outs = front(line, 0, v.a0.slots, v.x.pieces(), rows)
        v.w1a, v.w2a, v.bias, v.basis_a, *v.h12 = outs

    @task
    def rear_0():
        args = (v.b0.slots, v.h12[2], v.bias, v.basis_a, ())
        outs = rear(line, *args, width)
        v.w3a, v.w4a, v.wba, v.wfa = outs[:4]
        v.act, v.fore = outs[4:10], outs[10]
        v.h1a, v.d1a, v.h2a, v.d2a = v.h12

    @task
    def cast_0():
        outs = backcast(line, 0, v.c.slots, v.act[4], v.x.pieces(), v.act[0:2])
        v.wva, v.x2, v.cast, v.h3a, v.d3a = outs

    @task
    def front_1():
        outs = front(line, 1, v.a1.slots, [v.x2], rows, v.act[2:5])
        v.w1b, v.w2b, v.bias, v.basis_b, v.h1, v.d1, v.h2, v.d2 = outs[:8]
        v.h4a, v.d4a, v.bta = outs[8:]

    @task
    def rear_1():
        args = (v.b1.slots, v.h2, v.bias, v.basis_b, (v.fore, labels))
        outs = rear(line, *args, width, v.act[5:6])
        v.w3b, v.w4b, v.wbb, v.wfb = outs[:4]
        v.h3, v.d3, v.h4, v.d4, v.bt, v.ft, v.fore, v.fta = outs[4:]

    @task
    def cast_1():
        outs = backcast(line, 1, v.c.slots, v.bt, [v.cast])
        v.wvb, v.rem = outs[0], Exchange(line, outs[1:], n_tm)

    @task
    def chain_rear_1():
        weights = (v.wvb, v.basis_b, v.wbb, v.wfb, v.w4b)
        v.cr = chain_rear(line, v.g.pieces(), v.fg, weights, v.d4, v.d3, False)

    @task
    def terms_rear_1():
        args = ((*v.cr[0:3], v.fg), (v.bt, v.h4, v.ft), ())
        v.m1 = Message("m1", *terms_rear(line, 1, *args, False))

    @task
    def chain_front_1():
        weights = (v.w3b, v.w2b, v.w1b)
        outs = chain_front(line, v.cr[4], weights, v.d2, v.d1, None, False)
        v.cf, v.gh2 = outs[0:3], outs[3]

    @task
    def terms_front_1():
        more = (v.h3, v.h2, v.cr[3], v.cr[4])
        args = ((*v.cf, v.cr[5]), [v.x2], v.h1, more)
        v.m2 = Message("m2", *terms_front(line, 1, *args, False))

    @task
    def chain_rear_0():
        weights = (v.wva, v.basis_a, v.wba, v.wfa, v.w4a)
        gs = [*v.g.pieces(), v.gh2]
        v.cr = chain_rear(line, gs, v.fg, weights, v.d4a, v.d3a, False)

    @task
    def terms_rear_0():
        more = (v.h3a, v.h2a, v.cr[3], v.cr[4])
        args = ((*v.cr[0:3], v.fg), (v.bta, v.h4a, v.fta), more)
        v.m3 = Message("m3", *terms_rear(line, 0, *args, False))

    @task
    def chain_front_0():
        weights = (v.w3a, v.w2a, v.w1a)
        outs = chain_front(line, v.cr[4], weights, v.d2a, v.d1a, v.gh2, False)
        v.cf, v.der = outs[0:3], Exchange(line, outs[3:6], n_tm)

    @task
    def terms_front_0():
        args = ((*v.cf, v.cr[5]), v.x.pieces(), v.h1a, ())
        v.m4 = Message("m4", *terms_front(line, 0, *args, False))

    for name in ("m1", "m2", "m3", "m4"):
        setattr(t, "fold_" + name, lambda name=name: getattr(v, name).fold())
        setattr(t, "settle_" + name, lambda name=name: getattr(v, name).last())

    if not fast:
        masters = (
            affine_kernels,
            affine_offsets,
            expansion_projection,
            history_dictionary,
            prediction_dictionary,
        )
        blocks, bases = shares_plain(*masters, n_tm)
        v.a0, v.b0, v.a1, v.b1, v.c = (Gather.__new__(Gather) for _ in range(5))
        v.a0.slots, v.b0.slots = blocks[0]
        v.a1.slots, v.b1.slots = blocks[1]
        v.c.slots = bases
        for name in vars(t):
            if name.startswith(("cut", "step", "last", "fold", "settle")):
                setattr(t, name, lambda: None)
    for us, *runs in order(t):
        line.us = us
        steps = [step for step in [run() for run in runs] if step is not None]
        if steps:
            for step, result in zip(steps, line.batch([next(step) for step in steps])):
                try:
                    step.send(result)
                except StopIteration:
                    pass
    if fast:
        sums = (*v.m3.sums, *v.m4.sums, *v.m1.sums, *v.m2.sums)
        grads = finish(line, sums, width)
    else:
        records = [(v.m3.packed, v.m4.packed), (v.m1.packed, v.m2.packed)]
        grads = gradients_plain(records, n_tm, width)
    return (v.remainder, v.fore.T, v.derivative, *grads)


def order(t):
    return (
        (None, t.split_x),
        (None, t.cut),
        (None, t.step_a0),
        (3, t.step_b0),
        (1, t.step_a0),
        (0, t.last_a0),
        (None, t.step_b0),
        (0, t.step_a1),
        (1, t.relay_x),
        (0.2, t.cut_c),
        (None, t.front_0),
        (0.2, t.step_c),
        (None, t.step_a1),
        (None, t.step_c),
        (20, t.last_b0),
        (20, t.split_g),
        (8, t.step_b1),
        (1, t.rear_0),
        (None, t.step_b1),
        (3, t.last_c),
        (20, t.last_a1),
        (None, t.cast_0),
        (None, t.select),
        (None, t.front_1),
        (None, t.last_b1),
        (20, t.relay_g),
        (0.2, t.rear_1),
        (3, t.cast_1),
        (1, t.chain_rear_1),
        (8, t.terms_rear_1),
        (20, t.chain_front_1),
        (0, t.terms_front_1),
        (None, t.fold_m2),
        (None, t.fold_m1),
        (None, t.chain_rear_0),
        (20, t.chain_front_0),
        (None, t.fold_m1),
        (None, t.terms_rear_0),
        (None, t.fold_m1),
        (20, t.relay_rem),
        (None, t.fold_m3, t.fold_m2),
        (20, t.terms_front_0),
        (None, t.merge_rem),
        (1, t.fold_m4),
        (None, t.fold_m3),
        (20, t.fold_m2),
        (None, t.settle_m1, t.fold_m4),
        (None, t.settle_m2),
        (None, t.fold_m3),
        (None, t.relay_der),
        (None, t.merge_der),
        (None, t.fold_m4),
        (None, t.settle_m3),
        (0.2, t.settle_m4),
    )


def solution(mesh):
    return jax.shard_map(
        functools.partial(body, mesh.shape["dp"], mesh.shape["tm"]),
        mesh=mesh,
        in_specs=(
            P("dp", "tm"),
            P(("dp", "tm")),
            P(None, None, "dp", None),
            P(None, None, "dp"),
            P(None, None, "dp", None),
            P(None, "dp", "tm"),
            P(None, "dp", None),
            P("dp", "tm"),
            P(("dp", "tm"), None),
        ),
        out_specs=(
            P("dp", "tm"),
            P(("dp", "tm"), None),
            P("dp", "tm"),
            P(None, None, "dp", None),
            P(None, None, "dp"),
            P(None, None, "dp", None),
            P(None, "dp", "tm"),
            P(None, "dp", None),
        ),
        check_vma=False,
    )
```
